32 devices in a mesh: ctx: 8 (over y, x, core), wsh: 4 (over z).
Axes of the slice: x: 2, y: 2, z: 4, core: 2. Of those that a mesh axis runs over, the one named last changes fastest.
Arguments:
- tokens: bfloat16 [4, 2048, 1024], P('wsh', 'ctx'), may hold values from -6 to 6
- starts: int32 [4, 8], P('wsh'), may hold values from 0 to 2047, as said below
- query_weight: bfloat16 [1024, 1024], P('wsh'), may hold values from -0.1875 to 0.1875
- key_weight: bfloat16 [1024, 1024], P('wsh'), may hold values from -0.1875 to 0.1875
- value_weight: bfloat16 [1024, 1024], P('wsh'), may hold values from -0.1875 to 0.1875
- output_weight: bfloat16 [1024, 1024], P('wsh'), may hold values from -0.15625 to 0.15625
- inner_weight: bfloat16 [1024, 4096], P('wsh'), may hold values from -0.1875 to 0.1875
- outer_weight: bfloat16 [4096, 1024], P('wsh'), may hold values from -0.09375 to 0.09375
- query_bias: bfloat16 [1024], P('wsh'), may hold values from -3 to 3
- value_bias: bfloat16 [1024], P('wsh'), may hold values from -0.3125 to 0.3125
- output_bias: bfloat16 [1024], P('wsh'), may hold values from -1.75 to 1.75
- first_gain: bfloat16 [1024], P('wsh'), may hold values from 0.5 to 1.5
- first_shift: bfloat16 [1024], P('wsh'), may hold values from -1.75 to 1.75
- inner_bias: bfloat16 [4096], P('wsh'), may hold values from -3 to 3
- outer_bias: bfloat16 [1024], P('wsh'), may hold values from -1.75 to 1.75
- second_gain: bfloat16 [1024], P('wsh'), may hold values from 0.5 to 1.5
- second_shift: bfloat16 [1024], P('wsh'), may hold values from -1.75 to 1.75
- cotangent: bfloat16 [4, 2048, 1024], P('wsh', 'ctx'), may hold values from -6 to 6
Outputs:
- result: bfloat16 [4, 2048, 1024], P('wsh', 'ctx')
- input_grad: bfloat16 [4, 2048, 1024], P('wsh', 'ctx')
- query_weight_grad: float32 [1024, 1024], P('wsh')
- key_weight_grad: float32 [1024, 1024], P('wsh')
- value_weight_grad: float32 [1024, 1024], P('wsh')
- output_weight_grad: float32 [1024, 1024], P('wsh')
- inner_weight_grad: float32 [1024, 4096], P('wsh')
- outer_weight_grad: float32 [4096, 1024], P('wsh')
- query_bias_grad: float32 [1024], P('wsh')
- value_bias_grad: float32 [1024], P('wsh')
- output_bias_grad: float32 [1024], P('wsh')
- first_gain_grad: float32 [1024], P('wsh')
- first_shift_grad: float32 [1024], P('wsh')
- inner_bias_grad: float32 [4096], P('wsh')
- outer_bias_grad: float32 [1024], P('wsh')
- second_gain_grad: float32 [1024], P('wsh')
- second_shift_grad: float32 [1024], P('wsh')
The draws below stay inside these ranges and needn't reach their ends.
Inputs may be any that keep to these rules, and one draw needn't show every extreme that they name: `starts`: each row begins with 0 and rises strictly.
All inputs are finite; a program needn't handle non-finite values.
Results may differ from the reference program's by a relative error of at most 0.023.
Values may be sent and summed in bfloat16 or wider, within the bound.
No kernel may reach another device: no remote copies, remote signals or barrier semaphores. Data moves between devices by JAX's collectives and lax.ppermute only.
A program may use at most 320 MiB of HBM per device.

```python
import math
import jax
import jax.numpy as jnp
from jax import lax

D = 1024
HEADS = 16
FF = 4096
TOK_DEV = 256
STREAMS = 4
STREAM_LEN = 2048


def draw_starts(key, part):
    key = jax.random.fold_in(key, 11)
    keys = jax.random.split(key, 7)
    half_dev = TOK_DEV // 2
    head_end = jax.random.randint(keys[0], (STREAMS,), half_dev, TOK_DEV)
    tail_start = jax.random.randint(keys[1], (STREAMS,), STREAM_LEN - TOK_DEV, STREAM_LEN - half_dev)
    first_doc = jax.random.randint(keys[2], (STREAMS,), 1, head_end // 3 + 1)
    second_doc = first_doc + jax.random.randint(keys[3], (STREAMS,), 1, head_end // 3 + 1)
    room = STREAM_LEN - tail_start
    third_doc = tail_start + jax.random.randint(keys[4], (STREAMS,), 1, room // 4 + 1)
    fourth_doc = third_doc + jax.random.randint(keys[5], (STREAMS,), 1, room // 4 + 1)
    fifth_doc = fourth_doc + jax.random.randint(keys[6], (STREAMS,), 1, room // 4 + 1)
    anchor = jnp.zeros((STREAMS,), jnp.int32)
    table = jnp.stack([anchor, first_doc, second_doc, head_end, tail_start, third_doc, fourth_doc, fifth_doc], axis=1)
    return table.astype(jnp.int32)


def block_scale(own_key, dims, pieces, least, high):
    loudness = 1.0
    for dim, blocks in pieces:
        steps = jax.random.uniform(jax.random.fold_in(jax.random.fold_in(own_key, 6), dim), (blocks,), jnp.float32, least / len(pieces), high / len(pieces))
        loudness = loudness * jnp.repeat(jnp.exp(steps), dims[dim] // blocks).reshape((-1,) + (1,) * (len(dims) - 1 - dim))
    return loudness


def normal_values(rng, extent, scale, reach, pieces=(), kind=jnp.bfloat16):
    factor_of = block_scale(rng, extent, pieces, -0.22, 0.18) if pieces else 1.0
    array = jax.random.normal(rng, extent, jnp.float32) * scale * factor_of
    return jnp.minimum(jnp.maximum(array, -reach), reach).astype(kind)


def setup_inputs(seed: int = 0) -> dict:
    key_of = jax.random.split(jax.random.key(seed), 19)
    return {
        "tokens": normal_values(key_of[0], (STREAMS, STREAM_LEN, D), 1.0, 6.0, ((0, 4), (1, 8))),
        "starts": draw_starts(jax.random.fold_in(key_of[18], 71), 0),
        "query_weight": normal_values(key_of[2], (D, D), D ** -0.5, 0.1875, ((0, 4),)),
        "key_weight": normal_values(key_of[3], (D, D), D ** -0.5, 0.1875, ((0, 4),)),
        "value_weight": normal_values(key_of[4], (D, D), D ** -0.5, 0.1875, ((0, 4),)),
        "output_weight": normal_values(key_of[5], (D, D), (max(1, 3 * D * D // STREAM_LEN)) ** -0.5, 0.15625, ((0, 4),)),
        "inner_weight": normal_values(key_of[6], (D, FF), D ** -0.5, 0.1875, ((0, 4),)),
        "outer_weight": normal_values(key_of[7], (FF, D), FF ** -0.5, 0.09375, ((0, 4),)),
        "query_bias": normal_values(key_of[8], (D,), 0.5, 3.0, ((0, 4),)),
        "value_bias": normal_values(key_of[9], (D,), 0.05, 0.3125, ((0, 4),)),
        "output_bias": normal_values(key_of[10], (D,), 0.3, 1.75, ((0, 4),)),
        "first_gain": jnp.clip(1.0 + 0.1 * jax.random.normal(key_of[11], (D,), jnp.float32), 0.5, 1.5).astype(jnp.bfloat16),
        "first_shift": normal_values(key_of[12], (D,), 0.3, 1.75, ((0, 4),)),
        "inner_bias": normal_values(key_of[13], (FF,), 0.5, 3.0, ((0, 4),)),
        "outer_bias": normal_values(key_of[14], (D,), 0.3, 1.75, ((0, 4),)),
        "second_gain": jnp.clip(1.0 + 0.1 * jax.random.normal(key_of[15], (D,), jnp.float32), 0.5, 1.5).astype(jnp.bfloat16),
        "second_shift": normal_values(key_of[16], (D,), 0.3, 1.75, ((0, 4),)),
        "cotangent": normal_values(key_of[17], (STREAMS, STREAM_LEN, D), 1.0, 6.0, ((0, 4), (1, 8))),
    }


@jax.custom_vjp
def low(v):
    return lax.optimization_barrier(v.astype(jnp.bfloat16)).astype(jnp.float32)

@jax.custom_vjp
def low_back(v):
    return v

def low_keep(v):
    return (low(v), None)

def low_pass(kept, grad):
    return (grad,)

def back_keep(v):
    return (v, None)

def back_low(kept, grad):
    return (low(grad),)
low.defvjp(low_keep, low_pass)
low_back.defvjp(back_keep, back_low)

def matmul(left_side, right_side):
    return jnp.dot(left_side, right_side, precision=lax.Precision.HIGHEST, preferred_element_type=jnp.float32)

def layer_norm(residual, norm_gain, norm_shift):
    row_mean = lax.optimization_barrier(jnp.mean(residual, axis=-1, keepdims=True))
    centered = residual - row_mean
    spread = lax.optimization_barrier(jnp.mean(centered * centered, axis=-1, keepdims=True))
    return centered * lax.rsqrt(spread + 1e-05) * norm_gain + norm_shift

def exact_gelu(source):
    return jax.nn.gelu(source, approximate=False)

def segment_ids(starts_row, length):
    positions = jnp.arange(length, dtype=jnp.int32)
    return lax.optimization_barrier(jnp.sum((starts_row[None, :] <= positions[:, None]).astype(jnp.int32), axis=1)) - 1

def attend_block(queries, seg_rows, key_rows, value_rows, seg_keys):
    scores = low_back(jnp.einsum('qhe,khe->hqk', queries, key_rows, precision=lax.Precision.HIGHEST))
    scores = jnp.where((seg_rows[:, None] == seg_keys[None, :])[None], scores, -1e+30)
    maximum = lax.optimization_barrier(jnp.max(scores, axis=2, keepdims=True))
    exponent = jnp.exp(scores - maximum)
    attn_probs = low(exponent / lax.optimization_barrier(jnp.sum(exponent, axis=2, keepdims=True)))
    return jnp.einsum('hqk,khe->qhe', attn_probs, value_rows, precision=lax.Precision.HIGHEST)

def attention(queries, key_rows, value_rows, segment):
    length = queries.shape[0]
    block_len = math.gcd(512, length)

    def scan_step(running, inputs):
        return (running, attend_block(inputs[0], inputs[1], key_rows, value_rows, segment))
    query_blocks = queries.reshape(length // block_len, block_len, HEADS, queries.shape[2])
    seg_blocks = segment.reshape(length // block_len, block_len)
    _, blocks = lax.scan(jax.checkpoint(scan_step), jnp.zeros((), jnp.float32), (query_blocks, seg_blocks))
    return blocks.reshape(length, queries.shape[1] * queries.shape[2])

def forward(features, weights, segment):
    query_weight, key_weight, value_weight, output_weight, inner_weight, outer_weight, query_bias, value_bias, output_bias, first_gain, first_shift, inner_bias, outer_bias, second_gain, second_shift = weights
    length = features.shape[0]
    head_size = D // HEADS
    query_scale = head_size ** (-0.5)
    queries = low_back(low((matmul(features, query_weight) + query_bias) * query_scale))
    key_rows = low_back(low(matmul(features, key_weight)))
    value_rows = low_back(low(matmul(features, value_weight) + value_bias))
    attended = attention(queries.reshape(length, HEADS, head_size), key_rows.reshape(length, HEADS, head_size), value_rows.reshape(length, HEADS, head_size), segment)
    mixed = low_back(low(attended))
    attn_out = low_back(matmul(mixed, output_weight) + output_bias)
    hidden = layer_norm(features + attn_out, first_gain, first_shift)
    inner_act = low_back(matmul(low(hidden), inner_weight) + inner_bias)
    act_low = low_back(low(exact_gelu(inner_act)))
    branch = low_back(matmul(act_low, outer_weight) + outer_bias)
    return layer_norm(hidden + branch, second_gain, second_shift)

def reference(tokens, starts, query_weight, key_weight, value_weight, output_weight, inner_weight, outer_weight, query_bias, value_bias, output_bias, first_gain, first_shift, inner_bias, outer_bias, second_gain, second_shift, cotangent):
    weights = tuple((w.astype(jnp.float32) for w in (query_weight, key_weight, value_weight, output_weight, inner_weight, outer_weight, query_bias, value_bias, output_bias, first_gain, first_shift, inner_bias, outer_bias, second_gain, second_shift)))

    def stream_step(totals, inputs):
        stream_rows, starts_row, stream_cot = inputs
        segment = segment_ids(starts_row, stream_rows.shape[0])
        features = stream_rows.astype(jnp.float32)

        def apply_layer(layer_input, layer_weights):
            return forward(layer_input, layer_weights, segment)
        output, pullback = jax.vjp(apply_layer, features, weights)
        feature_grad, weight_grads = pullback(stream_cot.astype(jnp.float32))
        totals = jax.tree.map(lambda total_grad, new_grad: total_grad + new_grad, totals, weight_grads)
        return (totals, (output.astype(jnp.bfloat16), feature_grad.astype(jnp.bfloat16)))
    initial = tuple((jnp.zeros_like(w) for w in weights))
    totals, (outputs, input_grads) = lax.scan(stream_step, initial, (tokens, starts, cotangent))
    return (outputs, input_grads, totals[0], totals[1], totals[2], totals[3], totals[4], totals[5], totals[6], totals[7], totals[8], totals[9], totals[10], totals[11], totals[12], totals[13], totals[14])
```

```python
import functools

import jax
import jax.numpy as jnp
from jax import lax
from jax.experimental import pallas as pl
from jax.experimental.pallas import tpu as pltpu
from jax.sharding import PartitionSpec as P

HEADS = 16
LANES = 128
BF = jnp.bfloat16
F32 = jnp.float32
VMEM = 60 * 1024 * 1024


def dot(a, b):
    return lax.dot_general(a, b, (((1,), (0,)), ((), ())), preferred_element_type=F32)


def dot_nt(a, b):
    return lax.dot_general(a, b, (((1,), (1,)), ((), ())), preferred_element_type=F32)


def dot_tn(a, b):
    return lax.dot_general(a, b, (((0,), (0,)), ((), ())), preferred_element_type=F32)


def params(semantics=None):
    return pltpu.CompilerParams(vmem_limit_bytes=VMEM, dimension_semantics=semantics)


def as_row(column):
    return jnp.broadcast_to(column, (column.shape[0], LANES)).T[0:1, :]


def attend_kernel(q_ref, k_ref, v_ref, o_ref, lse_ref):
    scores = dot_nt(q_ref[0], k_ref[0])
    top = jnp.max(scores, axis=1, keepdims=True)
    probs = jnp.exp(scores - top)
    total = jnp.sum(probs, axis=1, keepdims=True)
    o_ref[0] = dot(probs.astype(BF), v_ref[0]) / total
    lse_ref[0] = as_row(top + jnp.log(total))


def attend(q, k, v, rows):
    heads, length, wide = q.shape
    size = v.shape[2]
    return pl.pallas_call(
        attend_kernel,
        grid=(heads, length // rows),
        in_specs=[
            pl.BlockSpec((1, rows, wide), lambda h, i: (h, i, 0)),
            pl.BlockSpec((1, length, wide), lambda h, i: (h, 0, 0)),
            pl.BlockSpec((1, length, size), lambda h, i: (h, 0, 0)),
        ],
        out_specs=[
            pl.BlockSpec((1, rows, size), lambda h, i: (h, i, 0)),
            pl.BlockSpec((1, 1, rows), lambda h, i: (h, 0, i)),
        ],
        out_shape=[
            jax.ShapeDtypeStruct((heads, length, size), F32),
            jax.ShapeDtypeStruct((heads, 1, length), F32),
        ],
        compiler_params=params(),
        name="attend",
    )(q, k, v)


def attend_back_kernel(
    q_ref, k_ref, v_ref, kt_ref, mg_ref, o_ref, lse_ref, dqt_ref, dk_ref, dv_ref, dk_acc, dv_acc
):
    step = pl.program_id(1)
    size = v_ref.shape[2]

    @pl.when(step == 0)
    def _():
        dk_acc[...] = jnp.zeros_like(dk_acc)
        dv_acc[...] = jnp.zeros_like(dv_acc)

    q = q_ref[0]
    mg = mg_ref[0]
    row_terms = as_row(jnp.sum(mg.astype(F32) * o_ref[0], axis=1, keepdims=True))
    probs = jnp.exp(dot_nt(k_ref[0], q) - lse_ref[0])
    dv_acc[...] += dot(probs.astype(BF), mg)
    grads = (probs * (dot_nt(v_ref[0], mg) - row_terms)).astype(BF)
    dk_acc[...] += dot(grads, q[:, :size])
    dqt_ref[0] = dot(kt_ref[0], grads).astype(BF)

    @pl.when(step == pl.num_programs(1) - 1)
    def _():
        dk_ref[0] = dk_acc[...].astype(BF)
        dv_ref[0] = dv_acc[...].astype(BF)


def attend_back(q, k, v, kt, mg, o, lse, rows):
    heads, length, wide = q.shape
    size = v.shape[2]
    whole = lambda h, i: (h, 0, 0)
    part = lambda h, i: (h, i, 0)
    lane = lambda h, i: (h, 0, i)
    return pl.pallas_call(
        attend_back_kernel,
        grid=(heads, length // rows),
        in_specs=[
            pl.BlockSpec((1, rows, wide), part),
            pl.BlockSpec((1, length, wide), whole),
            pl.BlockSpec((1, length, size), whole),
            pl.BlockSpec((1, size, length), whole),
            pl.BlockSpec((1, rows, size), part),
            pl.BlockSpec((1, rows, size), part),
            pl.BlockSpec((1, 1, rows), lane),
        ],
        out_specs=[
            pl.BlockSpec((1, size, rows), lane),
            pl.BlockSpec((1, length, size), whole),
            pl.BlockSpec((1, length, size), whole),
        ],
        out_shape=[
            jax.ShapeDtypeStruct((heads, size, length), BF),
            jax.ShapeDtypeStruct((heads, length, size), BF),
            jax.ShapeDtypeStruct((heads, length, size), BF),
        ],
        scratch_shapes=[pltpu.VMEM((length, size), F32), pltpu.VMEM((length, size), F32)],
        compiler_params=params(),
        name="attend_back",
    )(q, k, v, kt, mg, o, lse)


def normalize(source):
    mean = jnp.mean(source, axis=-1, keepdims=True)
    centered = source - mean
    root = lax.rsqrt(jnp.mean(centered * centered, axis=-1, keepdims=True) + 1e-05)
    return centered * root, root


def norm_back(normed, root, grad, gain):
    scaled = grad * gain
    mean = jnp.mean(scaled, axis=-1, keepdims=True)
    mix = jnp.mean(scaled * normed, axis=-1, keepdims=True)
    return root * (scaled - mean - normed * mix)


def first_norm_kernel(count, offs_ref, x_ref, wo_ref, vec_ref, *refs):
    blocks, (hidden_ref, low_ref, normed_ref, root_ref) = refs[:count], refs[count:]
    wide = blocks[0].shape[1]
    out = x_ref[...].astype(F32) + vec_ref[0:1, :]
    for r, block in enumerate(blocks):
        out = out + dot(block[...], wo_ref[pl.ds(pl.multiple_of(offs_ref[r], wide), wide), :])
    normed, root = normalize(out)
    hidden = normed * vec_ref[1:2, :] + vec_ref[2:3, :]
    hidden_ref[...] = hidden
    low_ref[...] = hidden.astype(BF)
    normed_ref[...] = normed
    root_ref[...] = root


def first_norm(offs, x, wo, vec, blocks):
    rows, width = x.shape
    vm = pl.BlockSpec(memory_space=pltpu.VMEM)
    return pl.pallas_call(
        functools.partial(first_norm_kernel, len(blocks)),
        in_specs=[pl.BlockSpec(memory_space=pltpu.SMEM)] + [vm] * (3 + len(blocks)),
        out_specs=[vm] * 4,
        out_shape=[
            jax.ShapeDtypeStruct((rows, width), F32),
            jax.ShapeDtypeStruct((rows, width), BF),
            jax.ShapeDtypeStruct((rows, width), F32),
            jax.ShapeDtypeStruct((rows, 1), F32),
        ],
        compiler_params=params(),
        name="first_norm",
    )(offs, x, wo, vec, *blocks)


def second_norm_kernel(hidden_ref, branch_ref, vec_ref, cot_ref, res_ref, resid_ref, bgrad_ref, sums_ref):
    normed, root = normalize(hidden_ref[...] + branch_ref[...].astype(F32) + vec_ref[0:1, :])
    gain = vec_ref[1:2, :]
    res_ref[...] = (normed * gain + vec_ref[2:3, :]).astype(BF)
    grad = cot_ref[...].astype(F32)
    resid = norm_back(normed, root, grad, gain)
    resid_ref[...] = resid
    low = resid.astype(BF)
    bgrad_ref[...] = low
    sums_ref[0:1, :] = jnp.sum(grad * normed, axis=0, keepdims=True)
    sums_ref[1:2, :] = jnp.sum(grad, axis=0, keepdims=True)
    sums_ref[2:3, :] = jnp.sum(low.astype(F32), axis=0, keepdims=True)
    sums_ref[3:8, :] = jnp.zeros((5, sums_ref.shape[1]), F32)


def second_norm(hidden, branch, vec, cot):
    rows, width = hidden.shape
    vm = pl.BlockSpec(memory_space=pltpu.VMEM)
    return pl.pallas_call(
        second_norm_kernel,
        in_specs=[vm] * 4,
        out_specs=[vm] * 4,
        out_shape=[
            jax.ShapeDtypeStruct((rows, width), BF),
            jax.ShapeDtypeStruct((rows, width), F32),
            jax.ShapeDtypeStruct((rows, width), BF),
            jax.ShapeDtypeStruct((8, width), F32),
        ],
        compiler_params=params(),
        name="second_norm",
    )(hidden, branch, vec, cot)


def first_back_kernel(count, offs_ref, resid_ref, more_ref, normed_ref, root_ref, vec_ref, wo_ref, *refs):
    blocks = refs[:count]
    first_ref, wog_ref, sums_ref = refs[count : count + 3]
    outs = refs[count + 3 :]
    wide = blocks[0].shape[1]
    grad = resid_ref[...] + more_ref[...].astype(F32)
    normed = normed_ref[...]
    first = norm_back(normed, root_ref[...], grad, vec_ref[1:2, :])
    first_ref[...] = first
    low = first.astype(BF)
    sums_ref[0:1, :] = jnp.sum(grad * normed, axis=0, keepdims=True)
    sums_ref[1:2, :] = jnp.sum(grad, axis=0, keepdims=True)
    sums_ref[2:3, :] = jnp.sum(low.astype(F32), axis=0, keepdims=True)
    sums_ref[3:8, :] = jnp.zeros((5, sums_ref.shape[1]), F32)
    for r in range(count):
        rows = pl.ds(pl.multiple_of(offs_ref[r], wide), wide)
        outs[r][...] = dot_nt(low, wo_ref[rows, :]).astype(BF)
        wog_ref[rows, :] = dot_tn(blocks[r][...], low).astype(BF)


def first_back(offs, resid, more, normed, root, vec, wo, blocks):
    rows, width = resid.shape
    wide = blocks[0].shape[1]
    vm = pl.BlockSpec(memory_space=pltpu.VMEM)
    return pl.pallas_call(
        functools.partial(first_back_kernel, len(blocks)),
        in_specs=[pl.BlockSpec(memory_space=pltpu.SMEM)] + [vm] * (6 + len(blocks)),
        out_specs=[vm] * (3 + len(blocks)),
        out_shape=[
            jax.ShapeDtypeStruct((rows, width), F32),
            jax.ShapeDtypeStruct((width, width), BF),
            jax.ShapeDtypeStruct((8, width), F32),
        ]
        + [jax.ShapeDtypeStruct((rows, wide), BF)] * len(blocks),
        compiler_params=params(),
        name="first_back",
    )(offs, resid, more, normed, root, vec, wo, *blocks)


def flip(source, bit):
    return lax.ppermute(source, "ctx", [(i, i ^ bit) for i in range(8)])


class Cube:
    def __init__(self):
        self.count = 8

    def at(self, r):
        return lax.axis_index("ctx") ^ r

    def gather(self, own):
        half = own.shape[0] // 2
        side = flip(own, 2)
        down = flip(own, 4)
        core = flip(own, 1)
        far = jnp.concatenate([flip(side[:half], 4), flip(down[half:], 2)], axis=0)
        return [own, core, side, flip(side, 1), down, flip(down, 1), far, flip(far, 1)]

    def scatter(self, blocks):
        half = blocks[0].shape[0] // 2
        low = [b.astype(BF) for b in blocks]
        far = blocks[6].astype(F32) + flip(low[7], 1).astype(F32)
        far = far.astype(BF)
        over_side = flip(far[:half], 2)
        over_down = flip(far[half:], 4)
        side = blocks[2].astype(F32) + flip(low[3], 1).astype(F32)
        down = blocks[4].astype(F32) + flip(low[5], 1).astype(F32)
        side_a = flip(side[:half].astype(BF), 2)
        down_b = flip(down[half:].astype(BF), 4)
        side_b = flip((side[half:] + over_down.astype(F32)).astype(BF), 2)
        down_a = flip((down[:half] + over_side.astype(F32)).astype(BF), 4)
        own = blocks[0].astype(F32) + flip(low[1], 1).astype(F32)
        return (
            own
            + jnp.concatenate([side_a, side_b], axis=0).astype(F32)
            + jnp.concatenate([down_a, down_b], axis=0).astype(F32)
        )

    def exchange(self, blocks):
        return [blocks[0]] + [flip(blocks[r], r) for r in range(1, 8)]


class Line:
    def __init__(self, count):
        self.count = count

    def at(self, r):
        return jnp.int32(r)

    def gather(self, own):
        return list(lax.all_gather(own, "ctx", axis=0, tiled=False))

    def scatter(self, blocks):
        whole = jnp.concatenate([b.astype(BF) for b in blocks], axis=0)
        return lax.psum_scatter(whole, "ctx", scatter_dimension=0, tiled=True).astype(F32)

    def exchange(self, blocks):
        return list(lax.all_to_all(jnp.stack(blocks), "ctx", 0, 0, tiled=False))


def gelu_pair(source):
    bell = 0.5 * (1.0 + lax.erf(source * (0.5**0.5)))
    slope = bell + source * jnp.exp(-0.5 * source * source) * ((2.0 * jnp.pi) ** -0.5)
    return source * bell, slope


def local(
    tokens, starts, query_weight, key_weight, value_weight, output_weight, inner_weight, outer_weight,
    query_bias, value_bias, output_bias, first_gain, first_shift, inner_bias, outer_bias,
    second_gain, second_shift, cotangent,
):
    count, shards = lax.axis_size("ctx"), lax.axis_size("wsh")
    net = Cube() if count == 8 else Line(count)
    me, shard = lax.axis_index("ctx"), lax.axis_index("wsh")
    x = tokens[0]
    rows, width = x.shape
    length = rows * count
    size = width // HEADS
    heads = max(1, HEADS // count)
    copies = max(1, count // HEADS)
    cols = heads * size
    depth = width // shards
    units = outer_weight.shape[0] // count
    strip = depth // count
    scale = size**-0.5

    first_col = me // copies * cols
    qkv_own = jnp.concatenate(
        [lax.dynamic_slice_in_dim(w, first_col, cols, 1) for w in (query_weight, key_weight, value_weight)],
        axis=1,
    )
    small_own = jnp.concatenate(
        [query_bias, value_bias, output_bias, first_gain, first_shift, outer_bias, second_gain,
         second_shift, inner_bias]
    )
    small = lax.all_gather(small_own, "wsh", axis=0, tiled=False).astype(F32)
    qkv = lax.all_gather(qkv_own, "wsh", axis=0, tiled=True)
    wo_own = lax.dynamic_slice_in_dim(output_weight, me * strip, strip, 0)
    wo_part = lax.all_gather(wo_own, "wsh", axis=0, tiled=False)
    inner_own = lax.dynamic_slice_in_dim(inner_weight.reshape(depth, shards, -1), me * units, units, 2)
    inner = lax.all_gather(inner_own.reshape(depth, shards * units), "wsh", axis=0, tiled=True)
    outer_own = lax.dynamic_slice_in_dim(outer_weight, me * units, units, 0)
    outer = lax.all_gather(outer_own, "wsh", axis=0, tiled=True)
    wo = lax.all_gather(wo_part, "ctx", axis=0, tiled=False)
    wo = wo.transpose(1, 0, 2, 3).reshape(width, width)

    def vector(i):
        return small[:, i * depth : (i + 1) * depth].reshape(1, width)

    query_b = lax.dynamic_slice_in_dim(vector(0), first_col, cols, 1)
    value_b = lax.dynamic_slice_in_dim(vector(1), first_col, cols, 1)
    pad = jnp.zeros((5, width), F32)
    first_vec = jnp.concatenate([vector(2), vector(3), vector(4), pad], axis=0)
    second_vec = jnp.concatenate([vector(5), vector(6), vector(7), pad], axis=0)
    inner_b = lax.dynamic_slice_in_dim(small[:, 8 * depth :], me * units, units, 1).reshape(1, -1)

    stream = jnp.concatenate(net.gather(x), axis=0)
    place = jnp.concatenate([net.at(r) * rows + jnp.arange(rows, dtype=jnp.int32) for r in range(count)])
    segment = jnp.sum((starts[0][None, :] <= place[:, None]).astype(jnp.int32), axis=1) - 1
    same = segment[:, None] == jnp.arange(starts.shape[1], dtype=jnp.int32)[None, :]
    fill = jnp.zeros((length, LANES - size - starts.shape[1]), BF)
    query_tail = jnp.concatenate([jnp.where(same, 0.0, -1e30).astype(BF), fill], axis=1)
    key_tail = jnp.concatenate([same.astype(BF), fill], axis=1)
    raw = dot(stream, qkv)
    queries = ((raw[:, :cols] + query_b) * scale).astype(BF)
    keys = raw[:, cols : 2 * cols].astype(BF)
    values = (raw[:, 2 * cols :] + value_b).astype(BF)

    def head(source, h):
        return source[:, h * size : (h + 1) * size]

    q_ext = jnp.stack([jnp.concatenate([head(queries, h), query_tail], axis=1) for h in range(heads)])
    k_ext = jnp.stack([jnp.concatenate([head(keys, h), key_tail], axis=1) for h in range(heads)])
    v_heads = jnp.stack([head(values, h) for h in range(heads)])
    mixed, lse = attend(q_ext, k_ext, v_heads, rows)
    mixed_low = jnp.concatenate([mixed[h] for h in range(heads)], axis=1).astype(BF)
    blocks = net.exchange([mixed_low[r * rows : (r + 1) * rows] for r in range(count)])[::copies]
    offs = jnp.stack([net.at(r) // copies * cols for r in range(0, count, copies)])
    hidden, hidden_low, normed, root = first_norm(offs, x, wo, first_vec, blocks)

    hidden_all = jnp.concatenate(net.gather(hidden_low), axis=0)
    act, slope = gelu_pair(dot(hidden_all, inner) + inner_b)
    act_low, slope = act.astype(BF), slope.astype(BF)
    branch = dot(act_low, outer).astype(BF)
    branch = net.scatter([branch[r * rows : (r + 1) * rows] for r in range(count)])
    result, resid, branch_grad, sums_two = second_norm(hidden, branch, second_vec, cotangent[0])

    grad_all = jnp.concatenate(net.gather(branch_grad), axis=0)
    inner_grad = (dot_nt(grad_all, outer) * slope.astype(F32)).astype(BF)
    hidden_grad = dot_nt(inner_grad, inner).astype(BF)
    hidden_grad = net.scatter([hidden_grad[r * rows : (r + 1) * rows] for r in range(count)])
    outer_wg = dot_tn(act_low, grad_all).astype(BF)
    inner_wg = dot_tn(hidden_all, inner_grad).astype(BF)
    inner_bg = jnp.sum(inner_grad.astype(F32), axis=0)

    first, wo_grad, sums_one, *mixed_grads = first_back(
        offs, resid, hidden_grad, normed, root, first_vec, wo, blocks
    )
    if copies > 1:
        mixed_grads = [b for b in mixed_grads for _ in range(copies)]
    mixed_grad = jnp.concatenate(net.exchange(mixed_grads), axis=0)
    mg_heads = jnp.stack([head(mixed_grad, h) for h in range(heads)])
    k_t = jnp.stack([head(keys, h).T for h in range(heads)])
    dqt, dk, dv = attend_back(q_ext, k_ext, v_heads, k_t, mg_heads, mixed, lse, rows)
    triple = jnp.concatenate(
        [dqt[h].T * BF(scale) for h in range(heads)]
        + [dk[h] for h in range(heads)]
        + [dv[h] for h in range(heads)],
        axis=1,
    )
    into = dot_nt(triple, qkv)
    if copies > 1:
        into = into * (1.0 / copies)
    into = into.astype(BF)
    into = net.scatter([into[r * rows : (r + 1) * rows] for r in range(count)])
    input_grad = (first + into).astype(BF)
    qkv_wg = dot_tn(stream, triple).astype(BF)
    qkv_bg = jnp.sum(triple.astype(F32), axis=0)

    def own_rows(source):
        return lax.psum_scatter(source, "wsh", scatter_dimension=0, tiled=True)

    def everywhere(source):
        return lax.all_gather(source, "ctx", axis=0, tiled=False).astype(F32)

    outer_out = everywhere(own_rows(outer_wg)).reshape(-1, width)
    inner_out = everywhere(own_rows(inner_wg)).reshape(count, depth, shards, units)
    inner_out = inner_out.transpose(1, 2, 0, 3).reshape(depth, -1)
    wo_grad = wo_grad.reshape(shards, count, strip, width).transpose(1, 0, 2, 3).reshape(width, width)
    wo_grad = lax.psum_scatter(wo_grad, "ctx", scatter_dimension=0, tiled=True)
    wo_out = everywhere(own_rows(wo_grad)).reshape(depth, width)
    qkv_out = everywhere(own_rows(qkv_wg))[::copies]
    qkv_out = qkv_out.reshape(-1, depth, 3, cols).transpose(2, 1, 0, 3).reshape(3, depth, width)

    zero = jnp.zeros((width,), F32)
    weight = 1.0 / copies
    vecs = jnp.concatenate(
        [
            lax.dynamic_update_slice(zero, qkv_bg[:cols] * weight, (first_col,)),
            lax.dynamic_update_slice(zero, qkv_bg[2 * cols :] * weight, (first_col,)),
            sums_one[2], sums_one[0], sums_one[1], sums_two[2], sums_two[0], sums_two[1],
            lax.dynamic_update_slice(
                jnp.zeros((shards, units * count), F32), inner_bg.reshape(shards, units),
                (jnp.int32(0), me * units),
            ).reshape(-1),
        ]
    )
    vecs = lax.psum(vecs, ("ctx", "wsh"))

    def piece(i):
        return lax.dynamic_slice_in_dim(vecs, i * width + shard * depth, depth, 0)

    inner_bias_out = lax.dynamic_slice_in_dim(vecs, 8 * width + shard * units * count, units * count, 0)
    return (
        result[None], input_grad[None], qkv_out[0], qkv_out[1], qkv_out[2], wo_out, inner_out, outer_out,
        piece(0), piece(1), piece(2), piece(3), piece(4), inner_bias_out, piece(5), piece(6), piece(7),
    )


def solution(mesh):
    sheet, matrix, vector = P("wsh", "ctx", None), P("wsh", None), P("wsh")
    return jax.shard_map(
        local,
        mesh=mesh,
        in_specs=(sheet, matrix) + (matrix,) * 6 + (vector,) * 9 + (sheet,),
        out_specs=(sheet, sheet) + (matrix,) * 6 + (vector,) * 9,
        check_vma=False,
    )
```

```python
import functools
import math

import jax
import jax.numpy as jnp
from jax import lax
from jax.experimental import pallas as pl
from jax.experimental.pallas import tpu as pltpu
from jax.sharding import PartitionSpec as P

HEADS = 16
LANES = 128
EXTRA = 16
BF = jnp.bfloat16
F32 = jnp.float32
MIB = 1024 * 1024
IN_VMEM = pl.BlockSpec(memory_space=pltpu.VMEM)
IN_SMEM = pl.BlockSpec(memory_space=pltpu.SMEM)


def dot(a, b):
    return lax.dot_general(a, b, (((1,), (0,)), ((), ())), preferred_element_type=F32)


def dot_nt(a, b):
    return lax.dot_general(a, b, (((1,), (1,)), ((), ())), preferred_element_type=F32)


def dot_tn(a, b):
    return lax.dot_general(a, b, (((0,), (0,)), ((), ())), preferred_element_type=F32)


def struct(shape, dtype):
    return jax.ShapeDtypeStruct(shape, dtype)


def micros(us):
    return pl.CostEstimate(flops=int(us * 1e9), bytes_accessed=0, transcendentals=0)


def params(limit):
    return pltpu.CompilerParams(vmem_limit_bytes=min(limit, 60 * MIB))


def after(value, *others):
    return lax.optimization_barrier((value, others))[0]


def bytes_of(arrays):
    return sum(math.prod(a.shape) * a.dtype.itemsize for a in arrays)


def call(kernel, scalars, arrays, out_shape, us, name, scratch=(), room=6):
    limit = 60 * MIB if room is None else bytes_of(arrays) + bytes_of(out_shape) + bytes_of(scratch) + room * MIB
    return pl.pallas_call(
        kernel,
        in_specs=[IN_SMEM] * len(scalars) + [IN_VMEM] * len(arrays),
        out_specs=[IN_VMEM] * len(out_shape),
        out_shape=out_shape,
        scratch_shapes=list(scratch),
        compiler_params=params(limit),
        cost_estimate=micros(us),
        name=name,
    )(*scalars, *arrays)


def block_at(index, size):
    return pl.ds(pl.multiple_of(index * size, size), size)


def as_row(column):
    return jnp.broadcast_to(column, (column.shape[0], LANES)).T[0:1, :]


def add_up(parts):
    total = parts[0].astype(F32)
    for part in parts[1:]:
        total = total + part.astype(F32)
    return total


def pack_kernel(first_ref, q_ref, k_ref, v_ref, *refs):
    vectors, out_ref = refs[:-1], refs[-1]
    depth, wide = q_ref.shape[0], out_ref.shape[1] // 3
    lanes = pl.ds(pl.multiple_of(first_ref[0], LANES), wide)
    for i, ref in enumerate((q_ref, k_ref, v_ref)):
        out_ref[:depth, i * wide : (i + 1) * wide] = ref[:, lanes]
    rows = jnp.concatenate([ref[...].astype(F32) for ref in vectors], axis=0)
    per = 3 * wide // LANES
    height = out_ref.shape[0] - depth
    if rows.shape[0] < height * per:
        rows = jnp.concatenate([rows, jnp.zeros((height * per - rows.shape[0], LANES), F32)], axis=0)
    packed = [
        jnp.concatenate([rows[i * per + j : i * per + j + 1, :] for j in range(per)], axis=1) for i in range(height)
    ]
    out_ref[depth:, :] = jnp.concatenate(packed, axis=0).astype(BF)


def unpack_kernel(count, shard_ref, *refs):
    packs, (vec_ref, inner_ref) = refs[:count], refs[count:]
    depth = vec_ref.shape[1] // count
    vec_ref[...] = jnp.zeros_like(vec_ref)
    inner_ref[...] = jnp.zeros_like(inner_ref)
    for r, pack in enumerate(packs):
        at = shard_ref[r]
        wide = pack.shape[1] // LANES
        rows = pack[depth:, :].astype(F32)

        def piece(i):
            return rows[i // wide : i // wide + 1, i % wide * LANES : (i % wide + 1) * LANES]

        per = depth // LANES
        for i in range(8):
            for j in range(per):
                vec_ref[i : i + 1, block_at(at * per + j, LANES)] = piece(i * per + j)
        for j in range(inner_ref.shape[1] // LANES):
            inner_ref[block_at(at, 8), j * LANES : (j + 1) * LANES] = jnp.broadcast_to(piece(8 * per + j), (8, LANES))


def project_kernel(count, shards, cols, scale, shard_ref, place_ref, starts_ref, *refs):
    pieces, packs = refs[:count], refs[count : count + shards]
    bias_ref, w_ref, q_ref, k_ref, v_ref, qt_ref, kt_ref = refs[count + shards :]
    depth = w_ref.shape[0] // shards
    for r, pack in enumerate(packs):
        w_ref[block_at(shard_ref[r], depth), :] = pack[:depth, :]
    weight = w_ref[...]
    documents = starts_ref.shape[0]
    row = 0
    for p, piece in enumerate(pieces):
        rows = piece.shape[0]
        at = slice(row, row + rows)
        raw = dot(piece[...], weight)
        q_ref[at, :] = ((raw[:, :cols] + bias_ref[0:1, :]) * scale).astype(BF)
        k_ref[at, :] = raw[:, cols : 2 * cols].astype(BF)
        v_ref[at, :] = (raw[:, 2 * cols :] + bias_ref[1:2, :]).astype(BF)
        place = place_ref[p] + lax.broadcasted_iota(jnp.int32, (rows, LANES), 0)
        segment = jnp.full((rows, LANES), -1, jnp.int32)
        for j in range(documents):
            segment = segment + (starts_ref[j] <= place).astype(jnp.int32)
        lane = lax.broadcasted_iota(jnp.int32, (rows, LANES), 1)
        same = segment == lane
        qt_ref[at, :] = jnp.where(same | (lane >= documents), 0.0, -1e30).astype(BF)
        kt_ref[at, :] = jnp.where(same, 1.0, 0.0).astype(BF)
        row += rows


def head_lanes(rows, wide, h, size):
    lane = lax.broadcasted_iota(jnp.int32, (rows, wide), 1)
    return (lane >= h * size) & (lane < (h + 1) * size)


def attend_kernel(heads, size, q_ref, qt_ref, k_ref, kt_ref, v_ref, low_ref, o_ref, lse_ref):
    rows, wide = q_ref.shape
    keys = jnp.concatenate([k_ref[...], kt_ref[...]], axis=1)
    query, tail = q_ref[...], qt_ref[...]
    out = jnp.zeros((rows, wide), F32)
    for h in range(heads):
        mine = head_lanes(rows, wide, h, size)
        scores = dot_nt(jnp.concatenate([jnp.where(mine, query, jnp.zeros_like(query)), tail], axis=1), keys)
        top = jnp.max(scores, axis=1, keepdims=True)
        probs = jnp.exp(scores - top)
        total = jnp.sum(probs, axis=1, keepdims=True)
        out = jnp.where(mine, dot(probs.astype(BF), v_ref[...]) / total, out)
        lse_ref[h : h + 1, :] = as_row(top + jnp.log(total))
    o_ref[...] = out
    low_ref[...] = out.astype(BF)


def attend(q, qt, k, kt, v, rows, heads, size):
    length, wide = q.shape
    part = pl.BlockSpec((rows, wide), lambda i: (i, 0))
    whole = pl.BlockSpec((length, wide), lambda i: (0, 0))
    tail = pl.BlockSpec((length, LANES), lambda i: (0, 0))
    return pl.pallas_call(
        functools.partial(attend_kernel, heads, size),
        grid=(length // rows,),
        in_specs=[part, pl.BlockSpec((rows, LANES), lambda i: (i, 0)), whole, tail, whole],
        out_specs=[part, part, pl.BlockSpec((8, rows), lambda i: (0, i))],
        out_shape=[struct((length, wide), BF), struct((length, wide), F32), struct((8, length), F32)],
        compiler_params=params(8 * MIB + 20 * rows * length + 8 * bytes_of([q])),
        cost_estimate=micros(18),
        name="attend",
    )(q, qt, k, kt, v)


def attend_back_kernel(
    heads, size, scale, q_ref, qt_ref, k_ref, kt_ref, v_ref, mg_ref, o_ref, lse_ref, out_ref, kx, dk_acc, dv_acc
):
    step = pl.program_id(0)
    rows, wide = q_ref.shape

    @pl.when(step == 0)
    def _():
        dk_acc[...] = jnp.zeros_like(dk_acc)
        dv_acc[...] = jnp.zeros_like(dv_acc)
        kx[...] = k_ref[...].astype(F32).T.astype(BF)

    keys = jnp.concatenate([k_ref[...], kt_ref[...]], axis=1)
    query, tail, mg = q_ref[...], qt_ref[...], mg_ref[...]
    spread = mg.astype(F32) * o_ref[...]
    turned = []
    for h in range(heads):
        mine = head_lanes(rows, wide, h, size)
        query_h = jnp.where(mine, query, jnp.zeros_like(query))
        mg_h = jnp.where(mine, mg, jnp.zeros_like(mg))
        row_terms = as_row(jnp.sum(jnp.where(mine, spread, 0.0), axis=1, keepdims=True))
        scores = dot_nt(keys, jnp.concatenate([query_h, tail], axis=1))
        probs = jnp.exp(scores - lse_ref[h : h + 1, :])
        dv_acc[...] += dot(probs.astype(BF), mg_h)
        grads = (probs * (dot_nt(v_ref[...], mg_h) - row_terms)).astype(BF)
        dk_acc[...] += dot(grads, query_h)
        turned.append(dot(kx[h * size : (h + 1) * size, :], grads))
    if heads * size < wide:
        turned.append(jnp.zeros((wide - heads * size, rows), F32))
    at = block_at(step, rows)
    out_ref[at, :wide] = (jnp.concatenate(turned, axis=0).T * scale).astype(BF)

    @pl.when(step == pl.num_programs(0) - 1)
    def _():
        out_ref[:, wide : 2 * wide] = dk_acc[...].astype(BF)
        out_ref[:, 2 * wide :] = dv_acc[...].astype(BF)


def attend_back(q, qt, k, kt, v, mg, o, lse, rows, heads, size, scale):
    length, wide = q.shape
    part = pl.BlockSpec((rows, wide), lambda i: (i, 0))
    whole = pl.BlockSpec((length, wide), lambda i: (0, 0))
    tail = pl.BlockSpec((length, LANES), lambda i: (0, 0))
    return pl.pallas_call(
        functools.partial(attend_back_kernel, heads, size, scale),
        grid=(length // rows,),
        in_specs=[
            part, pl.BlockSpec((rows, LANES), lambda i: (i, 0)), whole, tail, whole, part, part,
            pl.BlockSpec((8, rows), lambda i: (0, i)),
        ],
        out_specs=pl.BlockSpec((length, 3 * wide), lambda i: (0, 0)),
        out_shape=struct((length, 3 * wide), BF),
        scratch_shapes=[
            pltpu.VMEM((wide, length), BF), pltpu.VMEM((length, wide), F32), pltpu.VMEM((length, wide), F32)
        ],
        compiler_params=params(60 * MIB),
        cost_estimate=micros(27),
        name="attend_back",
    )(q, qt, k, kt, v, mg, o, lse)


def normalize(source):
    mean = jnp.mean(source, axis=-1, keepdims=True)
    centered = source - mean
    root = lax.rsqrt(jnp.mean(centered * centered, axis=-1, keepdims=True) + 1e-05)
    return centered * root, root


def norm_back(normed, root, grad, gain):
    scaled = grad * gain
    mean = jnp.mean(scaled, axis=-1, keepdims=True)
    mix = jnp.mean(scaled * normed, axis=-1, keepdims=True)
    return root * (scaled - mean - normed * mix)


def column_sums(sums_ref, rows):
    sums_ref[...] = jnp.zeros_like(sums_ref)
    for i, row in enumerate(rows):
        sums_ref[i : i + 1, :] = jnp.sum(row, axis=0, keepdims=True)


def collected(refs, whole, halves):
    full = add_up([r[...] for r in refs[:whole]])
    if not halves:
        return full
    upper = add_up([r[...] for r in refs[whole : whole + halves]])
    lower = add_up([r[...] for r in refs[whole + halves : whole + 2 * halves]])
    return full + jnp.concatenate([upper, lower], axis=0)


def first_norm_kernel(count, offs_ref, x_ref, wo_ref, vec_ref, *refs):
    blocks, (hidden_ref, low_ref, normed_ref, root_ref) = refs[:count], refs[count:]
    wide = wo_ref.shape[0] // count
    out = x_ref[...].astype(F32) + vec_ref[2:3, :]
    for r, block in enumerate(blocks):
        out = out + dot(block[...], wo_ref[block_at(offs_ref[r], wide), :])
    normed, root = normalize(out)
    hidden = normed * vec_ref[3:4, :] + vec_ref[4:5, :]
    hidden_ref[...] = hidden
    low_ref[...] = hidden.astype(BF)
    normed_ref[...] = normed
    root_ref[...] = root


def second_norm_kernel(whole, halves, hidden_ref, vec_ref, cot_ref, *refs):
    parts, (res_ref, resid_ref, low_ref, sums_ref) = refs[:-4], refs[-4:]
    normed, root = normalize(hidden_ref[...] + collected(parts, whole, halves) + vec_ref[5:6, :])
    gain = vec_ref[6:7, :]
    res_ref[...] = (normed * gain + vec_ref[7:8, :]).astype(BF)
    grad = cot_ref[...].astype(F32)
    resid = norm_back(normed, root, grad, gain)
    resid_ref[...] = resid
    low = resid.astype(BF)
    low_ref[...] = low
    column_sums(sums_ref, [low.astype(F32), grad * normed, grad])


def first_back_kernel(count, whole, halves, offs_ref, resid_ref, normed_ref, root_ref, vec_ref, wo_ref, *refs):
    parts = refs[: whole + 2 * halves]
    first_ref, low_ref, sums_ref, *outs = refs[whole + 2 * halves :]
    wide = wo_ref.shape[0] // count
    grad = resid_ref[...] + collected(parts, whole, halves)
    normed = normed_ref[...]
    first = norm_back(normed, root_ref[...], grad, vec_ref[3:4, :])
    first_ref[...] = first
    low = first.astype(BF)
    low_ref[...] = low
    for r in range(count):
        outs[r][...] = dot_nt(low, wo_ref[block_at(offs_ref[r], wide), :]).astype(BF)
    column_sums(sums_ref, [low.astype(F32), grad * normed, grad])


def input_kernel(whole, halves, first_ref, *refs):
    parts, out_ref = refs[:-1], refs[-1]
    out_ref[...] = (first_ref[...] + collected(parts, whole, halves)).astype(BF)


def assemble_kernel(shards, strip, shard_ref, ids_ref, *refs):
    slabs, out_ref = refs[:-1], refs[-1]
    per = slabs[0].shape[0] // (shards * strip)
    depth = out_ref.shape[0] // shards
    for i, slab in enumerate(slabs):
        for b in range(per):
            for r in range(shards):
                row = pl.multiple_of(shard_ref[r] * depth + ids_ref[i * per + b] * strip, strip)
                out_ref[pl.ds(row, strip), :] = slab[(b * shards + r) * strip : (b * shards + r + 1) * strip, :]


def gelu_pair(source):
    bell = 0.5 * (1.0 + lax.erf(source * (0.5**0.5)))
    slope = bell + source * jnp.exp(-0.5 * source * source) * ((2.0 * jnp.pi) ** -0.5)
    return source * bell, slope


def forward_kernel(count, inner_ref, bias_ref, outer_ref, *refs):
    for p in range(count):
        act, slope = gelu_pair(dot(refs[p][...], inner_ref[...]) + bias_ref[...])
        low = act.astype(BF)
        refs[count + p][...] = low
        refs[2 * count + p][...] = slope.astype(BF)
        refs[3 * count + p][...] = dot(low, outer_ref[...]).astype(BF)


def backward_kernel(count, inner_ref, outer_ref, *refs):
    total = jnp.zeros((1, inner_ref.shape[1]), F32)
    for p in range(count):
        grad = (dot_nt(refs[p][...], outer_ref[...]) * refs[count + p][...].astype(F32)).astype(BF)
        refs[2 * count + p][...] = grad
        refs[3 * count + p][...] = dot_nt(grad, inner_ref[...]).astype(BF)
        total = total + jnp.sum(grad.astype(F32), axis=0, keepdims=True)
    refs[-1][...] = total


def products_kernel(count, shard_ref, *refs):
    acts, grads, hidden, inner = [refs[i * count : (i + 1) * count] for i in range(4)]
    *outs, out_ref, outer_acc, inner_acc = refs[4 * count :]
    for p in range(count):
        term = dot_tn(acts[p][...], grads[p][...])
        if p == 0:
            outer_acc[...] = term
        else:
            outer_acc[...] += term
    for r, out in enumerate(outs):
        out[...] = outer_acc[block_at(shard_ref[r], out.shape[0]), :].astype(BF)
    for p in range(count):
        term = dot_tn(hidden[p][...], inner[p][...])
        if p == 0:
            inner_acc[...] = term
        else:
            inner_acc[...] += term
    out_ref[...] = inner_acc[...].astype(BF)


def inner_outer_kernel(inner_ref, *refs):
    parts, out_ref = refs[:-1], refs[-1]
    total = add_up([r[...] for r in parts])
    units = total.shape[0]
    out_ref[:units, :] = total.astype(BF)
    times = out_ref.shape[1] // inner_ref.shape[1]
    rows = inner_ref.shape[0] // times
    for i in range(times):
        out_ref[units:, i * inner_ref.shape[1] : (i + 1) * inner_ref.shape[1]] = inner_ref[i * rows : (i + 1) * rows, :]


def finish_forward_kernel(units, all_ref, outer_ref, inner_ref):
    count, height, width = all_ref.shape
    rows = height - units
    times = inner_ref.shape[0] // rows
    share = width // times
    stretch = units * count
    for c in range(count):
        outer_ref[c * units : (c + 1) * units, :] = all_ref[c, :units, :].astype(F32)
        for i in range(times):
            for s in range(share // units):
                inner_ref[i * rows : (i + 1) * rows, s * stretch + c * units : s * stretch + (c + 1) * units] = all_ref[
                    c, units:, i * share + s * units : i * share + (s + 1) * units
                ].astype(F32)


def last_sum_kernel(count, *refs):
    packs, wos, out_ref = refs[:count], refs[count : 2 * count], refs[-1]
    total = add_up([r[...] for r in packs]).astype(BF)
    height = total.shape[0]
    for i in range(total.shape[1] // LANES):
        out_ref[i * height : (i + 1) * height, :] = total[:, i * LANES : (i + 1) * LANES]
    total = add_up([r[...] for r in wos]).astype(BF)
    base = total.shape[1] // LANES
    strip = total.shape[0]
    for i in range(base):
        row = height * 3 + i * strip
        out_ref[row : row + strip, :] = total[:, i * LANES : (i + 1) * LANES]


def into_kernel(factor, triple_ref, w_ref, *outs):
    rows = outs[0].shape[0]
    for r, out in enumerate(outs):
        term = dot_nt(triple_ref[r * rows : (r + 1) * rows, :], w_ref[...])
        out[...] = (term if factor == 1.0 else term * factor).astype(BF)


def qkv_product_kernel(count, shard_ref, triple_ref, one_ref, two_ref, inner_ref, *refs):
    pieces, outs, (acc, bias) = refs[:count], refs[count:-2], refs[-2:]
    row = 0
    bias[...] = jnp.zeros_like(bias)
    bias[0:1, :] = jnp.sum(triple_ref[...].astype(F32), axis=0, keepdims=True)
    for p, piece in enumerate(pieces):
        rows = piece.shape[0]
        term = dot_tn(piece[...], triple_ref[row : row + rows, :])
        if p == 0:
            acc[...] = term
        else:
            acc[...] += term
        row += rows
    depth = acc.shape[0] // len(outs)
    units = inner_ref.shape[1]
    for r, out in enumerate(outs):
        at = shard_ref[r]
        out[:depth, :] = acc[block_at(at, depth), :].astype(BF)
        for i in range(3):
            bias[1 + i : 2 + i, :depth] = one_ref[i : i + 1, block_at(at, depth)]
            bias[4 + i : 5 + i, :depth] = two_ref[i : i + 1, block_at(at, depth)]
        bias[7:8, 2 * LANES : 2 * LANES + units] = inner_ref[pl.ds(at, 1), :]
        out[depth:, :] = bias[...].astype(BF)


def finish_kernel(shard_ref, offs_ref, *refs):
    pieces, (q_ref, k_ref, v_ref, wo_ref, vec_ref, inner_ref, bias) = refs[:-7], refs[-7:]
    depth = q_ref.shape[0]
    height = depth + EXTRA
    cols = LANES
    total = None
    for r, block in enumerate(Cube.blocks(pieces)):
        block = jnp.concatenate([p[...] for p in block], axis=0)
        lanes = block_at(offs_ref[r], cols)
        for i, out in enumerate((q_ref, k_ref, v_ref)):
            out[:, lanes] = block[i * height : i * height + depth, :].astype(F32)
        tails = [block[i * height + depth : (i + 1) * height, :].astype(F32) for i in range(3)]
        bias[0:8, lanes] = jnp.broadcast_to(tails[0][0:1, :], (8, cols))
        bias[8:16, lanes] = jnp.broadcast_to(tails[2][0:1, :], (8, cols))
        inner_ref[:, lanes] = jnp.broadcast_to(tails[2][7:8, :], (8, cols))
        tail = jnp.concatenate(tails, axis=1)
        total = tail if total is None else total + tail
        strip = (block.shape[0] - 3 * height) * LANES // wo_ref.shape[1]
        for i in range(wo_ref.shape[1] // LANES):
            row = 3 * height + i * strip
            wo_ref[block_at(offs_ref[r], strip), i * LANES : (i + 1) * LANES] = block[row : row + strip, :].astype(F32)
    mine = block_at(shard_ref[0], depth)
    vec_ref[0:1, :] = bias[0:1, mine]
    vec_ref[1:2, :] = bias[8:9, mine]
    vec_ref[2:8, :] = total[1:7, :depth]


def flip(source, bit):
    return lax.ppermute(source, "ctx", [(i, i ^ bit) for i in range(8)])


def shard_flip(source, bit, shards):
    return lax.ppermute(source, "wsh", [(i, i ^ bit) for i in range(shards)])


class Cube:
    def __init__(self):
        self.count = 8

    def at(self, r):
        return lax.axis_index("ctx") ^ r

    def gather(self, own, work=None, early=(), late=()):
        half = own.shape[0] // 32 * 16
        side, down, core = flip(own, 2), flip(own, 4), flip(own, 1)
        if work is not None:
            first = work([own, core])
        side, down, core = after((side, down, core), *([first] if work is not None else early))
        far_a, far_b = flip(side[:half], 4), flip(down[half:], 2)
        side1, down1 = flip(side, 1), flip(down, 1)
        if work is not None:
            second = work([side, side1, down, down1])
        far_a, far_b = after((far_a, far_b), *([second] if work is not None else late))
        far1_a, far1_b = flip(far_a, 1), flip(far_b, 1)
        pieces = [own, core, side, side1, down, down1, far_a, far_b, far1_a, far1_b]
        if work is None:
            return pieces
        third = work(pieces[6:])
        return pieces, [[*a, *b, *c] for a, b, c in zip(first, second, third)]

    def gather_slab(self, own, first, second):
        pair = jnp.concatenate([own, after(flip(own, 2), first)], axis=0)
        four = jnp.concatenate([pair, after(flip(pair, 4), second)], axis=0)
        return [four, flip(four, 1)]

    slab_order = (0, 2, 4, 6, 1, 3, 5, 7)

    def scatter_slab(self, keep, send):
        def fold(half, other):
            return half.astype(F32) + other.astype(F32)

        four = fold(keep, flip(send, 1)).astype(BF)
        half = four.shape[0] // 2
        two = fold(four[:half], flip(four[half:], 2)).astype(BF)
        half = half // 2
        return fold(two[:half], flip(two[half:], 4)).astype(BF)

    def places(self, rows):
        own = [self.at(r) * rows for r in range(8)]
        half = rows // 2
        return own[:6] + [own[6], own[6] + half, own[7], own[7] + half]

    @staticmethod
    def blocks(pieces):
        return [(p,) for p in pieces[:6]] + [(pieces[6], pieces[7]), (pieces[8], pieces[9])]

    def scatter(self, pieces):
        own, core, side, side1, down, down1, far_a, far_b, far1_a, far1_b = pieces
        half = own.shape[0] // 2
        far_a = (far_a.astype(F32) + flip(far1_a, 1).astype(F32)).astype(BF)
        over_side = flip(far_a, 2)
        far_b = (far_b.astype(F32) + flip(far1_b, 1).astype(F32)).astype(BF)
        over_down = flip(far_b, 4)
        side = side.astype(F32) + flip(side1, 1).astype(F32)
        down = down.astype(F32) + flip(down1, 1).astype(F32)
        side_a = flip(side[:half].astype(BF), 2)
        down_b = flip(down[half:].astype(BF), 4)
        side_b = flip((side[half:] + over_down.astype(F32)).astype(BF), 2)
        down_a = flip((down[:half] + over_side.astype(F32)).astype(BF), 4)
        return [own, flip(core, 1), side_a, down_a, side_b, down_b], 2, 2, (over_side, over_down)

    def exchange(self, blocks):
        return [blocks[0]] + [flip(blocks[r], r) for r in range(1, 8)]


class Line:
    def __init__(self, count):
        self.count = count

    def at(self, r):
        return jnp.int32(r)

    def gather(self, own, work=None, early=(), late=()):
        pieces = list(lax.all_gather(own, "ctx", axis=0, tiled=False))
        if work is None:
            return pieces
        groups = [work(group) for group in grouped(pieces, 4)]
        return pieces, [[piece for part in parts for piece in part] for parts in zip(*groups)]

    def places(self, rows):
        return [jnp.int32(r * rows) for r in range(self.count)]

    def scatter(self, pieces):
        whole = jnp.concatenate(pieces, axis=0)
        return [lax.psum_scatter(whole, "ctx", scatter_dimension=0, tiled=True)], 1, 0, ()

    def exchange(self, blocks):
        return list(lax.all_to_all(jnp.stack(blocks), "ctx", 0, 0, tiled=False))


def grouped(items, size):
    return [items[i : i + size] for i in range(0, len(items), size)]


def local(
    tokens, starts, query_weight, key_weight, value_weight, output_weight, inner_weight, outer_weight,
    query_bias, value_bias, output_bias, first_gain, first_shift, inner_bias, outer_bias,
    second_gain, second_shift, cotangent,
):
    count, shards = lax.axis_size("ctx"), lax.axis_size("wsh")
    net = Cube() if count == 8 else Line(count)
    me, shard = lax.axis_index("ctx"), lax.axis_index("wsh")
    x = tokens[0]
    rows, width = x.shape
    length = rows * count
    size = width // HEADS
    heads = max(1, HEADS // count)
    copies = max(1, count // HEADS)
    cols = heads * size
    wide = -(-cols // LANES) * LANES
    depth = width // shards
    units = outer_weight.shape[0] // count
    strip = depth // count
    scale = size**-0.5
    shard_ids = jnp.stack([shard ^ r for r in range(shards)])
    offs = jnp.stack([net.at(r) // copies for r in range(0, count, copies)])
    places = jnp.stack(net.places(rows))

    first_col = me // copies * cols

    def own_columns(w):
        return jnp.pad(lax.dynamic_slice_in_dim(w, first_col, cols, 1), ((0, 0), (0, wide - cols)))

    weights, lane = [query_weight, key_weight, value_weight], first_col
    if cols % LANES:
        weights, lane = [own_columns(w) for w in weights], jnp.int32(0)
    vectors = [query_bias, value_bias, output_bias, first_gain, first_shift, outer_bias, second_gain,
               second_shift, inner_bias]
    vectors = [v.reshape(-1, LANES) for v in vectors]
    height = -(-sum(v.shape[0] for v in vectors) * LANES // (24 * wide)) * 8
    (pack,) = call(
        pack_kernel, [lane[None]], [*weights, *vectors], [struct((depth + height, 3 * wide), BF)], 2, "pack"
    )
    packs = [pack] + [shard_flip(pack, r, shards) for r in range(1, shards)]
    vec, inner_all = call(
        functools.partial(unpack_kernel, shards), [shard_ids], packs,
        [struct((8, width), F32), struct((8 * shards, inner_bias.shape[0]), F32)], 2, "unpack",
    )
    pieces = net.gather(x, early=[pack], late=[vec])
    wo_own = lax.dynamic_slice_in_dim(output_weight, me * strip, strip, 0)
    wo_own = after(wo_own, pieces[6:8])
    wo_parts = [wo_own] + [shard_flip(wo_own, r, shards) for r in range(1, shards)]
    bias = jnp.pad(lax.dynamic_slice(vec, (0, first_col), (8, cols)), ((0, 0), (0, wide - cols)))
    inner_b = lax.dynamic_slice_in_dim(inner_all[::8], me * units, units, 1).reshape(1, -1)

    qkv_rows = []
    done = 0
    for group in grouped(pieces, 10):
        group_rows = sum(p.shape[0] for p in group)
        sheet = struct((group_rows, wide), BF)
        tail = struct((group_rows, LANES), BF)
        qkv, *made = call(
            functools.partial(project_kernel, len(group), shards, wide, scale),
            [shard_ids, places[done : done + len(group)], starts[0]],
            [*group, *packs, bias],
            [struct((width, 3 * wide), BF), sheet, sheet, sheet, tail, tail],
            4, "project",
        )
        qkv_rows.append(made)
        done += len(group)
    q, k, v, qt, kt = [made[0] if len(made) == 1 else jnp.concatenate(made) for made in zip(*qkv_rows)]

    inner_own = jnp.concatenate(
        [lax.dynamic_slice_in_dim(inner_weight, s * units * count + me * units, units, 1) for s in range(shards)],
        axis=1,
    )
    outer_own = lax.dynamic_slice_in_dim(outer_weight, me * units, units, 0)
    inner_own, outer_own = after((inner_own, outer_own), packs, pieces[6:8])
    inner = lax.all_gather(inner_own, "wsh", axis=0, tiled=True)
    outer = lax.all_gather(outer_own, "wsh", axis=0, tiled=True)
    mixed_low, mixed, lse = attend(q, qt, k, kt, v, rows, heads, size)
    if isinstance(net, Cube):
        ids = jnp.stack([net.at(r) for r in net.slab_order])
        slabs = net.gather_slab(jnp.concatenate(wo_parts, axis=0), q, mixed_low)
        (wo,) = call(
            functools.partial(assemble_kernel, shards, strip), [shard_ids, ids], slabs,
            [struct((width, width), BF)], 2, "assemble",
        )
    else:
        wo_slab = jnp.zeros((shards, strip, width), BF)
        for r in range(shards):
            wo_slab = lax.dynamic_update_slice(wo_slab, wo_parts[r][None], (shard ^ r, jnp.int32(0), jnp.int32(0)))
        wo = lax.all_gather(wo_slab, "ctx", axis=0, tiled=False)
        wo = wo.transpose(1, 0, 2, 3).reshape(width, width)

    blocks = net.exchange([mixed_low[r * rows : (r + 1) * rows, :cols] for r in range(count)])[::copies]
    groups = len(blocks)
    full, low_full, tall = struct((rows, width), F32), struct((rows, width), BF), struct((rows, 1), F32)
    sums = struct((8, width), F32)
    hidden, hidden_low, normed, root = call(
        functools.partial(first_norm_kernel, groups), [offs], [x, wo, vec, *blocks],
        [full, low_full, full, tall], 5, "first_norm",
    )

    def forward(group):
        sizes = [p.shape[0] for p in group]
        mids = [struct((s, units * shards), BF) for s in sizes]
        made = call(
            functools.partial(forward_kernel, len(group)), [], [inner, inner_b, outer, *group],
            mids + mids + [struct((s, width), BF) for s in sizes], 1.5 * sum(sizes) / 256, "forward",
        )
        n = len(group)
        return made[:n], made[n : 2 * n], made[2 * n :]

    hidden_all, (acts, slopes, branch) = net.gather(hidden_low, forward)
    parts, n_whole, n_half, _ = net.scatter(branch)
    result, resid, branch_grad, sums_two = call(
        functools.partial(second_norm_kernel, n_whole, n_half), [], [hidden, vec, cotangent[0], *parts],
        [low_full, full, low_full, sums], 4, "second_norm",
    )

    inner_sums, waiting = [], list(slopes)

    def backward(group):
        sizes = [p.shape[0] for p in group]
        n = len(group)
        slope, waiting[:n] = waiting[:n], []
        made = call(
            functools.partial(backward_kernel, n), [], [inner, outer, *group, *slope],
            [struct((s, units * shards), BF) for s in sizes]
            + [struct((s, width), BF) for s in sizes]
            + [struct((1, units * shards), F32)],
            1.5 * sum(sizes) / 256, "backward",
        )
        inner_sums.append(made[-1])
        return made[:n], made[n:-1]

    grad_all, (inner_grads, hidden_grads) = net.gather(branch_grad, backward)
    parts, n_whole, n_half, moved = net.scatter(hidden_grads)
    *outer_parts, inner_wg = call(
        functools.partial(products_kernel, len(acts)), [shard_ids],
        [*after(acts, moved), *grad_all, *hidden_all, *inner_grads],
        [struct((units, width), BF)] * shards + [struct((width, units * shards), BF)], 12, "products",
        [pltpu.VMEM((units * shards, width), F32), pltpu.VMEM((width, units * shards), F32)], None,
    )
    parts = after(parts, inner_wg)
    outer_parts = [outer_parts[0]] + [shard_flip(outer_parts[r], r, shards) for r in range(1, shards)]
    inner_own_grad = lax.psum_scatter(inner_wg, "wsh", scatter_dimension=0, tiled=True)

    first, attn_grad, sums_one, *mixed_grads = call(
        functools.partial(first_back_kernel, groups, n_whole, n_half), [offs],
        [resid, normed, root, vec, wo, *parts],
        [full, low_full, sums] + [struct((rows, cols), BF)] * groups, 5, "first_back",
    )
    if copies > 1:
        mixed_grads = [b for b in mixed_grads for _ in range(copies)]
    exchanged = net.exchange(mixed_grads)
    mixed_grad = jnp.concatenate(exchanged, axis=0)
    mixed_grad = jnp.pad(mixed_grad, ((0, 0), (0, wide - cols)))

    order = [0, 4, 2, 6, 1, 5, 3, 7] if isinstance(net, Cube) else list(range(count))
    halves = 2 if isinstance(net, Cube) else 1
    ids = jnp.stack([net.at(r) for r in order])

    def mixed_product(offs_ref, ids_ref, low_ref, *refs):
        outs, acc = refs[groups:-1], refs[-1]
        for r, block in enumerate(refs[:groups]):
            acc[block_at(offs_ref[r], cols), :] = dot_tn(block[...], low_ref[...])
        per = count // halves
        for i in range(count):
            for s in range(shards):
                row = (i % per * shards + s) * strip
                at = pl.multiple_of(s * depth + ids_ref[i] * strip, strip)
                outs[i // per][row : row + strip, :] = acc[pl.ds(at, strip), :].astype(BF)

    wo_grad = call(
        mixed_product, [offs, ids], [after(attn_grad, exchanged[1]), *blocks],
        [struct((width // halves, width), BF)] * halves, 4, "mixed_product", [pltpu.VMEM((width, width), F32)],
    )
    if isinstance(net, Cube):
        wo_grad = net.scatter_slab(*wo_grad)
    else:
        wo_grad = lax.psum_scatter(wo_grad[0], "ctx", scatter_dimension=0, tiled=True)
    wo_parts = [lax.dynamic_slice_in_dim(wo_grad, (shard ^ r) * strip, strip, 0) for r in range(shards)]
    wo_parts = [wo_parts[0]] + [shard_flip(wo_parts[r], r, shards) for r in range(1, shards)]
    triple = attend_back(q, qt, k, kt, v, mixed_grad, mixed, lse, rows, heads, size, scale)
    (forward_own,) = call(
        inner_outer_kernel, [], [inner_own_grad, *after(outer_parts, triple)],
        [struct((units + depth * units * shards // width, width), BF)], 2, "pack_forward",
    )
    forward_all = lax.all_gather(forward_own, "ctx", axis=0, tiled=False)
    inner_sum = add_up(inner_sums).reshape(shards, units)
    qkv_pack = struct((depth + EXTRA, 3 * wide), BF)
    packs = call(
        functools.partial(qkv_product_kernel, len(pieces)), [shard_ids],
        [triple, sums_one, sums_two, inner_sum, *pieces], [qkv_pack] * shards, 5, "qkv_product",
        [pltpu.VMEM((width, 3 * wide), F32), pltpu.VMEM((EXTRA, 3 * wide), F32)], None,
    )
    into = call(
        functools.partial(into_kernel, 1.0 / copies), [], [after(triple, packs), qkv], [low_full] * count, 3, "into",
    )
    if isinstance(net, Cube):
        half = rows // 2
        into = [*into[:6]] + [into[6][:half], into[6][half:], into[7][:half], into[7][half:]]
    parts, n_whole, n_half, _ = net.scatter(into)
    (input_grad,) = call(
        functools.partial(input_kernel, n_whole, n_half), [], [first, *parts], [low_full], 2, "input_sum"
    )
    packs = [packs[0]] + [shard_flip(packs[r], r, shards) for r in range(1, shards)]
    if isinstance(net, Cube):
        (last_own,) = call(
            functools.partial(last_sum_kernel, shards), [], [*packs, *wo_parts],
            [struct((3 * (depth + EXTRA) + strip * width // LANES, LANES), BF)], 2, "last_sum",
        )
        square = struct((depth, width), F32)
        query_out, key_out, value_out, wo_out, vecs, inner_vec = call(
            finish_kernel, [shard_ids, offs], net.gather(last_own),
            [square, square, square, square, struct((8, depth), F32), struct((8, units * count), F32)], 4, "finish",
            [pltpu.VMEM((16, width), F32)],
        )
        outer_out, inner_out = call(
            functools.partial(finish_forward_kernel, units), [], [forward_all],
            [struct((units * count, width), F32), struct((depth, units * count * shards), F32)], 6, "finish_forward",
        )
        vecs = [vecs[i] for i in range(8)]
        inner_vec = inner_vec[0]
    else:

        def everywhere(parts):
            return lax.all_gather(add_up(parts).astype(BF), "ctx", axis=0, tiled=False).astype(F32)

        wo_out = everywhere(wo_parts).reshape(depth, width)
        gathered = everywhere(packs)
        out3 = gathered[::copies, :depth].reshape(-1, depth, 3, wide)[..., :cols]
        query_out, key_out, value_out = out3.transpose(2, 1, 0, 3).reshape(3, depth, width)
        tail = gathered[:, depth:]
        both = tail[::copies, 0].reshape(-1, 3, wide)[..., :cols].transpose(1, 0, 2).reshape(3, width)
        both = lax.dynamic_slice_in_dim(both, shard * depth, depth, 1)
        six = jnp.sum(tail[:, 1:7, :depth], axis=0)
        vecs = [both[0], both[2]] + [six[i] for i in range(6)]
        inner_vec = tail[:, 7, 2 * wide : 2 * wide + units].reshape(-1)
        forward_all = forward_all.astype(F32)
        outer_out = forward_all[:, :units].reshape(-1, width)
        times = width // (units * shards)
        inner_out = forward_all[:, units:].reshape(count, depth // times, times, shards, units)
        inner_out = inner_out.transpose(2, 1, 3, 0, 4).reshape(depth, -1)
    return (
        result[None], input_grad[None], query_out, key_out, value_out, wo_out, inner_out, outer_out,
        vecs[0], vecs[1], vecs[2], vecs[3], vecs[4], inner_vec, vecs[5], vecs[6], vecs[7],
    )


def solution(mesh):
    sheet, matrix, vector = P("wsh", "ctx", None), P("wsh", None), P("wsh")
    return jax.shard_map(
        local,
        mesh=mesh,
        in_specs=(sheet, matrix) + (matrix,) * 6 + (vector,) * 9 + (sheet,),
        out_specs=(sheet, sheet) + (matrix,) * 6 + (vector,) * 9,
        check_vma=False,
    )
```

```python
import functools
import math

import jax
import jax.numpy as jnp
from jax import lax
from jax.experimental import pallas as pl
from jax.experimental.pallas import tpu as pltpu
from jax.sharding import PartitionSpec as P

HEADS = 16
LANES = 128
EXTRA = 16
BF = jnp.bfloat16
F32 = jnp.float32
MIB = 1024 * 1024
IN_VMEM = pl.BlockSpec(memory_space=pltpu.VMEM)
IN_SMEM = pl.BlockSpec(memory_space=pltpu.SMEM)


def dot(a, b):
    return lax.dot_general(a, b, (((1,), (0,)), ((), ())), preferred_element_type=F32)


def dot_nt(a, b):
    return lax.dot_general(a, b, (((1,), (1,)), ((), ())), preferred_element_type=F32)


def dot_tn(a, b):
    return lax.dot_general(a, b, (((0,), (0,)), ((), ())), preferred_element_type=F32)


def struct(shape, dtype):
    return jax.ShapeDtypeStruct(shape, dtype)


def micros(us):
    return pl.CostEstimate(flops=int(us * 1e9), bytes_accessed=0, transcendentals=0)


def params(limit):
    return pltpu.CompilerParams(vmem_limit_bytes=min(limit, 60 * MIB))


def after(value, *others):
    return lax.optimization_barrier((value, others))[0]


def bytes_of(arrays):
    return sum(math.prod(a.shape) * a.dtype.itemsize for a in arrays)


def call(kernel, scalars, arrays, out_shape, us, name, scratch=(), room=6):
    limit = 60 * MIB if room is None else bytes_of(arrays) + bytes_of(out_shape) + bytes_of(scratch) + room * MIB
    return pl.pallas_call(
        kernel,
        in_specs=[IN_SMEM] * len(scalars) + [IN_VMEM] * len(arrays),
        out_specs=[IN_VMEM] * len(out_shape),
        out_shape=out_shape,
        scratch_shapes=list(scratch),
        compiler_params=params(limit),
        cost_estimate=micros(us),
        name=name,
    )(*scalars, *arrays)


def block_at(index, size):
    return pl.ds(pl.multiple_of(index * size, size), size)


def as_row(column):
    return jnp.broadcast_to(column, (column.shape[0], LANES)).T[0:1, :]


def add_up(parts):
    total = parts[0].astype(F32)
    for part in parts[1:]:
        total = total + part.astype(F32)
    return total


def pack_kernel(first_ref, q_ref, k_ref, v_ref, *refs):
    vectors, out_ref = refs[:-1], refs[-1]
    depth, wide = q_ref.shape[0], out_ref.shape[1] // 3
    lanes = pl.ds(pl.multiple_of(first_ref[0], LANES), wide)
    for i, ref in enumerate((q_ref, k_ref, v_ref)):
        out_ref[:depth, i * wide : (i + 1) * wide] = ref[:, lanes]
    rows = jnp.concatenate([ref[...].astype(F32) for ref in vectors], axis=0)
    per = 3 * wide // LANES
    height = out_ref.shape[0] - depth
    if rows.shape[0] < height * per:
        rows = jnp.concatenate([rows, jnp.zeros((height * per - rows.shape[0], LANES), F32)], axis=0)
    packed = [
        jnp.concatenate([rows[i * per + j : i * per + j + 1, :] for j in range(per)], axis=1) for i in range(height)
    ]
    out_ref[depth:, :] = jnp.concatenate(packed, axis=0).astype(BF)


def unpack_kernel(count, shard_ref, *refs):
    packs, (vec_ref, inner_ref) = refs[:count], refs[count:]
    depth = vec_ref.shape[1] // count
    vec_ref[...] = jnp.zeros_like(vec_ref)
    inner_ref[...] = jnp.zeros_like(inner_ref)
    for r, pack in enumerate(packs):
        at = shard_ref[r]
        wide = pack.shape[1] // LANES
        rows = pack[depth:, :].astype(F32)

        def piece(i):
            return rows[i // wide : i // wide + 1, i % wide * LANES : (i % wide + 1) * LANES]

        per = depth // LANES
        for i in range(8):
            for j in range(per):
                vec_ref[i : i + 1, block_at(at * per + j, LANES)] = piece(i * per + j)
        for j in range(inner_ref.shape[1] // LANES):
            inner_ref[block_at(at, 8), j * LANES : (j + 1) * LANES] = jnp.broadcast_to(piece(8 * per + j), (8, LANES))


def project_kernel(count, shards, cols, scale, shard_ref, place_ref, starts_ref, *refs):
    pieces, packs = refs[:count], refs[count : count + shards]
    bias_ref, w_ref, q_ref, k_ref, v_ref, qt_ref, kt_ref = refs[count + shards :]
    depth = w_ref.shape[0] // shards
    for r, pack in enumerate(packs):
        w_ref[block_at(shard_ref[r], depth), :] = pack[:depth, :]
    weight = w_ref[...]
    documents = starts_ref.shape[0]
    row = 0
    for p, piece in enumerate(pieces):
        rows = piece.shape[0]
        at = slice(row, row + rows)
        raw = dot(piece[...], weight)
        q_ref[at, :] = ((raw[:, :cols] + bias_ref[0:1, :]) * scale).astype(BF)
        k_ref[at, :] = raw[:, cols : 2 * cols].astype(BF)
        v_ref[at, :] = (raw[:, 2 * cols :] + bias_ref[1:2, :]).astype(BF)
        place = place_ref[p] + lax.broadcasted_iota(jnp.int32, (rows, LANES), 0)
        segment = jnp.full((rows, LANES), -1, jnp.int32)
        for j in range(documents):
            segment = segment + (starts_ref[j] <= place).astype(jnp.int32)
        lane = lax.broadcasted_iota(jnp.int32, (rows, LANES), 1)
        same = segment == lane
        qt_ref[at, :] = jnp.where(same | (lane >= documents), 0.0, -1e30).astype(BF)
        kt_ref[at, :] = jnp.where(same, 1.0, 0.0).astype(BF)
        row += rows


def head_lanes(rows, wide, h, size):
    lane = lax.broadcasted_iota(jnp.int32, (rows, wide), 1)
    return (lane >= h * size) & (lane < (h + 1) * size)


def attend_kernel(heads, size, q_ref, qt_ref, k_ref, kt_ref, v_ref, low_ref, o_ref, lse_ref):
    rows, wide = q_ref.shape
    keys = jnp.concatenate([k_ref[...], kt_ref[...]], axis=1)
    query, tail = q_ref[...], qt_ref[...]
    out = jnp.zeros((rows, wide), F32)
    for h in range(heads):
        mine = head_lanes(rows, wide, h, size)
        scores = dot_nt(jnp.concatenate([jnp.where(mine, query, jnp.zeros_like(query)), tail], axis=1), keys)
        top = jnp.max(scores, axis=1, keepdims=True)
        probs = jnp.exp(scores - top)
        total = jnp.sum(probs, axis=1, keepdims=True)
        out = jnp.where(mine, dot(probs.astype(BF), v_ref[...]) / total, out)
        lse_ref[h : h + 1, :] = as_row(top + jnp.log(total))
    o_ref[...] = out
    low_ref[...] = out.astype(BF)


def attend(q, qt, k, kt, v, rows, heads, size, low, high):
    length, wide = q.shape
    part = pl.BlockSpec((rows, wide), lambda i: (i + low, 0))
    whole = pl.BlockSpec((length, wide), lambda i: (0, 0))
    tail = pl.BlockSpec((length, LANES), lambda i: (0, 0))
    out = pl.BlockSpec((rows, wide), lambda i: (i, 0))
    count = (high - low) * rows
    return pl.pallas_call(
        functools.partial(attend_kernel, heads, size),
        grid=(high - low,),
        in_specs=[part, pl.BlockSpec((rows, LANES), lambda i: (i + low, 0)), whole, tail, whole],
        out_specs=[out, out, pl.BlockSpec((8, rows), lambda i: (0, i))],
        out_shape=[struct((count, wide), BF), struct((count, wide), F32), struct((8, count), F32)],
        compiler_params=params(8 * MIB + 20 * rows * length + 8 * bytes_of([q])),
        cost_estimate=micros(9),
        name="attend",
    )(q, qt, k, kt, v)


def attend_back_kernel(heads, size, scale, first, last, count, done, q_ref, qt_ref, k_ref, kt_ref, v_ref, o_ref, lse_ref, *refs):
    mgs, refs = refs[:count], refs[count:]
    prior = ()
    if not first:
        prior, refs = refs[:3], refs[3:]
    if last:
        out_ref, kx, mg_s, dk_acc, dv_acc = refs
    else:
        out_ref, dk_acc, dv_acc, kx, mg_s = refs
    step = pl.program_id(0)
    rows, wide = q_ref.shape

    @pl.when(step == 0)
    def _():
        if first:
            dk_acc[...] = jnp.zeros_like(dk_acc)
            dv_acc[...] = jnp.zeros_like(dv_acc)
        else:
            out_ref[:done, :wide] = prior[0][...]
            dk_acc[...] = prior[1][...]
            dv_acc[...] = prior[2][...]
        kx[...] = k_ref[...].astype(F32).T.astype(BF)

    for i in range(count):

        @pl.when(step == i)
        def _(i=i):
            mg_s[...] = mgs[i][...]

    keys = jnp.concatenate([k_ref[...], kt_ref[...]], axis=1)
    query, tail, mg = q_ref[...], qt_ref[...], mg_s[...]
    spread = mg.astype(F32) * o_ref[...]
    turned = []
    for h in range(heads):
        mine = head_lanes(rows, wide, h, size)
        query_h = jnp.where(mine, query, jnp.zeros_like(query))
        mg_h = jnp.where(mine, mg, jnp.zeros_like(mg))
        row_terms = as_row(jnp.sum(jnp.where(mine, spread, 0.0), axis=1, keepdims=True))
        scores = dot_nt(keys, jnp.concatenate([query_h, tail], axis=1))
        probs = jnp.exp(scores - lse_ref[h : h + 1, :])
        dv_acc[...] += dot(probs.astype(BF), mg_h)
        grads = (probs * (dot_nt(v_ref[...], mg_h) - row_terms)).astype(BF)
        dk_acc[...] += dot(grads, query_h)
        turned.append(dot(kx[h * size : (h + 1) * size, :], grads))
    if heads * size < wide:
        turned.append(jnp.zeros((wide - heads * size, rows), F32))
    at = pl.ds(pl.multiple_of(done + step * rows, rows), rows) if last else block_at(step, rows)
    out_ref[at, :wide] = (jnp.concatenate(turned, axis=0).T * scale).astype(BF)
    if last:

        @pl.when(step == pl.num_programs(0) - 1)
        def _():
            out_ref[:, wide : 2 * wide] = dk_acc[...].astype(BF)
            out_ref[:, 2 * wide :] = dv_acc[...].astype(BF)


def attend_back(q, qt, k, kt, v, mgs, o, lse, rows, heads, size, scale, low, high, prior):
    length, wide = q.shape
    last = high * rows == length
    fixed = lambda i: (0, 0)
    whole = pl.BlockSpec((length, wide), fixed)
    full = struct((length, wide), F32)
    scratch = [pltpu.VMEM((wide, length), BF), pltpu.VMEM((rows, wide), BF)]
    if last:
        out_specs = pl.BlockSpec((length, 3 * wide), fixed)
        out_shape = struct((length, 3 * wide), BF)
        scratch += [pltpu.VMEM((length, wide), F32)] * 2
    else:
        count = (high - low) * rows
        out_specs = [pl.BlockSpec((count, wide), fixed), whole, whole]
        out_shape = [struct((count, wide), BF), full, full]
    return pl.pallas_call(
        functools.partial(
            attend_back_kernel, heads, size, scale, prior is None, last, high - low, low * rows
        ),
        grid=(high - low,),
        in_specs=[
            pl.BlockSpec((rows, wide), lambda i: (i + low, 0)),
            pl.BlockSpec((rows, LANES), lambda i: (i + low, 0)),
            whole,
            pl.BlockSpec((length, LANES), fixed),
            whole,
            pl.BlockSpec((rows, wide), lambda i: (i, 0)),
            pl.BlockSpec((8, rows), lambda i: (0, i)),
        ]
        + [pl.BlockSpec((rows, wide), fixed)] * (high - low)
        + ([] if prior is None else [pl.BlockSpec((low * rows, wide), fixed), whole, whole]),
        out_specs=out_specs,
        out_shape=out_shape,
        scratch_shapes=scratch,
        compiler_params=params(60 * MIB),
        cost_estimate=micros(25),
        name="attend_back",
    )(q, qt, k, kt, v, o, lse, *mgs, *(prior or ()))


def normalize(source):
    mean = jnp.mean(source, axis=-1, keepdims=True)
    centered = source - mean
    root = lax.rsqrt(jnp.mean(centered * centered, axis=-1, keepdims=True) + 1e-05)
    return centered * root, root


def norm_back(normed, root, grad, gain):
    scaled = grad * gain
    mean = jnp.mean(scaled, axis=-1, keepdims=True)
    mix = jnp.mean(scaled * normed, axis=-1, keepdims=True)
    return root * (scaled - mean - normed * mix)


def column_sums(sums_ref, rows):
    sums_ref[...] = jnp.zeros_like(sums_ref)
    for i, row in enumerate(rows):
        sums_ref[i : i + 1, :] = jnp.sum(row, axis=0, keepdims=True)


def collected(refs, whole, halves):
    full = add_up([r[...] for r in refs[:whole]])
    if not halves:
        return full
    upper = add_up([r[...] for r in refs[whole : whole + halves]])
    lower = add_up([r[...] for r in refs[whole + halves : whole + 2 * halves]])
    return full + jnp.concatenate([upper, lower], axis=0)


def first_norm_kernel(count, offs_ref, x_ref, wo_ref, vec_ref, *refs):
    blocks, (low_ref, normed_ref, root_ref) = refs[:count], refs[count:]
    wide = wo_ref.shape[0] // count
    out = x_ref[...].astype(F32) + vec_ref[2:3, :]
    for r, block in enumerate(blocks):
        out = out + dot(block[...], wo_ref[block_at(offs_ref[r], wide), :])
    normed, root = normalize(out)
    low_ref[...] = (normed * vec_ref[3:4, :] + vec_ref[4:5, :]).astype(BF)
    normed_ref[...] = normed.astype(BF)
    root_ref[...] = root


def second_norm_kernel(whole, halves, hidden_ref, vec_ref, cot_ref, *refs):
    parts, (res_ref, low_ref, sums_ref) = refs[:-3], refs[-3:]
    normed, root = normalize(hidden_ref[...].astype(F32) + collected(parts, whole, halves) + vec_ref[5:6, :])
    gain = vec_ref[6:7, :]
    res_ref[...] = (normed * gain + vec_ref[7:8, :]).astype(BF)
    grad = cot_ref[...].astype(F32)
    low = norm_back(normed, root, grad, gain).astype(BF)
    low_ref[...] = low
    column_sums(sums_ref, [low.astype(F32), grad * normed, grad])


def first_back_kernel(count, whole, halves, offs_ref, resid_ref, normed_ref, root_ref, vec_ref, wo_ref, *refs):
    parts = refs[: whole + 2 * halves]
    low_ref, sums_ref, *outs = refs[whole + 2 * halves :]
    wide = wo_ref.shape[0] // count
    grad = resid_ref[...].astype(F32) + collected(parts, whole, halves)
    normed = normed_ref[...].astype(F32)
    low = norm_back(normed, root_ref[...], grad, vec_ref[3:4, :]).astype(BF)
    low_ref[...] = low
    for r in range(count):
        outs[r][...] = dot_nt(low, wo_ref[block_at(offs_ref[r], wide), :]).astype(BF)
    column_sums(sums_ref, [low.astype(F32), grad * normed, grad])


def input_kernel(whole, halves, first_ref, *refs):
    parts, out_ref = refs[:-1], refs[-1]
    out_ref[...] = (first_ref[...].astype(F32) + collected(parts, whole, halves)).astype(BF)


def assemble_kernel(shards, strip, shard_ref, ids_ref, *refs):
    slabs, out_ref = refs[:-1], refs[-1]
    per = slabs[0].shape[0] // (shards * strip)
    depth = out_ref.shape[0] // shards
    for i, slab in enumerate(slabs):
        for b in range(per):
            for r in range(shards):
                row = pl.multiple_of(shard_ref[r] * depth + ids_ref[i * per + b] * strip, strip)
                out_ref[pl.ds(row, strip), :] = slab[(b * shards + r) * strip : (b * shards + r + 1) * strip, :]


def gelu_pair(source):
    bell = 0.5 * (1.0 + lax.erf(source * (0.5**0.5)))
    slope = bell + source * jnp.exp(-0.5 * source * source) * ((2.0 * jnp.pi) ** -0.5)
    return source * bell, slope


def forward_kernel(count, inner_ref, bias_ref, outer_ref, *refs):
    for p in range(count):
        act, slope = gelu_pair(dot(refs[p][...], inner_ref[...]) + bias_ref[...])
        low = act.astype(BF)
        refs[count + p][...] = low
        refs[2 * count + p][...] = slope.astype(BF)
        refs[3 * count + p][...] = dot(low, outer_ref[...]).astype(BF)


def backward_kernel(count, inner_ref, outer_ref, *refs):
    total = jnp.zeros((1, inner_ref.shape[1]), F32)
    for p in range(count):
        grad = (dot_nt(refs[p][...], outer_ref[...]) * refs[count + p][...].astype(F32)).astype(BF)
        refs[2 * count + p][...] = grad
        refs[3 * count + p][...] = dot_nt(grad, inner_ref[...]).astype(BF)
        total = total + jnp.sum(grad.astype(F32), axis=0, keepdims=True)
    refs[-1][...] = total


def early_product_kernel(count, *refs):
    acts, grads, hidden, inner = [refs[i * count : (i + 1) * count] for i in range(4)]
    outer_ref, inner_ref = refs[4 * count :]
    for left, right, out in ((acts, grads, outer_ref), (hidden, inner, inner_ref)):
        for p in range(count):
            term = dot_tn(left[p][...], right[p][...])
            if p == 0:
                out[...] = term
            else:
                out[...] += term


def late_product_kernel(count, given, shards, *refs):
    sources, refs = refs[: 4 * count + given], refs[4 * count + given :]
    out_ref, buffers, (outer_acc, inner_acc, sems) = refs[0], refs[1 : 4 * count + 1], refs[4 * count + 1 :]
    targets = [*buffers, outer_acc, inner_acc]
    copies = [pltpu.make_async_copy(a, b, sems.at[i]) for i, (a, b) in enumerate(zip(sources, targets))]
    order = [4 * count + i for i in range(given)]
    order += [i + g * count for g in (0, 2) for p in range(count) for i in (p, count + p)]
    for i in order:
        copies[i].start()
    units = outer_acc.shape[0] // shards
    height = out_ref.shape[0] // shards
    depth, share = inner_acc.shape[0] // shards, inner_acc.shape[1]
    for g, acc in ((0, outer_acc), (2, inner_acc)):
        if given:
            copies[4 * count + g // 2].wait()
        for p in range(count):
            left, right = g * count + p, (g + 1) * count + p
            copies[left].wait()
            copies[right].wait()
            term = dot_tn(buffers[left][...], buffers[right][...])
            if not given and p == 0:
                acc[...] = term
            else:
                acc[...] += term
    rows = height - units
    for s in range(shards):
        out_ref[s * height : s * height + units, :] = outer_acc[s * units : (s + 1) * units, :].astype(BF)
        for i in range(depth // rows):
            out_ref[s * height + units : (s + 1) * height, i * share : (i + 1) * share] = inner_acc[
                s * depth + i * rows : s * depth + (i + 1) * rows, :
            ].astype(BF)


def weights_kernel(units, all_ref, inner_ref, outer_ref):
    shards, height, width = all_ref.shape
    rows = height - units
    share = inner_ref.shape[1]
    for s in range(shards):
        outer_ref[s * units : (s + 1) * units, :] = all_ref[s, :units, :]
        for i in range(width // share):
            row = (s * (width // share) + i) * rows
            inner_ref[row : row + rows, :] = all_ref[s, units:, i * share : (i + 1) * share]


def finish_forward_kernel(units, all_ref, outer_ref, inner_ref):
    count, height, width = all_ref.shape
    rows = height - units
    times = inner_ref.shape[0] // rows
    share = width // times
    stretch = units * count
    for c in range(count):
        outer_ref[c * units : (c + 1) * units, :] = all_ref[c, :units, :].astype(F32)
        for i in range(times):
            for s in range(share // units):
                inner_ref[i * rows : (i + 1) * rows, s * stretch + c * units : s * stretch + (c + 1) * units] = all_ref[
                    c, units:, i * share + s * units : i * share + (s + 1) * units
                ].astype(F32)


def into_kernel(factor, order, triple_ref, w_ref, *outs):
    rows = triple_ref.shape[0] // len(order)
    per = len(order) // len(outs)
    for i, r in enumerate(order):
        term = dot_nt(triple_ref[r * rows : (r + 1) * rows, :], w_ref[...])
        at = i % per * rows
        outs[i // per][at : at + rows, :] = (term if factor == 1.0 else term * factor).astype(BF)


def qkv_product_kernel(count, shard_ref, triple_ref, one_ref, two_ref, inner_ref, wo_ref, *refs):
    pieces, outs, (acc, bias) = refs[:count], refs[count:-2], refs[-2:]
    row = 0
    bias[...] = jnp.zeros_like(bias)
    bias[0:1, :] = jnp.sum(triple_ref[...].astype(F32), axis=0, keepdims=True)
    for p, piece in enumerate(pieces):
        rows = piece.shape[0]
        term = dot_tn(piece[...], triple_ref[row : row + rows, :])
        if p == 0:
            acc[...] = term
        else:
            acc[...] += term
        row += rows
    depth = acc.shape[0] // len(outs)
    units = inner_ref.shape[1]
    strip = wo_ref.shape[0] // len(outs)
    height = depth + EXTRA
    for r, out in enumerate(outs):
        at = shard_ref[r]
        for i in range(3):
            bias[1 + i : 2 + i, :depth] = one_ref[i : i + 1, block_at(at, depth)]
            bias[4 + i : 5 + i, :depth] = two_ref[i : i + 1, block_at(at, depth)]
        bias[7:8, 2 * LANES : 2 * LANES + units] = inner_ref[pl.ds(at, 1), :]
        for i in range(3):
            lanes = slice(i * LANES, (i + 1) * LANES)
            out[i * height : i * height + depth, :] = acc[block_at(at, depth), lanes].astype(BF)
            out[i * height + depth : (i + 1) * height, :] = bias[:, lanes].astype(BF)
        for i in range(wo_ref.shape[1] // LANES):
            row = 3 * height + i * strip
            out[row : row + strip, :] = wo_ref[block_at(at, strip), i * LANES : (i + 1) * LANES]


def sum_kernel(*refs):
    refs[-1][...] = add_up([r[...] for r in refs[:-1]]).astype(BF)


def fold_kernel(keep_ref, other_ref, own_ref, *outs):
    total = keep_ref[...].astype(F32) + other_ref[...].astype(F32)
    rows = own_ref.shape[0]
    own_ref[...] = total[:rows].astype(BF)
    for i, out in enumerate(outs):
        out[...] = total[rows + i * rows // 2 : rows + (i + 1) * rows // 2].astype(BF)


def finish_kernel(shard_ref, offs_ref, *refs):
    pieces, (q_ref, k_ref, v_ref, wo_ref, inner_ref, *vecs, inner_all, bias) = refs[:-15], refs[-15:]
    depth = q_ref.shape[0]
    height = depth + EXTRA
    cols = LANES
    total = None
    for r, block in enumerate(Cube.blocks(pieces)):
        block = jnp.concatenate([p[...] for p in block], axis=0)
        lanes = block_at(offs_ref[r], cols)
        for i, out in enumerate((q_ref, k_ref, v_ref)):
            out[:, lanes] = block[i * height : i * height + depth, :].astype(F32)
        tails = [block[i * height + depth : (i + 1) * height, :].astype(F32) for i in range(3)]
        bias[0:8, lanes] = jnp.broadcast_to(tails[0][0:1, :], (8, cols))
        bias[8:16, lanes] = jnp.broadcast_to(tails[2][0:1, :], (8, cols))
        inner_all[:, lanes] = jnp.broadcast_to(tails[2][7:8, :], (8, cols))
        tail = jnp.concatenate(tails, axis=1)
        total = tail if total is None else total + tail
        strip = (block.shape[0] - 3 * height) * LANES // wo_ref.shape[1]
        for i in range(wo_ref.shape[1] // LANES):
            row = 3 * height + i * strip
            wo_ref[block_at(offs_ref[r], strip), i * LANES : (i + 1) * LANES] = block[row : row + strip, :].astype(F32)
    mine = block_at(shard_ref[0], depth)
    vecs[0][...] = bias[0:1, mine]
    vecs[1][...] = bias[8:9, mine]
    for i in range(6):
        vecs[2 + i][...] = total[1 + i : 2 + i, :depth]
    inner_ref[...] = inner_all[0:1, :]


def flip(source, bit):
    return lax.ppermute(source, "ctx", [(i, i ^ bit) for i in range(8)])


def shard_flip(source, bit, shards):
    return lax.ppermute(source, "wsh", [(i, i ^ bit) for i in range(shards)])


class Cube:
    def __init__(self):
        self.count = 8

    def at(self, r):
        return lax.axis_index("ctx") ^ r

    def gather(self, own, work=None, early=(), late=()):
        half = own.shape[0] // 32 * 16
        side, down, core = flip(own, 2), flip(own, 4), flip(own, 1)
        if work is not None:
            first = work([own, core])
        side, down, core = after((side, down, core), *([first] if work is not None else early))
        far_a, far_b = flip(side[:half], 4), flip(down[half:], 2)
        side1, down1 = flip(side, 1), flip(down, 1)
        if work is not None:
            second = work([side, side1, down, down1])
        far_a, far_b = after((far_a, far_b), *([second] if work is not None else late))
        far1_a, far1_b = flip(far_a, 1), flip(far_b, 1)
        pieces = [own, core, side, side1, down, down1, far_a, far_b, far1_a, far1_b]
        if work is None:
            return pieces
        third = work(pieces[6:])
        return pieces, [[*a, *b, *c] for a, b, c in zip(first, second, third)]

    def gather_slab(self, own, beside):
        others = after([flip(own, r) for r in (2, 4, 6)], beside)
        four = jnp.concatenate([own, *others], axis=0)
        return [four, flip(four, 1)]

    slab_order = (0, 2, 4, 6, 1, 3, 5, 7)

    def scatter_whole(self, keep, send):
        rows, width = keep.shape[0] // 4, keep.shape[1]
        own, side_a, side_b, down_a, down_b, far_a, far_b = call(
            fold_kernel, [], [keep, flip(send, 1)],
            [struct((rows, width), BF)] + [struct((rows // 2, width), BF)] * 6, 3, "fold",
        )
        over_side, over_down = flip(far_a, 2), flip(far_b, 4)
        side_a, down_b = flip(side_a, 2), flip(down_b, 4)
        moved = self.fold(side_b, over_down), self.fold(down_a, over_side)
        side_b, down_a = flip(moved[0], 2), flip(moved[1], 4)
        return [own, side_a, down_a, side_b, down_b], 1, 2, moved

    @staticmethod
    def fold(half, other):
        return (half.astype(F32) + other.astype(F32)).astype(BF)

    def places(self, rows):
        own = [self.at(r) * rows for r in range(8)]
        half = rows // 2
        return own[:6] + [own[6], own[6] + half, own[7], own[7] + half]

    @staticmethod
    def blocks(pieces):
        return [(p,) for p in pieces[:6]] + [(pieces[6], pieces[7]), (pieces[8], pieces[9])]

    def scatter(self, pieces):
        own, core, side, side1, down, down1, far_a, far_b, far1_a, far1_b = pieces
        half = own.shape[0] // 2
        far_a = (far_a.astype(F32) + flip(far1_a, 1).astype(F32)).astype(BF)
        over_side = flip(far_a, 2)
        far_b = (far_b.astype(F32) + flip(far1_b, 1).astype(F32)).astype(BF)
        over_down = flip(far_b, 4)
        side = side.astype(F32) + flip(side1, 1).astype(F32)
        down = down.astype(F32) + flip(down1, 1).astype(F32)
        side_a = flip(side[:half].astype(BF), 2)
        down_b = flip(down[half:].astype(BF), 4)
        side_b = (side[half:] + over_down.astype(F32)).astype(BF)
        down_a = (down[:half] + over_side.astype(F32)).astype(BF)
        return [own, flip(core, 1), side_a, flip(down_a, 4), flip(side_b, 2), down_b], 2, 2, (side_b, down_a)

    parts = ((0, 4), (4, 8))

    def exchange(self, blocks, low):
        return [flip(block, low + i) if low + i else block for i, block in enumerate(blocks)]


class Line:
    def __init__(self, count):
        self.count = count

    def at(self, r):
        return jnp.int32(r)

    def gather(self, own, work=None, early=(), late=()):
        pieces = list(lax.all_gather(own, "ctx", axis=0, tiled=False))
        if work is None:
            return pieces
        groups = [work(group) for group in grouped(pieces, 4)]
        return pieces, [[piece for part in parts for piece in part] for parts in zip(*groups)]

    def places(self, rows):
        return [jnp.int32(r * rows) for r in range(self.count)]

    def scatter(self, pieces):
        whole = jnp.concatenate(pieces, axis=0)
        return [lax.psum_scatter(whole, "ctx", scatter_dimension=0, tiled=True)], 1, 0, ()

    @property
    def parts(self):
        return ((0, self.count),)

    def scatter_whole(self, addends):
        return [lax.psum_scatter(addends, "ctx", scatter_dimension=0, tiled=True)], 1, 0, ()

    def exchange(self, blocks, low):
        return list(lax.all_to_all(jnp.stack(blocks), "ctx", 0, 0, tiled=False))


def grouped(items, size):
    return [items[i : i + size] for i in range(0, len(items), size)]


def local(
    tokens, starts, query_weight, key_weight, value_weight, output_weight, inner_weight, outer_weight,
    query_bias, value_bias, output_bias, first_gain, first_shift, inner_bias, outer_bias,
    second_gain, second_shift, cotangent,
):
    count, shards = lax.axis_size("ctx"), lax.axis_size("wsh")
    net = Cube() if count == 8 else Line(count)
    me, shard = lax.axis_index("ctx"), lax.axis_index("wsh")
    x = tokens[0]
    rows, width = x.shape
    length = rows * count
    size = width // HEADS
    heads = max(1, HEADS // count)
    copies = max(1, count // HEADS)
    cols = heads * size
    wide = -(-cols // LANES) * LANES
    depth = width // shards
    units = outer_weight.shape[0] // count
    strip = depth // count
    scale = size**-0.5
    shard_ids = jnp.stack([shard ^ r for r in range(shards)])
    places = jnp.stack(net.places(rows))

    first_col = me // copies * cols

    def own_columns(w):
        return jnp.pad(lax.dynamic_slice_in_dim(w, first_col, cols, 1), ((0, 0), (0, wide - cols)))

    weights, lane = [query_weight, key_weight, value_weight], first_col
    if cols % LANES:
        weights, lane = [own_columns(w) for w in weights], jnp.int32(0)
    vectors = [query_bias, value_bias, output_bias, first_gain, first_shift, outer_bias, second_gain,
               second_shift, inner_bias]
    vectors = [v.reshape(-1, LANES) for v in vectors]
    height = -(-sum(v.shape[0] for v in vectors) * LANES // (24 * wide)) * 8
    (pack,) = call(
        pack_kernel, [lane[None]], [*weights, *vectors], [struct((depth + height, 3 * wide), BF)], 20, "pack", (), None,
    )
    packs = [pack] + [shard_flip(pack, r, shards) for r in range(1, shards)]
    vec, inner_all = call(
        functools.partial(unpack_kernel, shards), [shard_ids], packs,
        [struct((8, width), F32), struct((8 * shards, inner_bias.shape[0]), F32)], 2, "unpack",
    )
    share = units * shards
    times = width // share
    inner_own = [
        lax.dynamic_slice_in_dim(inner_weight, s * units * count + me * units, units, 1) for s in range(shards)
    ]
    inner_own = jnp.concatenate(inner_own, axis=1)
    inner_own = jnp.concatenate([inner_own[i * depth // times : (i + 1) * depth // times] for i in range(times)], axis=1)
    outer_own = lax.dynamic_slice_in_dim(outer_weight, me * units, units, 0)
    forward_pack = jnp.concatenate([outer_own, inner_own], axis=0)
    wo_own = lax.dynamic_slice_in_dim(output_weight, me * strip, strip, 0)
    pieces = net.gather(x, early=[pack], late=[vec, forward_pack, wo_own])
    bias = jnp.pad(lax.dynamic_slice(vec, (0, first_col), (8, cols)), ((0, 0), (0, wide - cols)))
    inner_b = lax.dynamic_slice_in_dim(inner_all[::8], me * units, units, 1).reshape(1, -1)

    qkv_rows = []
    done = 0
    for group in grouped(pieces, 10):
        group_rows = sum(p.shape[0] for p in group)
        sheet = struct((group_rows, wide), BF)
        tail = struct((group_rows, LANES), BF)
        qkv, *made = call(
            functools.partial(project_kernel, len(group), shards, wide, scale),
            [shard_ids, places[done : done + len(group)], starts[0]],
            [*group, *packs, bias],
            [struct((width, 3 * wide), BF), sheet, sheet, sheet, tail, tail],
            4, "project",
        )
        qkv_rows.append(made)
        done += len(group)
    q, k, v, qt, kt = [made[0] if len(made) == 1 else jnp.concatenate(made) for made in zip(*qkv_rows)]

    wo_own = after(wo_own, q)
    wo_parts = [wo_own] + [shard_flip(wo_own, r, shards) for r in range(1, shards)]

    forward_pack = lax.all_gather(after(forward_pack, packs, pieces[6:8]), "wsh", axis=0, tiled=False)

    attended, blocks = [], []
    for low, high in net.parts:
        made = attend(q, qt, k, kt, v, rows, heads, size, low, high)
        attended.append(made)
        blocks += net.exchange([made[0][i * rows : (i + 1) * rows, :cols] for i in range(high - low)], low)
        q, k = (q, k) if high == count else after((q, k), made[0])
    if isinstance(net, Cube):
        ids = jnp.stack([net.at(r) for r in net.slab_order])
        slab = jnp.concatenate([wo_parts[0], *after(wo_parts[1:], attended[0][0])], axis=0)
        slabs = net.gather_slab(slab, attended[1][0])
        (wo,) = call(
            functools.partial(assemble_kernel, shards, strip), [shard_ids, ids], slabs,
            [struct((width, width), BF)], 2, "assemble",
        )
    else:
        wo_slab = jnp.zeros((shards, strip, width), BF)
        for r in range(shards):
            wo_slab = lax.dynamic_update_slice(wo_slab, wo_parts[r][None], (shard ^ r, jnp.int32(0), jnp.int32(0)))
        wo = lax.all_gather(wo_slab, "ctx", axis=0, tiled=False)
        wo = wo.transpose(1, 0, 2, 3).reshape(width, width)
    blocks = blocks[::copies]
    offs = jnp.stack([net.at(r) // copies for r in range(0, count, copies)])
    groups = len(blocks)
    low_full, tall = struct((rows, width), BF), struct((rows, 1), F32)
    sums = struct((8, width), F32)
    hidden_low, normed, root = call(
        functools.partial(first_norm_kernel, groups), [offs], [x, wo, vec, *blocks],
        [low_full, low_full, tall], 5, "first_norm",
    )
    inner, outer = call(
        functools.partial(weights_kernel, units), [], [forward_pack],
        [struct((width, share), BF), struct((share, width), BF)], 2, "weights",
    )

    def forward(group):
        sizes = [p.shape[0] for p in group]
        mids = [struct((s, units * shards), BF) for s in sizes]
        made = call(
            functools.partial(forward_kernel, len(group)), [], [inner, inner_b, outer, *group],
            mids + mids + [struct((s, width), BF) for s in sizes], 1.5 * sum(sizes) / 256, "forward",
        )
        n = len(group)
        return made[:n], made[n : 2 * n], made[2 * n :]

    hidden_all, (acts, slopes, branch) = net.gather(hidden_low, forward)
    parts, n_whole, n_half, _ = net.scatter(branch)
    result, branch_grad, sums_two = call(
        functools.partial(second_norm_kernel, n_whole, n_half), [], [hidden_low, vec, cotangent[0], *parts],
        [low_full, low_full, sums], 4, "second_norm",
    )

    inner_sums, waiting = [], list(slopes)

    def backward(group):
        sizes = [p.shape[0] for p in group]
        n = len(group)
        slope, waiting[:n] = waiting[:n], []
        made = call(
            functools.partial(backward_kernel, n), [], [inner, outer, *group, *slope],
            [struct((s, units * shards), BF) for s in sizes]
            + [struct((s, width), BF) for s in sizes]
            + [struct((1, units * shards), F32)],
            1.5 * sum(sizes) / 256, "backward",
        )
        inner_sums.append(made[-1])
        given = []
        if isinstance(net, Cube) and len(inner_sums) == 1:
            given = call(
                functools.partial(early_product_kernel, n), [], [*acts[:n], *group, *hidden_all[:n], *made[:n]],
                [struct((share, width), F32), struct((width, share), F32)], 4, "early_product",
            )
        return made[:n], made[n:-1], given

    grad_all, (inner_grads, hidden_grads, given) = net.gather(branch_grad, backward)
    parts, n_whole, n_half, moved = net.scatter(hidden_grads)
    skip = 2 if given else 0
    terms = [*acts[skip:], *grad_all[skip:], *hidden_all[skip:], *inner_grads[skip:]]
    height = units + depth * share // width
    forward_wg = pl.pallas_call(
        functools.partial(late_product_kernel, len(acts) - skip, len(given), shards),
        in_specs=[pl.BlockSpec(memory_space=pl.ANY)] * (len(terms) + len(given)),
        out_specs=IN_VMEM,
        out_shape=struct((shards * height, width), BF),
        scratch_shapes=[pltpu.VMEM(t.shape, BF) for t in terms]
        + [pltpu.VMEM((share, width), F32), pltpu.VMEM((width, share), F32)]
        + [pltpu.SemaphoreType.DMA((len(terms) + 2,))],
        compiler_params=params(60 * MIB),
        cost_estimate=micros(12),
        name="late_product",
    )(*after(terms, moved), *given)
    parts = after(parts, forward_wg)
    forward_own = lax.psum_scatter(forward_wg, "wsh", scatter_dimension=0, tiled=True)
    attn_grad, sums_one, *mixed_grads = call(
        functools.partial(first_back_kernel, groups, n_whole, n_half), [offs],
        [branch_grad, normed, root, vec, wo, *parts],
        [low_full, sums] + [struct((rows, cols), BF)] * groups, 5, "first_back",
    )
    if copies > 1:
        mixed_grads = [b for b in mixed_grads for _ in range(copies)]
    exchanged = []
    for low, high in net.parts:
        exchanged += net.exchange(mixed_grads[low:high], low)
    order = [0, 4, 2, 6, 1, 5, 3, 7] if isinstance(net, Cube) else list(range(count))
    halves = 2 if isinstance(net, Cube) else 1
    ids = jnp.stack([net.at(r) for r in order])

    def mixed_product(offs_ref, ids_ref, low_ref, *refs):
        outs, acc = refs[groups:-1], refs[-1]
        for r, block in enumerate(refs[:groups]):
            acc[block_at(offs_ref[r], cols), :] = dot_tn(block[...], low_ref[...])
        per = count // halves
        for i in range(count):
            for s in range(shards):
                row = (i % per * shards + s) * strip
                at = pl.multiple_of(s * depth + ids_ref[i] * strip, strip)
                outs[i // per][row : row + strip, :] = acc[pl.ds(at, strip), :].astype(BF)

    wo_grad = call(
        mixed_product, [offs, ids], [after(attn_grad, exchanged[1]), *blocks],
        [struct((width // halves, width), BF)] * halves, 4, "mixed_product", [pltpu.VMEM((width, width), F32)],
    )
    if isinstance(net, Cube):
        folded = net.fold(wo_grad[0], flip(wo_grad[1], 1))
    else:
        folded = lax.psum_scatter(wo_grad[0], "ctx", scatter_dimension=0, tiled=True)
    prior = None
    for (low, high), (_, o, lse) in zip(net.parts, attended):
        mgs = [jnp.pad(b, ((0, 0), (0, wide - cols))) for b in exchanged[low:high]]
        mgs = after(mgs, folded)
        prior = attend_back(q, qt, k, kt, v, mgs, o, lse, rows, heads, size, scale, low, high, prior)
        if isinstance(net, Cube):
            half = folded.shape[0] // 2
            sent = flip(folded[half:], 2 if low == 0 else 4)
            folded = net.fold(folded[:half], after(sent, prior if high == count else prior[0]))
    triple = after(prior, folded)
    forward_all = lax.all_gather(after(forward_own, triple), "ctx", axis=0, tiled=False)
    inner_sum = add_up(inner_sums).reshape(shards, units)
    last_pack = struct((3 * (depth + EXTRA) + strip * width // LANES, LANES), BF)
    packs = call(
        functools.partial(qkv_product_kernel, len(pieces)), [shard_ids],
        [triple, sums_one, sums_two, inner_sum, folded, *pieces], [last_pack] * shards, 6, "qkv_product",
        [pltpu.VMEM((width, 3 * wide), F32), pltpu.VMEM((EXTRA, 3 * wide), F32)], None,
    )
    order = [0, 2, 4, 6, 1, 3, 5, 7] if isinstance(net, Cube) else list(range(count))
    into = call(
        functools.partial(into_kernel, 1.0 / copies, order), [], [after(triple, packs), qkv],
        [struct((length // halves, width), BF)] * halves, 4, "into",
    )
    parts, n_whole, n_half, moved = net.scatter_whole(*into)
    (input_grad,) = call(
        functools.partial(input_kernel, n_whole, n_half), [], [attn_grad, *parts], [low_full], 2, "input_sum"
    )
    packs = [packs[0]] + [shard_flip(packs[r], r, shards) for r in range(1, shards)]
    (last_own,) = call(sum_kernel, [], after(packs, moved), [last_pack], 2, "last_sum")
    if isinstance(net, Cube):
        outer_out, inner_out = call(
            functools.partial(finish_forward_kernel, units), [], [forward_all],
            [struct((units * count, width), F32), struct((depth, units * count * shards), F32)], 6, "finish_forward",
            (), None,
        )
        last_all = net.gather(last_own, late=[outer_out])
        square = struct((depth, width), F32)
        query_out, key_out, value_out, wo_out, *vecs = call(
            finish_kernel, [shard_ids, offs], last_all,
            [square] * 4 + [struct((1, units * count), F32)] + [struct((1, depth), F32)] * 8, 4, "finish",
            [pltpu.VMEM((8, units * count), F32), pltpu.VMEM((16, width), F32)], None,
        )
        inner_vec, *vecs = [v.reshape(-1) for v in vecs]
    else:
        last_all = jnp.stack(net.gather(last_own)).astype(F32)
        triples = last_all[:, : 3 * (depth + EXTRA)].reshape(count, 3, depth + EXTRA, LANES)
        wo_out = last_all[:, 3 * (depth + EXTRA) :].reshape(count, width // LANES, strip, LANES)
        wo_out = wo_out.transpose(0, 2, 1, 3).reshape(depth, width)
        out3 = triples[::copies, :, :depth, :cols].transpose(1, 2, 0, 3).reshape(3, depth, width)
        query_out, key_out, value_out = out3[0], out3[1], out3[2]
        both = triples[::copies, :, depth, :cols].transpose(1, 0, 2).reshape(3, width)
        both = lax.dynamic_slice_in_dim(both, shard * depth, depth, 1)
        tail = triples[:, :, depth:].transpose(0, 2, 1, 3).reshape(count, EXTRA, 3 * LANES)
        six = jnp.sum(tail[:, 1:7, :depth], axis=0)
        vecs = [both[0], both[2]] + [six[i] for i in range(6)]
        inner_vec = tail[:, 7, 2 * LANES : 2 * LANES + units].reshape(-1)
        forward_all = forward_all.astype(F32)
        outer_out = forward_all[:, :units].reshape(-1, width)
        inner_out = forward_all[:, units:].reshape(count, depth // times, times, shards, units)
        inner_out = inner_out.transpose(2, 1, 3, 0, 4).reshape(depth, -1)
    return (
        result[None], input_grad[None], query_out, key_out, value_out, wo_out, inner_out, outer_out,
        vecs[0], vecs[1], vecs[2], vecs[3], vecs[4], inner_vec, vecs[5], vecs[6], vecs[7],
    )


def solution(mesh):
    sheet, matrix, vector = P("wsh", "ctx", None), P("wsh", None), P("wsh")
    return jax.shard_map(
        local,
        mesh=mesh,
        in_specs=(sheet, matrix) + (matrix,) * 6 + (vector,) * 9 + (sheet,),
        out_specs=(sheet, sheet) + (matrix,) * 6 + (vector,) * 9,
        check_vma=False,
    )
```

```python
import functools
import math

import jax
import jax.numpy as jnp
from jax import lax
from jax.experimental import pallas as pl
from jax.experimental.pallas import tpu as pltpu
from jax.sharding import PartitionSpec as P

HEADS = 16
LANES = 128
VECTORS = 32
EXTRA = 16
BF = jnp.bfloat16
F32 = jnp.float32
MIB = 1024 * 1024
IN_VMEM = pl.BlockSpec(memory_space=pltpu.VMEM)
IN_SMEM = pl.BlockSpec(memory_space=pltpu.SMEM)


def dot(a, b):
    return lax.dot_general(a, b, (((1,), (0,)), ((), ())), preferred_element_type=F32)


def dot_nt(a, b):
    return lax.dot_general(a, b, (((1,), (1,)), ((), ())), preferred_element_type=F32)


def dot_tn(a, b):
    return lax.dot_general(a, b, (((0,), (0,)), ((), ())), preferred_element_type=F32)


def struct(shape, dtype):
    return jax.ShapeDtypeStruct(shape, dtype)


def micros(us):
    return pl.CostEstimate(flops=int(us * 1e9), bytes_accessed=0, transcendentals=0)


def params(limit):
    return pltpu.CompilerParams(vmem_limit_bytes=min(limit, 60 * MIB))


def after(value, *others):
    return lax.optimization_barrier((value, others))[0]


def bytes_of(arrays):
    return sum(math.prod(a.shape) * a.dtype.itemsize for a in arrays)


def call(kernel, scalars, arrays, out_shape, us, name, scratch=(), room=6):
    limit = 60 * MIB if room is None else bytes_of(arrays) + bytes_of(out_shape) + bytes_of(scratch) + room * MIB
    return pl.pallas_call(
        kernel,
        in_specs=[IN_SMEM] * len(scalars) + [IN_VMEM] * len(arrays),
        out_specs=[IN_VMEM] * len(out_shape),
        out_shape=out_shape,
        scratch_shapes=list(scratch),
        compiler_params=params(limit),
        cost_estimate=micros(us),
        name=name,
    )(*scalars, *arrays)


def block_at(index, size):
    return pl.ds(pl.multiple_of(index * size, size), size)


def as_row(column):
    return jnp.broadcast_to(column, (column.shape[0], LANES)).T[0:1, :]


def add_up(parts):
    total = parts[0].astype(F32)
    for part in parts[1:]:
        total = total + part.astype(F32)
    return total


def pack_kernel(at_ref, q_ref, k_ref, v_ref, wo_ref, *refs):
    vectors, out_ref = refs[:-1], refs[-1]
    depth = q_ref.shape[0]
    strip = (out_ref.shape[0] - 3 * depth - VECTORS) * LANES // wo_ref.shape[1]
    lanes = pl.ds(pl.multiple_of(at_ref[0], LANES), LANES)
    for i, ref in enumerate((q_ref, k_ref, v_ref)):
        out_ref[i * depth : (i + 1) * depth, :] = ref[:, lanes]
    rows = jnp.concatenate([ref[...].astype(F32) for ref in vectors], axis=0)
    rows = jnp.concatenate([rows, jnp.zeros((VECTORS - rows.shape[0], LANES), F32)], axis=0)
    out_ref[3 * depth : 3 * depth + VECTORS, :] = rows.astype(BF)
    for i in range(wo_ref.shape[1] // LANES):
        row = 3 * depth + VECTORS + i * strip
        out_ref[row : row + strip, :] = wo_ref[block_at(at_ref[1], strip), i * LANES : (i + 1) * LANES]


def unpack_kernel(count, shard_ref, *refs):
    packs, (vec_ref, inner_ref) = refs[:count], refs[count:]
    depth = vec_ref.shape[1] // count
    vec_ref[...] = jnp.zeros_like(vec_ref)
    inner_ref[...] = jnp.zeros_like(inner_ref)
    per = depth // LANES
    for r, pack in enumerate(packs):
        at = shard_ref[r]
        rows = pack[3 * depth : 3 * depth + VECTORS, :].astype(F32)
        for i in range(8):
            for j in range(per):
                vec_ref[i : i + 1, block_at(at * per + j, LANES)] = rows[i * per + j : i * per + j + 1, :]
        for j in range(inner_ref.shape[1] // LANES):
            row = rows[8 * per + j : 8 * per + j + 1, :]
            inner_ref[block_at(at, 8), j * LANES : (j + 1) * LANES] = jnp.broadcast_to(row, (8, LANES))


def stack_kernel(start, *refs):
    row = 0
    for ref in refs[:-1]:
        rows = ref.shape[0] - start
        refs[-1][row : row + rows, :] = ref[start:, :]
        row += rows


def stack(arrays, start=0):
    rows = sum(a.shape[0] - start for a in arrays)
    out = struct((rows, arrays[0].shape[1]), arrays[0].dtype)
    return call(functools.partial(stack_kernel, start), [], arrays, [out], 1, "stack", (), 1)[0]


def project_kernel(count, shards, cols, scale, shard_ref, place_ref, starts_ref, *refs):
    pieces, packs = refs[:count], refs[count : count + shards]
    bias_ref, w_ref, q_ref, k_ref, v_ref, qt_ref, kt_ref = refs[count + shards :]
    depth = w_ref.shape[0] // shards
    for r, pack in enumerate(packs):
        for i in range(3):
            rows = pack[i * depth : (i + 1) * depth, :]
            w_ref[block_at(shard_ref[r], depth), i * LANES : (i + 1) * LANES] = rows
    weight = w_ref[...]
    documents = starts_ref.shape[0]
    row = 0
    for p, piece in enumerate(pieces):
        rows = piece.shape[0]
        at = slice(row, row + rows)
        raw = dot(piece[...], weight)
        q_ref[at, :] = ((raw[:, :cols] + bias_ref[0:1, :]) * scale).astype(BF)
        k_ref[at, :] = raw[:, cols : 2 * cols].astype(BF)
        v_ref[at, :] = (raw[:, 2 * cols :] + bias_ref[1:2, :]).astype(BF)
        place = place_ref[p] + lax.broadcasted_iota(jnp.int32, (rows, LANES), 0)
        segment = jnp.full((rows, LANES), -1, jnp.int32)
        for j in range(documents):
            segment = segment + (starts_ref[j] <= place).astype(jnp.int32)
        lane = lax.broadcasted_iota(jnp.int32, (rows, LANES), 1)
        same = segment == lane
        qt_ref[at, :] = jnp.where(same | (lane >= documents), 0.0, -1e30).astype(BF)
        kt_ref[at, :] = jnp.where(same, 1.0, 0.0).astype(BF)
        row += rows


def head_lanes(rows, wide, h, size):
    lane = lax.broadcasted_iota(jnp.int32, (rows, wide), 1)
    return (lane >= h * size) & (lane < (h + 1) * size)


def attend_kernel(heads, size, q_ref, qt_ref, k_ref, kt_ref, v_ref, low_ref, o_ref, lse_ref):
    rows, wide = q_ref.shape
    keys = jnp.concatenate([k_ref[...], kt_ref[...]], axis=1)
    query, tail = q_ref[...], qt_ref[...]
    out = jnp.zeros((rows, wide), F32)
    for h in range(heads):
        mine = head_lanes(rows, wide, h, size)
        scores = dot_nt(jnp.concatenate([jnp.where(mine, query, jnp.zeros_like(query)), tail], axis=1), keys)
        top = jnp.max(scores, axis=1, keepdims=True)
        probs = jnp.exp(scores - top)
        total = jnp.sum(probs, axis=1, keepdims=True)
        out = jnp.where(mine, dot(probs.astype(BF), v_ref[...]) / total, out)
        lse_ref[h : h + 1, :] = as_row(top + jnp.log(total))
    o_ref[...] = out
    low_ref[...] = out.astype(BF)


def attend(q, qt, k, kt, v, rows, heads, size, low, high):
    length, wide = q.shape
    part = pl.BlockSpec((rows, wide), lambda i: (i + low, 0))
    whole = pl.BlockSpec((length, wide), lambda i: (0, 0))
    tail = pl.BlockSpec((length, LANES), lambda i: (0, 0))
    out = pl.BlockSpec((rows, wide), lambda i: (i, 0))
    count = (high - low) * rows
    return pl.pallas_call(
        functools.partial(attend_kernel, heads, size),
        grid=(high - low,),
        in_specs=[part, pl.BlockSpec((rows, LANES), lambda i: (i + low, 0)), whole, tail, whole],
        out_specs=[out, out, pl.BlockSpec((8, rows), lambda i: (0, i))],
        out_shape=[struct((count, wide), BF), struct((count, wide), F32), struct((8, count), F32)],
        compiler_params=params(8 * MIB + 20 * rows * length + 8 * bytes_of([q])),
        cost_estimate=micros(9),
        name="attend",
    )(q, qt, k, kt, v)


def attend_back_kernel(heads, size, scale, first, last, count, done, q_ref, qt_ref, k_ref, kt_ref, v_ref, o_ref, lse_ref, *refs):
    mgs, refs = refs[:count], refs[count:]
    prior = ()
    if not first:
        prior, refs = refs[:3], refs[3:]
    if last:
        out_ref, kx, mg_s, dk_acc, dv_acc = refs
    else:
        out_ref, dk_acc, dv_acc, kx, mg_s = refs
    step = pl.program_id(0)
    rows, wide = q_ref.shape

    @pl.when(step == 0)
    def _():
        if first:
            dk_acc[...] = jnp.zeros_like(dk_acc)
            dv_acc[...] = jnp.zeros_like(dv_acc)
        else:
            out_ref[:done, :wide] = prior[0][...]
            dk_acc[...] = prior[1][...]
            dv_acc[...] = prior[2][...]
        kx[...] = k_ref[...].astype(F32).T.astype(BF)

    for i in range(count):

        @pl.when(step == i)
        def _(i=i):
            mg_s[...] = mgs[i][...]

    keys = jnp.concatenate([k_ref[...], kt_ref[...]], axis=1)
    query, tail, mg = q_ref[...], qt_ref[...], mg_s[...]
    spread = mg.astype(F32) * o_ref[...]
    turned = []
    for h in range(heads):
        mine = head_lanes(rows, wide, h, size)
        query_h = jnp.where(mine, query, jnp.zeros_like(query))
        mg_h = jnp.where(mine, mg, jnp.zeros_like(mg))
        row_terms = as_row(jnp.sum(jnp.where(mine, spread, 0.0), axis=1, keepdims=True))
        scores = dot_nt(keys, jnp.concatenate([query_h, tail], axis=1))
        probs = jnp.exp(scores - lse_ref[h : h + 1, :])
        dv_acc[...] += dot(probs.astype(BF), mg_h)
        grads = (probs * (dot_nt(v_ref[...], mg_h) - row_terms)).astype(BF)
        dk_acc[...] += dot(grads, query_h)
        turned.append(dot(kx[h * size : (h + 1) * size, :], grads))
    if heads * size < wide:
        turned.append(jnp.zeros((wide - heads * size, rows), F32))
    at = pl.ds(pl.multiple_of(done + step * rows, rows), rows) if last else block_at(step, rows)
    out_ref[at, :wide] = (jnp.concatenate(turned, axis=0).T * scale).astype(BF)
    if last:

        @pl.when(step == pl.num_programs(0) - 1)
        def _():
            out_ref[:, wide : 2 * wide] = dk_acc[...].astype(BF)
            out_ref[:, 2 * wide :] = dv_acc[...].astype(BF)


def attend_back(q, qt, k, kt, v, mgs, o, lse, rows, heads, size, scale, low, high, prior):
    length, wide = q.shape
    last = high * rows == length
    fixed = lambda i: (0, 0)
    whole = pl.BlockSpec((length, wide), fixed)
    full = struct((length, wide), F32)
    scratch = [pltpu.VMEM((wide, length), BF), pltpu.VMEM((rows, wide), BF)]
    if last:
        out_specs = pl.BlockSpec((length, 3 * wide), fixed)
        out_shape = struct((length, 3 * wide), BF)
        scratch += [pltpu.VMEM((length, wide), F32)] * 2
    else:
        count = (high - low) * rows
        out_specs = [pl.BlockSpec((count, wide), fixed), whole, whole]
        out_shape = [struct((count, wide), BF), full, full]
    return pl.pallas_call(
        functools.partial(
            attend_back_kernel, heads, size, scale, prior is None, last, high - low, low * rows
        ),
        grid=(high - low,),
        in_specs=[
            pl.BlockSpec((rows, wide), lambda i: (i + low, 0)),
            pl.BlockSpec((rows, LANES), lambda i: (i + low, 0)),
            whole,
            pl.BlockSpec((length, LANES), fixed),
            whole,
            pl.BlockSpec((rows, wide), lambda i: (i, 0)),
            pl.BlockSpec((8, rows), lambda i: (0, i)),
        ]
        + [pl.BlockSpec((rows, wide), fixed)] * (high - low)
        + ([] if prior is None else [pl.BlockSpec((low * rows, wide), fixed), whole, whole]),
        out_specs=out_specs,
        out_shape=out_shape,
        scratch_shapes=scratch,
        compiler_params=params(60 * MIB),
        cost_estimate=micros(12),
        name="attend_back",
    )(q, qt, k, kt, v, o, lse, *mgs, *(prior or ()))


def normalize(source):
    mean = jnp.mean(source, axis=-1, keepdims=True)
    centered = source - mean
    root = lax.rsqrt(jnp.mean(centered * centered, axis=-1, keepdims=True) + 1e-05)
    return centered * root, root


def norm_back(normed, root, grad, gain):
    scaled = grad * gain
    mean = jnp.mean(scaled, axis=-1, keepdims=True)
    mix = jnp.mean(scaled * normed, axis=-1, keepdims=True)
    return root * (scaled - mean - normed * mix)


def column_sums(sums_ref, rows):
    sums_ref[...] = jnp.zeros_like(sums_ref)
    for i, row in enumerate(rows):
        sums_ref[i : i + 1, :] = jnp.sum(row, axis=0, keepdims=True)


def collected(refs, whole, halves):
    full = add_up([r[...] for r in refs[:whole]])
    if not halves:
        return full
    upper = add_up([r[...] for r in refs[whole : whole + halves]])
    lower = add_up([r[...] for r in refs[whole + halves : whole + 2 * halves]])
    return full + jnp.concatenate([upper, lower], axis=0)


def first_norm_kernel(count, offs_ref, x_ref, wo_ref, vec_ref, *refs):
    blocks, (low_ref, normed_ref, root_ref) = refs[:count], refs[count:]
    wide = wo_ref.shape[0] // count
    out = x_ref[...].astype(F32) + vec_ref[2:3, :]
    for r, block in enumerate(blocks):
        out = out + dot(block[...], wo_ref[block_at(offs_ref[r], wide), :])
    normed, root = normalize(out)
    low_ref[...] = (normed * vec_ref[3:4, :] + vec_ref[4:5, :]).astype(BF)
    normed_ref[...] = normed.astype(BF)
    root_ref[...] = root


def second_norm_kernel(whole, halves, hidden_ref, vec_ref, cot_ref, *refs):
    parts, (res_ref, low_ref, sums_ref) = refs[:-3], refs[-3:]
    normed, root = normalize(hidden_ref[...].astype(F32) + collected(parts, whole, halves) + vec_ref[5:6, :])
    gain = vec_ref[6:7, :]
    res_ref[...] = (normed * gain + vec_ref[7:8, :]).astype(BF)
    grad = cot_ref[...].astype(F32)
    low = norm_back(normed, root, grad, gain).astype(BF)
    low_ref[...] = low
    column_sums(sums_ref, [low.astype(F32), grad * normed, grad])


def first_back_kernel(count, whole, halves, offs_ref, resid_ref, normed_ref, root_ref, vec_ref, wo_ref, *refs):
    parts = refs[: whole + 2 * halves]
    low_ref, sums_ref, *outs = refs[whole + 2 * halves :]
    wide = wo_ref.shape[0] // count
    grad = resid_ref[...].astype(F32) + collected(parts, whole, halves)
    normed = normed_ref[...].astype(F32)
    low = norm_back(normed, root_ref[...], grad, vec_ref[3:4, :]).astype(BF)
    low_ref[...] = low
    for r in range(count):
        outs[r][...] = dot_nt(low, wo_ref[block_at(offs_ref[r], wide), :]).astype(BF)
    column_sums(sums_ref, [low.astype(F32), grad * normed, grad])


def input_kernel(whole, halves, first_ref, *refs):
    parts, out_ref = refs[:-1], refs[-1]
    out_ref[...] = (first_ref[...].astype(F32) + collected(parts, whole, halves)).astype(BF)


def assemble_kernel(shards, strip, shard_ref, ids_ref, *refs):
    slabs, out_ref = refs[:-1], refs[-1]
    tiles = out_ref.shape[1] // LANES
    per = slabs[0].shape[0] // (shards * tiles * strip)
    depth = out_ref.shape[0] // shards
    for i, slab in enumerate(slabs):
        for b in range(per):
            for r in range(shards):
                row = pl.multiple_of(shard_ref[r] * depth + ids_ref[i * per + b] * strip, strip)
                for t in range(tiles):
                    source = ((b * shards + r) * tiles + t) * strip
                    out_ref[pl.ds(row, strip), t * LANES : (t + 1) * LANES] = slab[source : source + strip, :]


def gelu_pair(source):
    bell = 0.5 * (1.0 + lax.erf(source * (0.5**0.5)))
    slope = bell + source * jnp.exp(-0.5 * source * source) * ((2.0 * jnp.pi) ** -0.5)
    return source * bell, slope


def forward_kernel(count, inner_ref, bias_ref, outer_ref, *refs):
    for p in range(count):
        act, slope = gelu_pair(dot(refs[p][...], inner_ref[...]) + bias_ref[...])
        low = act.astype(BF)
        refs[count + p][...] = low
        refs[2 * count + p][...] = slope.astype(BF)
        refs[3 * count + p][...] = dot(low, outer_ref[...]).astype(BF)


def backward_kernel(count, inner_ref, outer_ref, *refs):
    total = jnp.zeros((1, inner_ref.shape[1]), F32)
    for p in range(count):
        grad = (dot_nt(refs[p][...], outer_ref[...]) * refs[count + p][...].astype(F32)).astype(BF)
        refs[2 * count + p][...] = grad
        refs[3 * count + p][...] = dot_nt(grad, inner_ref[...]).astype(BF)
        total = total + jnp.sum(grad.astype(F32), axis=0, keepdims=True)
    refs[-1][...] = total


def product_kernel(count, given, *refs):
    acts, grads, hidden, inner = [refs[i * count : (i + 1) * count] for i in range(4)]
    prior, outs = refs[4 * count : 4 * count + given], refs[4 * count + given :]
    for i, (left, right, out) in enumerate(((acts, grads, outs[0]), (hidden, inner, outs[1]))):
        total = prior[i][...] if given else None
        for p in range(count):
            term = dot_tn(left[p][...], right[p][...])
            total = term if total is None else total + term
        out[...] = total


def last_product_kernel(count, given, shards, *refs):
    outer_acc, inner_acc = refs[-2:]
    out_ref = refs[-3]
    product_kernel(count, given, *refs[:-3], outer_acc, inner_acc)
    units = outer_acc.shape[0] // shards
    height = out_ref.shape[0] // shards
    depth, share = inner_acc.shape[0] // shards, inner_acc.shape[1]
    rows = height - units
    for s in range(shards):
        out_ref[s * height : s * height + units, :] = outer_acc[s * units : (s + 1) * units, :].astype(BF)
        for i in range(depth // rows):
            out_ref[s * height + units : (s + 1) * height, i * share : (i + 1) * share] = inner_acc[
                s * depth + i * rows : s * depth + (i + 1) * rows, :
            ].astype(BF)


def weights_kernel(units, all_ref, inner_ref, outer_ref):
    shards, height, width = all_ref.shape
    rows = height - units
    share = inner_ref.shape[1]
    for s in range(shards):
        outer_ref[s * units : (s + 1) * units, :] = all_ref[s, :units, :]
        for i in range(width // share):
            row = (s * (width // share) + i) * rows
            inner_ref[row : row + rows, :] = all_ref[s, units:, i * share : (i + 1) * share]


def finish_forward_kernel(units, all_ref, outer_ref, inner_ref):
    count, height, width = all_ref.shape
    rows = height - units
    times = inner_ref.shape[0] // rows
    share = width // times
    stretch = units * count
    for c in range(count):
        outer_ref[c * units : (c + 1) * units, :] = all_ref[c, :units, :].astype(F32)
        for i in range(times):
            for s in range(share // units):
                inner_ref[i * rows : (i + 1) * rows, s * stretch + c * units : s * stretch + (c + 1) * units] = all_ref[
                    c, units:, i * share + s * units : i * share + (s + 1) * units
                ].astype(F32)


def into_kernel(factor, order, triple_ref, w_ref, *outs):
    rows = triple_ref.shape[0] // len(order)
    per = len(order) // len(outs)
    for i, r in enumerate(order):
        term = dot_nt(triple_ref[r * rows : (r + 1) * rows, :], w_ref[...])
        at = i % per * rows
        outs[i // per][at : at + rows, :] = (term if factor == 1.0 else term * factor).astype(BF)


def qkv_product_kernel(count, shard_ref, triple_ref, one_ref, two_ref, inner_ref, wo_ref, *refs):
    pieces, outs, (acc, bias) = refs[:count], refs[count:-2], refs[-2:]
    row = 0
    bias[...] = jnp.zeros_like(bias)
    bias[0:1, :] = jnp.sum(triple_ref[...].astype(F32), axis=0, keepdims=True)
    for p, piece in enumerate(pieces):
        rows = piece.shape[0]
        term = dot_tn(piece[...], triple_ref[row : row + rows, :])
        if p == 0:
            acc[...] = term
        else:
            acc[...] += term
        row += rows
    depth = acc.shape[0] // len(outs)
    units = inner_ref.shape[1]
    strip = wo_ref.shape[0] // len(outs)
    height = depth + EXTRA
    for r, out in enumerate(outs):
        at = shard_ref[r]
        for i in range(3):
            bias[1 + i : 2 + i, :depth] = one_ref[i : i + 1, block_at(at, depth)]
            bias[4 + i : 5 + i, :depth] = two_ref[i : i + 1, block_at(at, depth)]
        bias[7:8, 2 * LANES : 2 * LANES + units] = inner_ref[pl.ds(at, 1), :]
        for i in range(3):
            lanes = slice(i * LANES, (i + 1) * LANES)
            out[i * height : i * height + depth, :] = acc[block_at(at, depth), lanes].astype(BF)
            out[i * height + depth : (i + 1) * height, :] = bias[:, lanes].astype(BF)
        for i in range(wo_ref.shape[1] // LANES):
            row = 3 * height + i * strip
            out[row : row + strip, :] = wo_ref[block_at(at, strip), i * LANES : (i + 1) * LANES]


def sum_kernel(*refs):
    refs[-1][...] = add_up([r[...] for r in refs[:-1]]).astype(BF)


def fold_kernel(keep_ref, other_ref, own_ref, *outs):
    total = keep_ref[...].astype(F32) + other_ref[...].astype(F32)
    rows = own_ref.shape[0]
    own_ref[...] = total[:rows].astype(BF)
    for i, out in enumerate(outs):
        out[...] = total[rows + i * rows // 2 : rows + (i + 1) * rows // 2].astype(BF)


def finish_kernel(shard_ref, offs_ref, *refs):
    pieces, (q_ref, k_ref, v_ref, wo_ref, inner_ref, *vecs, inner_all, bias) = refs[:-15], refs[-15:]
    depth = q_ref.shape[0]
    height = depth + EXTRA
    cols = LANES
    total = None
    for r, block in enumerate(Cube.blocks(pieces)):
        block = jnp.concatenate([p[...] for p in block], axis=0)
        lanes = block_at(offs_ref[r], cols)
        for i, out in enumerate((q_ref, k_ref, v_ref)):
            out[:, lanes] = block[i * height : i * height + depth, :].astype(F32)
        tails = [block[i * height + depth : (i + 1) * height, :].astype(F32) for i in range(3)]
        bias[0:8, lanes] = jnp.broadcast_to(tails[0][0:1, :], (8, cols))
        bias[8:16, lanes] = jnp.broadcast_to(tails[2][0:1, :], (8, cols))
        inner_all[:, lanes] = jnp.broadcast_to(tails[2][7:8, :], (8, cols))
        tail = jnp.concatenate(tails, axis=1)
        total = tail if total is None else total + tail
        strip = (block.shape[0] - 3 * height) * LANES // wo_ref.shape[1]
        for i in range(wo_ref.shape[1] // LANES):
            row = 3 * height + i * strip
            wo_ref[block_at(offs_ref[r], strip), i * LANES : (i + 1) * LANES] = block[row : row + strip, :].astype(F32)
    mine = block_at(shard_ref[0], depth)
    vecs[0][...] = bias[0:1, mine]
    vecs[1][...] = bias[8:9, mine]
    for i in range(6):
        vecs[2 + i][...] = total[1 + i : 2 + i, :depth]
    inner_ref[...] = inner_all[0:1, :]


def flip(source, bit):
    return lax.ppermute(source, "ctx", [(i, i ^ bit) for i in range(8)])


def shard_flip(source, bit, shards):
    return lax.ppermute(source, "wsh", [(i, i ^ bit) for i in range(shards)])


class Cube:
    def __init__(self):
        self.count = 8

    def at(self, r):
        return lax.axis_index("ctx") ^ r

    def gather(self, own, work=None, early=(), late=()):
        half = own.shape[0] // 32 * 16
        side, down = flip(own, 2), flip(own, 4)
        if work is not None:
            core = flip(own, 1)
            first = work([own, core])
        side, down = after((side, down), *([first] if work is not None else early))
        far_a, far_b = flip(side[:half], 4), flip(down[half:], 2)
        if work is None:
            own_, side_, down_ = after((own, side, down), far_a, far_b)
            core, side1, down1 = flip(own_, 1), flip(side_, 1), flip(down_, 1)
            late = late((far_a, far_b)) if callable(late) else late
        else:
            side1, down1 = flip(side, 1), flip(down, 1)
            second = work([side, side1, down, down1])
        far_a, far_b = after((far_a, far_b), *([second] if work is not None else late))
        far1_a, far1_b = flip(far_a, 1), flip(far_b, 1)
        pieces = [own, core, side, side1, down, down1, far_a, far_b, far1_a, far1_b]
        if work is None:
            return pieces
        third = work(pieces[6:])
        return pieces, [[*a, *b, *c] for a, b, c in zip(first, second, third)]

    def gather_slab(self, own, beside):
        others = after([flip(own, r) for r in (2, 4, 6)], beside)
        four = stack([own, *others])
        return [four, flip(four, 1)]

    slab_order = (0, 2, 4, 6, 1, 3, 5, 7)

    def scatter_whole(self, keep, send, first, second):
        rows, width = keep.shape[0] // 4, keep.shape[1]
        own, side_a, side_b, down_a, down_b, far_a, far_b = call(
            fold_kernel, [], [keep, after(flip(send, 1), first)],
            [struct((rows, width), BF)] + [struct((rows // 2, width), BF)] * 6, 3, "fold",
        )
        over_side, over_down = after((flip(far_a, 2), flip(far_b, 4)), second)
        side_a, down_b = flip(side_a, 2), flip(down_b, 4)
        moved = self.fold(side_b, over_down), self.fold(down_a, over_side)
        side_b, down_a = flip(moved[0], 2), flip(moved[1], 4)
        return [own, side_a, down_a, side_b, down_b], 1, 2

    @staticmethod
    def fold(half, other):
        return (half.astype(F32) + other.astype(F32)).astype(BF)

    def places(self, rows):
        own = [self.at(r) * rows for r in range(8)]
        half = rows // 2
        return own[:6] + [own[6], own[6] + half, own[7], own[7] + half]

    @staticmethod
    def blocks(pieces):
        return [(p,) for p in pieces[:6]] + [(pieces[6], pieces[7]), (pieces[8], pieces[9])]

    def scatter(self, pieces):
        own, core, side, side1, down, down1, far_a, far_b, far1_a, far1_b = pieces
        half = own.shape[0] // 2
        far_a = (far_a.astype(F32) + flip(far1_a, 1).astype(F32)).astype(BF)
        over_side = flip(far_a, 2)
        far_b = (far_b.astype(F32) + flip(far1_b, 1).astype(F32)).astype(BF)
        over_down = flip(far_b, 4)
        side = side.astype(F32) + flip(side1, 1).astype(F32)
        down = down.astype(F32) + flip(down1, 1).astype(F32)
        side_a = flip(side[:half].astype(BF), 2)
        down_b = flip(down[half:].astype(BF), 4)
        side_b = (side[half:] + over_down.astype(F32)).astype(BF)
        down_a = (down[:half] + over_side.astype(F32)).astype(BF)
        return [own, flip(core, 1), side_a, flip(down_a, 4), flip(side_b, 2), down_b], 2, 2, (side_b, down_a)

    parts = ((0, 4), (4, 8))

    def exchange(self, blocks, low):
        return [flip(block, low + i) if low + i else block for i, block in enumerate(blocks)]


class Line:
    def __init__(self, count):
        self.count = count

    def at(self, r):
        return jnp.int32(r)

    def gather(self, own, work=None, early=(), late=()):
        pieces = list(lax.all_gather(own, "ctx", axis=0, tiled=False))
        if callable(late):
            late(own)
        if work is None:
            return pieces
        groups = [work(group) for group in grouped(pieces, 4)]
        return pieces, [[piece for part in parts for piece in part] for parts in zip(*groups)]

    def places(self, rows):
        return [jnp.int32(r * rows) for r in range(self.count)]

    def scatter(self, pieces):
        whole = jnp.concatenate(pieces, axis=0)
        return [lax.psum_scatter(whole, "ctx", scatter_dimension=0, tiled=True)], 1, 0, ()

    @property
    def parts(self):
        return ((0, self.count),)

    def scatter_whole(self, addends, first, second):
        return [lax.psum_scatter(addends, "ctx", scatter_dimension=0, tiled=True)], 1, 0

    def exchange(self, blocks, low):
        return list(lax.all_to_all(jnp.stack(blocks), "ctx", 0, 0, tiled=False))


def grouped(items, size):
    return [items[i : i + size] for i in range(0, len(items), size)]


def local(
    tokens, starts, query_weight, key_weight, value_weight, output_weight, inner_weight, outer_weight,
    query_bias, value_bias, output_bias, first_gain, first_shift, inner_bias, outer_bias,
    second_gain, second_shift, cotangent,
):
    count, shards = lax.axis_size("ctx"), lax.axis_size("wsh")
    net = Cube() if count == 8 else Line(count)
    me, shard = lax.axis_index("ctx"), lax.axis_index("wsh")
    x = tokens[0]
    rows, width = x.shape
    length = rows * count
    size = width // HEADS
    heads = max(1, HEADS // count)
    copies = max(1, count // HEADS)
    cols = heads * size
    wide = -(-cols // LANES) * LANES
    depth = width // shards
    units = outer_weight.shape[0] // count
    strip = depth // count
    scale = size**-0.5
    shard_ids = jnp.stack([shard ^ r for r in range(shards)])
    places = jnp.stack(net.places(rows))

    first_col = me // copies * cols

    def own_columns(w):
        return jnp.pad(lax.dynamic_slice_in_dim(w, first_col, cols, 1), ((0, 0), (0, wide - cols)))

    weights, lane = [query_weight, key_weight, value_weight], first_col
    if cols % LANES:
        weights, lane = [own_columns(w) for w in weights], jnp.int32(0)
    wo_own, wo_at = output_weight, me
    if strip % 16:
        wo_own, wo_at = lax.dynamic_slice_in_dim(output_weight, me * strip, strip, 0), jnp.int32(0)
    vectors = [query_bias, value_bias, output_bias, first_gain, first_shift, outer_bias, second_gain,
               second_shift, inner_bias]
    vectors = [v.reshape(-1, LANES) for v in vectors]
    (pack,) = call(
        pack_kernel, [jnp.stack([lane, wo_at])], [*weights, wo_own, *vectors],
        [struct((3 * depth + VECTORS + strip * width // LANES, LANES), BF)], 20, "pack", (), None,
    )
    packs = [pack] + [shard_flip(pack, r, shards) for r in range(1, shards)]
    share = units * shards
    times = width // share
    inner_own = [
        lax.dynamic_slice_in_dim(inner_weight, s * units * count + me * units, units, 1) for s in range(shards)
    ]
    inner_own = jnp.concatenate(inner_own, axis=1)
    inner_own = jnp.concatenate([inner_own[i * depth // times : (i + 1) * depth // times] for i in range(times)], axis=1)
    outer_own = lax.dynamic_slice_in_dim(outer_weight, me * units, units, 0)
    forward_pack = jnp.concatenate([outer_own, inner_own], axis=0)
    unpacked = []

    def unpack(marker):
        made = call(
            functools.partial(unpack_kernel, shards), [shard_ids], after(packs, marker),
            [struct((8, width), F32), struct((8 * shards, inner_bias.shape[0]), F32)], 20, "unpack",
        )
        unpacked.extend(made)
        return [forward_pack]

    pieces = net.gather(x, early=[pack], late=unpack)
    vec, inner_all = unpacked
    bias = jnp.pad(lax.dynamic_slice(vec, (0, first_col), (8, cols)), ((0, 0), (0, wide - cols)))
    inner_b = lax.dynamic_slice_in_dim(inner_all[::8], me * units, units, 1).reshape(1, -1)

    qkv_rows = []
    done = 0
    for group in grouped(pieces, 10):
        group_rows = sum(p.shape[0] for p in group)
        sheet = struct((group_rows, wide), BF)
        tail = struct((group_rows, LANES), BF)
        qkv, *made = call(
            functools.partial(project_kernel, len(group), shards, wide, scale),
            [shard_ids, places[done : done + len(group)], starts[0]],
            [*group, *packs, bias],
            [struct((width, 3 * wide), BF), sheet, sheet, sheet, tail, tail],
            4, "project",
        )
        qkv_rows.append(made)
        done += len(group)
    q, k, v, qt, kt = [made[0] if len(made) == 1 else jnp.concatenate(made) for made in zip(*qkv_rows)]

    forward_pack = lax.all_gather(after(forward_pack, packs, pieces[6:8]), "wsh", axis=0, tiled=False)

    attended, blocks = [], []
    for low, high in net.parts:
        made = attend(q, qt, k, kt, v, rows, heads, size, low, high)
        attended.append(made)
        blocks += net.exchange([made[0][i * rows : (i + 1) * rows, :cols] for i in range(high - low)], low)
        q, k = (q, k) if high == count else after((q, k), made[0])
    if isinstance(net, Cube):
        ids = jnp.stack([net.at(r) for r in net.slab_order])
        slabs = net.gather_slab(stack(packs, 3 * depth + VECTORS), attended[1][0])
        (wo,) = call(
            functools.partial(assemble_kernel, shards, strip), [shard_ids, ids], slabs,
            [struct((width, width), BF)], 2, "assemble",
        )
    else:
        wo_slab = jnp.zeros((shards, strip, width), BF)
        for r in range(shards):
            part = packs[r][3 * depth + VECTORS :].reshape(width // LANES, strip, LANES).transpose(1, 0, 2).reshape(1, strip, width)
            wo_slab = lax.dynamic_update_slice(wo_slab, part, (shard ^ r, jnp.int32(0), jnp.int32(0)))
        wo = lax.all_gather(wo_slab, "ctx", axis=0, tiled=False)
        wo = wo.transpose(1, 0, 2, 3).reshape(width, width)
    blocks = blocks[::copies]
    offs = jnp.stack([net.at(r) // copies for r in range(0, count, copies)])
    groups = len(blocks)
    low_full, tall = struct((rows, width), BF), struct((rows, 1), F32)
    sums = struct((8, width), F32)
    hidden_low, normed, root = call(
        functools.partial(first_norm_kernel, groups), [offs], [x, wo, vec, *blocks],
        [low_full, low_full, tall], 5, "first_norm",
    )
    inner, outer = call(
        functools.partial(weights_kernel, units), [], [forward_pack],
        [struct((width, share), BF), struct((share, width), BF)], 2, "weights",
    )

    def forward(group):
        sizes = [p.shape[0] for p in group]
        mids = [struct((s, units * shards), BF) for s in sizes]
        made = call(
            functools.partial(forward_kernel, len(group)), [], [inner, inner_b, outer, *group],
            mids + mids + [struct((s, width), BF) for s in sizes], 1.5 * sum(sizes) / 256, "forward",
        )
        n = len(group)
        return made[:n], made[n : 2 * n], made[2 * n :]

    hidden_all, (acts, slopes, branch) = net.gather(hidden_low, forward)
    parts, n_whole, n_half, _ = net.scatter(branch)
    result, branch_grad, sums_two = call(
        functools.partial(second_norm_kernel, n_whole, n_half), [], [hidden_low, vec, cotangent[0], *parts],
        [low_full, low_full, sums], 4, "second_norm",
    )

    inner_sums, waiting, products = [], list(slopes), []

    def backward(group):
        sizes = [p.shape[0] for p in group]
        n, at = len(group), len(acts) - len(waiting)
        slope, waiting[:n] = waiting[:n], []
        made = call(
            functools.partial(backward_kernel, n), [], [inner, outer, *group, *slope],
            [struct((s, units * shards), BF) for s in sizes]
            + [struct((s, width), BF) for s in sizes]
            + [struct((1, units * shards), F32)],
            1.5 * sum(sizes) / 256, "backward",
        )
        inner_sums.append(made[-1])
        terms = [*acts[at : at + n], *group, *hidden_all[at : at + n], *made[:n]]
        if at + n < len(acts):
            given = products[-1] if products else []
            products.append(
                pl.pallas_call(
                    functools.partial(product_kernel, n, len(given)),
                    in_specs=[IN_VMEM] * (4 * n + len(given)),
                    out_specs=[IN_VMEM] * 2,
                    out_shape=[struct((share, width), F32), struct((width, share), F32)],
                    input_output_aliases={4 * n + i: i for i in range(len(given))},
                    compiler_params=params(bytes_of(terms) + 2 * 4 * share * width + 8 * MIB),
                    cost_estimate=micros(3),
                    name="product",
                )(*terms, *given)
            )
            return made[:n], made[n:-1], list(products[-1])
        return made[:n], made[n:-1], terms

    grad_all, (inner_grads, hidden_grads, terms) = net.gather(branch_grad, backward)
    n = len(terms[2 * len(products) :]) // 4
    given, terms = products[-1], terms[2 * len(products) :]
    parts, n_whole, n_half, moved = net.scatter(hidden_grads)
    height = units + depth * share // width
    (forward_wg,) = call(
        functools.partial(last_product_kernel, n, len(given), shards), [], [*after(terms, moved), *given],
        [struct((shards * height, width), BF)], 5, "last_product",
        [pltpu.VMEM((share, width), F32), pltpu.VMEM((width, share), F32)],
    )
    parts = after(parts, forward_wg)
    forward_own = lax.psum_scatter(forward_wg, "wsh", scatter_dimension=0, tiled=True)
    attn_grad, sums_one, *mixed_grads = call(
        functools.partial(first_back_kernel, groups, n_whole, n_half), [offs],
        [branch_grad, normed, root, vec, wo, *parts],
        [low_full, sums] + [struct((rows, cols), BF)] * groups, 5, "first_back", (), None,
    )
    if copies > 1:
        mixed_grads = [b for b in mixed_grads for _ in range(copies)]
    exchanged = []
    for low, high in net.parts:
        exchanged += net.exchange(mixed_grads[low:high], low)
    order = [0, 4, 2, 6, 1, 5, 3, 7] if isinstance(net, Cube) else list(range(count))
    halves = 2 if isinstance(net, Cube) else 1
    ids = jnp.stack([net.at(r) for r in order])

    def mixed_product(offs_ref, ids_ref, low_ref, *refs):
        outs, acc = refs[groups:-1], refs[-1]
        for r, block in enumerate(refs[:groups]):
            acc[block_at(offs_ref[r], cols), :] = dot_tn(block[...], low_ref[...])
        per = count // halves
        for i in range(count):
            for s in range(shards):
                row = (i % per * shards + s) * strip
                at = pl.multiple_of(s * depth + ids_ref[i] * strip, strip)
                outs[i // per][row : row + strip, :] = acc[pl.ds(at, strip), :].astype(BF)

    wo_grad = call(
        mixed_product, [offs, ids], [after(attn_grad, exchanged[1]), *blocks],
        [struct((width // halves, width), BF)] * halves, 4, "mixed_product", [pltpu.VMEM((width, width), F32)],
    )
    if isinstance(net, Cube):
        folded = net.fold(wo_grad[0], flip(wo_grad[1], 1))
    else:
        folded = lax.psum_scatter(wo_grad[0], "ctx", scatter_dimension=0, tiled=True)
    prior = None
    for (low, high), (_, o, lse) in zip(net.parts, attended):
        mgs = [jnp.pad(b, ((0, 0), (0, wide - cols))) for b in exchanged[low:high]]
        mgs = after(mgs, folded)
        prior = attend_back(q, qt, k, kt, v, mgs, o, lse, rows, heads, size, scale, low, high, prior)
        if isinstance(net, Cube):
            half = folded.shape[0] // 2
            sent = flip(folded[half:], 2 if low == 0 else 4)
            folded = net.fold(folded[:half], after(sent, prior if high == count else prior[0]))
    triple = after(prior, folded)
    forward_all = lax.all_gather(after(forward_own, triple), "ctx", axis=0, tiled=False)
    inner_sum = add_up(inner_sums).reshape(shards, units)
    last_pack = struct((3 * (depth + EXTRA) + strip * width // LANES, LANES), BF)
    order = [0, 2, 4, 6, 1, 3, 5, 7] if isinstance(net, Cube) else list(range(count))
    into = call(
        functools.partial(into_kernel, 1.0 / copies, order), [], [triple, qkv],
        [struct((length // halves, width), BF)] * halves, 4, "into", (), None,
    )
    packs = call(
        functools.partial(qkv_product_kernel, len(pieces)), [shard_ids],
        [after(triple, into), sums_one, sums_two, inner_sum, folded, *pieces], [last_pack] * shards, 60, "qkv_product",
        [pltpu.VMEM((width, 3 * wide), F32), pltpu.VMEM((EXTRA, 3 * wide), F32)], None,
    )
    packs = [packs[0]] + [shard_flip(packs[r], r, shards) for r in range(1, shards)]
    (last_own,) = call(sum_kernel, [], packs, [last_pack], 2, "last_sum")
    parts, n_whole, n_half = net.scatter_whole(*into, packs[0], last_own)
    (input_grad,) = call(
        functools.partial(input_kernel, n_whole, n_half), [], [attn_grad, *parts], [low_full], 2, "input_sum"
    )
    if isinstance(net, Cube):
        outer_out, inner_out = call(
            functools.partial(finish_forward_kernel, units), [], [forward_all],
            [struct((units * count, width), F32), struct((depth, units * count * shards), F32)], 6, "finish_forward",
            (), None,
        )
        last_all = net.gather(last_own, early=[outer_out])
        square = struct((depth, width), F32)
        query_out, key_out, value_out, wo_out, *vecs = call(
            finish_kernel, [shard_ids, offs], last_all,
            [square] * 4 + [struct((1, units * count), F32)] + [struct((1, depth), F32)] * 8, 4, "finish",
            [pltpu.VMEM((8, units * count), F32), pltpu.VMEM((16, width), F32)], None,
        )
        inner_vec, *vecs = [v.reshape(-1) for v in vecs]
    else:
        last_all = jnp.stack(net.gather(last_own)).astype(F32)
        triples = last_all[:, : 3 * (depth + EXTRA)].reshape(count, 3, depth + EXTRA, LANES)
        wo_out = last_all[:, 3 * (depth + EXTRA) :].reshape(count, width // LANES, strip, LANES)
        wo_out = wo_out.transpose(0, 2, 1, 3).reshape(depth, width)
        out3 = triples[::copies, :, :depth, :cols].transpose(1, 2, 0, 3).reshape(3, depth, width)
        query_out, key_out, value_out = out3[0], out3[1], out3[2]
        both = triples[::copies, :, depth, :cols].transpose(1, 0, 2).reshape(3, width)
        both = lax.dynamic_slice_in_dim(both, shard * depth, depth, 1)
        tail = triples[:, :, depth:].transpose(0, 2, 1, 3).reshape(count, EXTRA, 3 * LANES)
        six = jnp.sum(tail[:, 1:7, :depth], axis=0)
        vecs = [both[0], both[2]] + [six[i] for i in range(6)]
        inner_vec = tail[:, 7, 2 * LANES : 2 * LANES + units].reshape(-1)
        forward_all = forward_all.astype(F32)
        outer_out = forward_all[:, :units].reshape(-1, width)
        inner_out = forward_all[:, units:].reshape(count, depth // times, times, shards, units)
        inner_out = inner_out.transpose(2, 1, 3, 0, 4).reshape(depth, -1)
    return (
        result[None], input_grad[None], query_out, key_out, value_out, wo_out, inner_out, outer_out,
        vecs[0], vecs[1], vecs[2], vecs[3], vecs[4], inner_vec, vecs[5], vecs[6], vecs[7],
    )


def solution(mesh):
    sheet, matrix, vector = P("wsh", "ctx", None), P("wsh", None), P("wsh")
    return jax.shard_map(
        local,
        mesh=mesh,
        in_specs=(sheet, matrix) + (matrix,) * 6 + (vector,) * 9 + (sheet,),
        out_specs=(sheet, sheet) + (matrix,) * 6 + (vector,) * 9,
        check_vma=False,
    )
```

```python
import functools
import math

import jax
import jax.numpy as jnp
from jax import lax
from jax.experimental import pallas as pl
from jax.experimental.pallas import tpu as pltpu
from jax.sharding import PartitionSpec as P

HEADS = 16
LANES = 128
VECTORS = 32
EXTRA = 16
BF = jnp.bfloat16
F32 = jnp.float32
MIB = 1024 * 1024
IN_VMEM = pl.BlockSpec(memory_space=pltpu.VMEM)
IN_SMEM = pl.BlockSpec(memory_space=pltpu.SMEM)


def dot(a, b):
    return lax.dot_general(a, b, (((1,), (0,)), ((), ())), preferred_element_type=F32)


def dot_nt(a, b):
    return lax.dot_general(a, b, (((1,), (1,)), ((), ())), preferred_element_type=F32)


def dot_tn(a, b):
    return lax.dot_general(a, b, (((0,), (0,)), ((), ())), preferred_element_type=F32)


def struct(shape, dtype):
    return jax.ShapeDtypeStruct(shape, dtype)


def micros(us):
    return pl.CostEstimate(flops=int(us * 1e9), bytes_accessed=0, transcendentals=0)


def params(limit):
    return pltpu.CompilerParams(vmem_limit_bytes=min(limit, 60 * MIB))


def after(value, *others):
    return lax.optimization_barrier((value, others))[0]


def bytes_of(arrays):
    return sum(math.prod(a.shape) * a.dtype.itemsize for a in arrays)


def call(kernel, scalars, arrays, out_shape, us, name, scratch=(), room=6):
    limit = 60 * MIB if room is None else bytes_of(arrays) + bytes_of(out_shape) + bytes_of(scratch) + room * MIB
    return pl.pallas_call(
        kernel,
        in_specs=[IN_SMEM] * len(scalars) + [IN_VMEM] * len(arrays),
        out_specs=[IN_VMEM] * len(out_shape),
        out_shape=out_shape,
        scratch_shapes=list(scratch),
        compiler_params=params(limit),
        cost_estimate=micros(us),
        name=name,
    )(*scalars, *arrays)


def block_at(index, size):
    return pl.ds(pl.multiple_of(index * size, size), size)


def as_row(column):
    return jnp.broadcast_to(column, (column.shape[0], LANES)).T[0:1, :]


def add_up(parts):
    total = parts[0].astype(F32)
    for part in parts[1:]:
        total = total + part.astype(F32)
    return total


def pack_kernel(at_ref, q_ref, k_ref, v_ref, wo_ref, *refs):
    vectors, out_ref = refs[:-1], refs[-1]
    depth = q_ref.shape[0]
    strip = (out_ref.shape[0] - 3 * depth - VECTORS) * LANES // wo_ref.shape[1]
    lanes = pl.ds(pl.multiple_of(at_ref[0], LANES), LANES)
    for i, ref in enumerate((q_ref, k_ref, v_ref)):
        out_ref[i * depth : (i + 1) * depth, :] = ref[:, lanes]
    rows = jnp.concatenate([ref[...].astype(F32) for ref in vectors], axis=0)
    rows = jnp.concatenate([rows, jnp.zeros((VECTORS - rows.shape[0], LANES), F32)], axis=0)
    out_ref[3 * depth : 3 * depth + VECTORS, :] = rows.astype(BF)
    for i in range(wo_ref.shape[1] // LANES):
        row = 3 * depth + VECTORS + i * strip
        out_ref[row : row + strip, :] = wo_ref[block_at(at_ref[1], strip), i * LANES : (i + 1) * LANES]


def unpack_kernel(count, shard_ref, *refs):
    packs, (vec_ref, inner_ref) = refs[:count], refs[count:]
    depth = vec_ref.shape[1] // count
    vec_ref[...] = jnp.zeros_like(vec_ref)
    inner_ref[...] = jnp.zeros_like(inner_ref)
    per = depth // LANES
    for r, pack in enumerate(packs):
        at = shard_ref[r]
        rows = pack[3 * depth : 3 * depth + VECTORS, :].astype(F32)
        for i in range(8):
            for j in range(per):
                vec_ref[i : i + 1, block_at(at * per + j, LANES)] = rows[i * per + j : i * per + j + 1, :]
        for j in range(inner_ref.shape[1] // LANES):
            row = rows[8 * per + j : 8 * per + j + 1, :]
            inner_ref[block_at(at, 8), j * LANES : (j + 1) * LANES] = jnp.broadcast_to(row, (8, LANES))


def stack_kernel(start, *refs):
    row = 0
    for ref in refs[:-1]:
        rows = ref.shape[0] - start
        refs[-1][row : row + rows, :] = ref[start:, :]
        row += rows


def stack(arrays, start=0):
    rows = sum(a.shape[0] - start for a in arrays)
    out = struct((rows, arrays[0].shape[1]), arrays[0].dtype)
    return call(functools.partial(stack_kernel, start), [], arrays, [out], 1, "stack", (), 1)[0]


def project_kernel(count, shards, cols, scale, shard_ref, place_ref, starts_ref, *refs):
    pieces, packs = refs[:count], refs[count : count + shards]
    bias_ref, w_ref, q_ref, k_ref, v_ref, qt_ref, kt_ref = refs[count + shards :]
    depth = w_ref.shape[0] // shards
    for r, pack in enumerate(packs):
        for i in range(3):
            rows = pack[i * depth : (i + 1) * depth, :]
            w_ref[block_at(shard_ref[r], depth), i * LANES : (i + 1) * LANES] = rows
    weight = w_ref[...]
    documents = starts_ref.shape[0]
    row = 0
    for p, piece in enumerate(pieces):
        rows = piece.shape[0]
        at = slice(row, row + rows)
        raw = dot(piece[...], weight)
        q_ref[at, :] = ((raw[:, :cols] + bias_ref[0:1, :]) * scale).astype(BF)
        k_ref[at, :] = raw[:, cols : 2 * cols].astype(BF)
        v_ref[at, :] = (raw[:, 2 * cols :] + bias_ref[1:2, :]).astype(BF)
        place = place_ref[p] + lax.broadcasted_iota(jnp.int32, (rows, LANES), 0)
        segment = jnp.full((rows, LANES), -1, jnp.int32)
        for j in range(documents):
            segment = segment + (starts_ref[j] <= place).astype(jnp.int32)
        lane = lax.broadcasted_iota(jnp.int32, (rows, LANES), 1)
        same = segment == lane
        qt_ref[at, :] = jnp.where(same | (lane >= documents), 0.0, -1e30).astype(BF)
        kt_ref[at, :] = jnp.where(same, 1.0, 0.0).astype(BF)
        row += rows


def head_lanes(rows, wide, h, size):
    lane = lax.broadcasted_iota(jnp.int32, (rows, wide), 1)
    return (lane >= h * size) & (lane < (h + 1) * size)


def attend_kernel(heads, size, q_ref, qt_ref, k_ref, kt_ref, v_ref, low_ref, o_ref, lse_ref):
    rows, wide = q_ref.shape
    keys = jnp.concatenate([k_ref[...], kt_ref[...]], axis=1)
    query, tail = q_ref[...], qt_ref[...]
    out = jnp.zeros((rows, wide), F32)
    for h in range(heads):
        mine = head_lanes(rows, wide, h, size)
        scores = dot_nt(jnp.concatenate([jnp.where(mine, query, jnp.zeros_like(query)), tail], axis=1), keys)
        top = jnp.max(scores, axis=1, keepdims=True)
        probs = jnp.exp(scores - top)
        total = jnp.sum(probs, axis=1, keepdims=True)
        out = jnp.where(mine, dot(probs.astype(BF), v_ref[...]) / total, out)
        lse_ref[h : h + 1, :] = as_row(top + jnp.log(total))
    o_ref[...] = out
    low_ref[...] = out.astype(BF)


def attend(q, qt, k, kt, v, rows, heads, size, low, high):
    length, wide = q.shape
    part = pl.BlockSpec((rows, wide), lambda i: (i + low, 0))
    whole = pl.BlockSpec((length, wide), lambda i: (0, 0))
    tail = pl.BlockSpec((length, LANES), lambda i: (0, 0))
    out = pl.BlockSpec((rows, wide), lambda i: (i, 0))
    count = (high - low) * rows
    return pl.pallas_call(
        functools.partial(attend_kernel, heads, size),
        grid=(high - low,),
        in_specs=[part, pl.BlockSpec((rows, LANES), lambda i: (i + low, 0)), whole, tail, whole],
        out_specs=[out, out, pl.BlockSpec((8, rows), lambda i: (0, i))],
        out_shape=[struct((count, wide), BF), struct((count, wide), F32), struct((8, count), F32)],
        compiler_params=params(8 * MIB + 20 * rows * length + 8 * bytes_of([q])),
        cost_estimate=micros(9),
        name="attend",
    )(q, qt, k, kt, v)


def attend_back_kernel(heads, size, scale, first, last, count, done, q_ref, qt_ref, k_ref, kt_ref, v_ref, o_ref, lse_ref, *refs):
    mgs, refs = refs[:count], refs[count:]
    prior = ()
    if not first:
        prior, refs = refs[:3], refs[3:]
    if last:
        out_ref, kx, mg_s, dk_acc, dv_acc = refs
    else:
        out_ref, dk_acc, dv_acc, kx, mg_s = refs
    step = pl.program_id(0)
    rows, wide = q_ref.shape

    @pl.when(step == 0)
    def _():
        if first:
            dk_acc[...] = jnp.zeros_like(dk_acc)
            dv_acc[...] = jnp.zeros_like(dv_acc)
        else:
            out_ref[:done, :wide] = prior[0][...]
            dk_acc[...] = prior[1][...]
            dv_acc[...] = prior[2][...]
        kx[...] = k_ref[...].astype(F32).T.astype(BF)

    each = mg_s.shape[0] // mgs[0].shape[0]
    for i in range(count // each):

        @pl.when(step == i)
        def _(i=i):
            for j in range(each):
                block = mgs[i * each + j]
                mg_s[j * block.shape[0] : (j + 1) * block.shape[0], :] = block[...]

    keys = jnp.concatenate([k_ref[...], kt_ref[...]], axis=1)
    query, tail, mg = q_ref[...], qt_ref[...], mg_s[...]
    spread = mg.astype(F32) * o_ref[...]
    turned = []
    for h in range(heads):
        mine = head_lanes(rows, wide, h, size)
        query_h = jnp.where(mine, query, jnp.zeros_like(query))
        mg_h = jnp.where(mine, mg, jnp.zeros_like(mg))
        row_terms = as_row(jnp.sum(jnp.where(mine, spread, 0.0), axis=1, keepdims=True))
        scores = dot_nt(keys, jnp.concatenate([query_h, tail], axis=1))
        probs = jnp.exp(scores - lse_ref[h : h + 1, :])
        dv_acc[...] += dot(probs.astype(BF), mg_h)
        grads = (probs * (dot_nt(v_ref[...], mg_h) - row_terms)).astype(BF)
        dk_acc[...] += dot(grads, query_h)
        turned.append(dot(kx[h * size : (h + 1) * size, :], grads))
    if heads * size < wide:
        turned.append(jnp.zeros((wide - heads * size, rows), F32))
    at = pl.ds(pl.multiple_of(done + step * rows, rows), rows) if last else block_at(step, rows)
    out_ref[at, :wide] = (jnp.concatenate(turned, axis=0).T * scale).astype(BF)
    if last:

        @pl.when(step == pl.num_programs(0) - 1)
        def _():
            out_ref[:, wide : 2 * wide] = dk_acc[...].astype(BF)
            out_ref[:, 2 * wide :] = dv_acc[...].astype(BF)


def attend_back(q, qt, k, kt, v, mgs, o, lse, rows, heads, size, scale, low, high, prior):
    length, wide = q.shape
    last = high * rows == length
    piece, count = rows, high - low
    if count % 2 == 0 and low % 2 == 0 and 2 * rows * length <= MIB:
        rows, low, high = 2 * rows, low // 2, high // 2
    fixed = lambda i: (0, 0)
    whole = pl.BlockSpec((length, wide), fixed)
    full = struct((length, wide), F32)
    scratch = [pltpu.VMEM((wide, length), BF), pltpu.VMEM((rows, wide), BF)]
    if last:
        out_specs = pl.BlockSpec((length, 3 * wide), fixed)
        out_shape = struct((length, 3 * wide), BF)
        scratch += [pltpu.VMEM((length, wide), F32)] * 2
    else:
        out_specs = [pl.BlockSpec((count * piece, wide), fixed), whole, whole]
        out_shape = [struct((count * piece, wide), BF), full, full]
    return pl.pallas_call(
        functools.partial(
            attend_back_kernel, heads, size, scale, prior is None, last, count, low * rows
        ),
        grid=(high - low,),
        in_specs=[
            pl.BlockSpec((rows, wide), lambda i: (i + low, 0)),
            pl.BlockSpec((rows, LANES), lambda i: (i + low, 0)),
            whole,
            pl.BlockSpec((length, LANES), fixed),
            whole,
            pl.BlockSpec((rows, wide), lambda i: (i, 0)),
            pl.BlockSpec((8, rows), lambda i: (0, i)),
        ]
        + [pl.BlockSpec((piece, wide), fixed)] * count
        + ([] if prior is None else [pl.BlockSpec((low * rows, wide), fixed), whole, whole]),
        out_specs=out_specs,
        out_shape=out_shape,
        scratch_shapes=scratch,
        compiler_params=params(60 * MIB),
        cost_estimate=micros(7),
        name="attend_back",
    )(q, qt, k, kt, v, o, lse, *mgs, *(prior or ()))


def normalize(source):
    mean = jnp.mean(source, axis=-1, keepdims=True)
    centered = source - mean
    root = lax.rsqrt(jnp.mean(centered * centered, axis=-1, keepdims=True) + 1e-05)
    return centered * root, root


def norm_back(normed, root, grad, gain):
    scaled = grad * gain
    mean = jnp.mean(scaled, axis=-1, keepdims=True)
    mix = jnp.mean(scaled * normed, axis=-1, keepdims=True)
    return root * (scaled - mean - normed * mix)


def column_sums(sums_ref, rows):
    sums_ref[...] = jnp.zeros_like(sums_ref)
    for i, row in enumerate(rows):
        sums_ref[i : i + 1, :] = jnp.sum(row, axis=0, keepdims=True)


def collected(refs, whole, halves):
    full = add_up([r[...] for r in refs[:whole]])
    if not halves:
        return full
    upper = add_up([r[...] for r in refs[whole : whole + halves]])
    lower = add_up([r[...] for r in refs[whole + halves : whole + 2 * halves]])
    return full + jnp.concatenate([upper, lower], axis=0)


def first_norm_kernel(count, offs_ref, x_ref, wo_ref, vec_ref, *refs):
    blocks, (low_ref, normed_ref, root_ref) = refs[:count], refs[count:]
    wide = wo_ref.shape[0] // count
    out = x_ref[...].astype(F32) + vec_ref[2:3, :]
    for r, block in enumerate(blocks):
        out = out + dot(block[...], wo_ref[block_at(offs_ref[r], wide), :])
    normed, root = normalize(out)
    low_ref[...] = (normed * vec_ref[3:4, :] + vec_ref[4:5, :]).astype(BF)
    normed_ref[...] = normed.astype(BF)
    root_ref[...] = root


def second_norm_kernel(whole, halves, hidden_ref, vec_ref, cot_ref, *refs):
    parts, (res_ref, low_ref, sums_ref) = refs[:-3], refs[-3:]
    normed, root = normalize(hidden_ref[...].astype(F32) + collected(parts, whole, halves) + vec_ref[5:6, :])
    gain = vec_ref[6:7, :]
    res_ref[...] = (normed * gain + vec_ref[7:8, :]).astype(BF)
    grad = cot_ref[...].astype(F32)
    low = norm_back(normed, root, grad, gain).astype(BF)
    low_ref[...] = low
    column_sums(sums_ref, [low.astype(F32), grad * normed, grad])


def first_back_kernel(count, whole, halves, offs_ref, resid_ref, normed_ref, root_ref, vec_ref, wo_ref, *refs):
    parts = refs[: whole + 2 * halves]
    low_ref, sums_ref, *outs = refs[whole + 2 * halves :]
    wide = wo_ref.shape[0] // count
    grad = resid_ref[...].astype(F32) + collected(parts, whole, halves)
    normed = normed_ref[...].astype(F32)
    low = norm_back(normed, root_ref[...], grad, vec_ref[3:4, :]).astype(BF)
    low_ref[...] = low
    for r in range(count):
        outs[r][...] = dot_nt(low, wo_ref[block_at(offs_ref[r], wide), :]).astype(BF)
    column_sums(sums_ref, [low.astype(F32), grad * normed, grad])


def input_kernel(whole, halves, first_ref, *refs):
    parts, out_ref = refs[:-1], refs[-1]
    out_ref[...] = (first_ref[...].astype(F32) + collected(parts, whole, halves)).astype(BF)


def assemble_kernel(shards, strip, shard_ref, ids_ref, *refs):
    slabs, out_ref = refs[:-1], refs[-1]
    tiles = out_ref.shape[1] // LANES
    per = slabs[0].shape[0] // (shards * tiles * strip)
    depth = out_ref.shape[0] // shards
    for i, slab in enumerate(slabs):
        for b in range(per):
            for r in range(shards):
                row = pl.multiple_of(shard_ref[r] * depth + ids_ref[i * per + b] * strip, strip)
                for t in range(tiles):
                    source = ((b * shards + r) * tiles + t) * strip
                    out_ref[pl.ds(row, strip), t * LANES : (t + 1) * LANES] = slab[source : source + strip, :]


def gelu_pair(source):
    bell = 0.5 * (1.0 + lax.erf(source * (0.5**0.5)))
    slope = bell + source * jnp.exp(-0.5 * source * source) * ((2.0 * jnp.pi) ** -0.5)
    return source * bell, slope


def forward_kernel(count, inner_ref, bias_ref, outer_ref, *refs):
    for p in range(count):
        act, slope = gelu_pair(dot(refs[p][...], inner_ref[...]) + bias_ref[...])
        low = act.astype(BF)
        refs[count + p][...] = low
        refs[2 * count + p][...] = slope.astype(BF)
        refs[3 * count + p][...] = dot(low, outer_ref[...]).astype(BF)


def backward_kernel(count, inner_ref, outer_ref, *refs):
    total = jnp.zeros((1, inner_ref.shape[1]), F32)
    for p in range(count):
        grad = (dot_nt(refs[p][...], outer_ref[...]) * refs[count + p][...].astype(F32)).astype(BF)
        refs[2 * count + p][...] = grad
        refs[3 * count + p][...] = dot_nt(grad, inner_ref[...]).astype(BF)
        total = total + jnp.sum(grad.astype(F32), axis=0, keepdims=True)
    refs[-1][...] = total


def product_kernel(count, given, *refs):
    acts, grads, hidden, inner = [refs[i * count : (i + 1) * count] for i in range(4)]
    prior, outs = refs[4 * count : 4 * count + given], refs[4 * count + given :]
    for i, (left, right, out) in enumerate(((acts, grads, outs[0]), (hidden, inner, outs[1]))):
        total = prior[i][...] if given else None
        for p in range(count):
            term = dot_tn(left[p][...], right[p][...])
            total = term if total is None else total + term
        out[...] = total


def last_product_kernel(count, given, shards, *refs):
    outer_acc, inner_acc = refs[-2:]
    out_ref = refs[-3]
    product_kernel(count, given, *refs[:-3], outer_acc, inner_acc)
    units = outer_acc.shape[0] // shards
    height = out_ref.shape[0] // shards
    depth, share = inner_acc.shape[0] // shards, inner_acc.shape[1]
    rows = height - units
    for s in range(shards):
        out_ref[s * height : s * height + units, :] = outer_acc[s * units : (s + 1) * units, :].astype(BF)
        for i in range(depth // rows):
            out_ref[s * height + units : (s + 1) * height, i * share : (i + 1) * share] = inner_acc[
                s * depth + i * rows : s * depth + (i + 1) * rows, :
            ].astype(BF)


def weights_kernel(units, all_ref, inner_ref, outer_ref):
    shards, height, width = all_ref.shape
    rows = height - units
    share = inner_ref.shape[1]
    for s in range(shards):
        outer_ref[s * units : (s + 1) * units, :] = all_ref[s, :units, :]
        for i in range(width // share):
            row = (s * (width // share) + i) * rows
            inner_ref[row : row + rows, :] = all_ref[s, units:, i * share : (i + 1) * share]


def finish_forward_kernel(units, all_ref, outer_ref, inner_ref):
    count, height, width = all_ref.shape
    rows = height - units
    times = inner_ref.shape[0] // rows
    share = width // times
    stretch = units * count
    for c in range(count):
        outer_ref[c * units : (c + 1) * units, :] = all_ref[c, :units, :].astype(F32)
        for i in range(times):
            for s in range(share // units):
                inner_ref[i * rows : (i + 1) * rows, s * stretch + c * units : s * stretch + (c + 1) * units] = all_ref[
                    c, units:, i * share + s * units : i * share + (s + 1) * units
                ].astype(F32)


def into_kernel(factor, triple_ref, w_ref, *outs):
    rows = outs[0].shape[0]
    for i, out in enumerate(outs):
        term = dot_nt(triple_ref[i * rows : (i + 1) * rows, :], w_ref[...])
        out[...] = (term if factor == 1.0 else term * factor).astype(BF)


def input_terms(triple, w, rows, outs, factor):
    length, (width, wide) = triple.shape[0], w.shape
    steps = length // (rows * outs)
    return pl.pallas_call(
        functools.partial(into_kernel, factor),
        grid=(steps,),
        in_specs=[pl.BlockSpec((rows * outs, wide), lambda i: (i, 0)), pl.BlockSpec((width, wide), lambda i: (0, 0))],
        out_specs=[pl.BlockSpec((rows, width), lambda i: (i, 0))] * outs,
        out_shape=[struct((steps * rows, width), BF)] * outs,
        compiler_params=params(60 * MIB),
        cost_estimate=micros(4),
        name="into",
    )(triple, w)


def qkv_product_kernel(count, shards, shard_ref, triple_ref, one_ref, two_ref, inner_ref, wo_ref, *refs):
    sources, outs, buffers = refs[:count], refs[count : count + shards], refs[count + shards : 2 * count + shards]
    acc, bias, sems = refs[2 * count + shards :]
    copies = [pltpu.make_async_copy(a, b, sems.at[i]) for i, (a, b) in enumerate(zip(sources, buffers))]
    for copy in copies:
        copy.start()
    row = 0
    bias[...] = jnp.zeros_like(bias)
    bias[0:1, :] = jnp.sum(triple_ref[...].astype(F32), axis=0, keepdims=True)
    for p, piece in enumerate(buffers):
        copies[p].wait()
        rows = piece.shape[0]
        term = dot_tn(triple_ref[row : row + rows, :], piece[...])
        if p == 0:
            acc[...] = term
        else:
            acc[...] += term
        row += rows
    depth = acc.shape[1] // len(outs)
    units = inner_ref.shape[1]
    strip = wo_ref.shape[0] // len(outs)
    height = depth + EXTRA
    for r, out in enumerate(outs):
        at = shard_ref[r]
        for i in range(3):
            bias[1 + i : 2 + i, :depth] = one_ref[i : i + 1, block_at(at, depth)]
            bias[4 + i : 5 + i, :depth] = two_ref[i : i + 1, block_at(at, depth)]
        bias[7:8, 2 * LANES : 2 * LANES + units] = inner_ref[pl.ds(at, 1), :]
        for i in range(3):
            lanes = slice(i * LANES, (i + 1) * LANES)
            out[i * height : i * height + depth, :] = acc[lanes, block_at(at, depth)].T.astype(BF)
            out[i * height + depth : (i + 1) * height, :] = bias[:, lanes].astype(BF)
        for i in range(wo_ref.shape[1] // LANES):
            row = 3 * height + i * strip
            out[row : row + strip, :] = wo_ref[block_at(at, strip), i * LANES : (i + 1) * LANES]


def sum_kernel(*refs):
    refs[-1][...] = add_up([r[...] for r in refs[:-1]]).astype(BF)


def fold_kernel(keep_ref, other_ref, own_ref, *outs):
    total = keep_ref[...].astype(F32) + other_ref[...].astype(F32)
    rows = own_ref.shape[0]
    own_ref[...] = total[:rows].astype(BF)
    for i, out in enumerate(outs):
        out[...] = total[rows + i * rows // 2 : rows + (i + 1) * rows // 2].astype(BF)


def finish_kernel(shard_ref, offs_ref, *refs):
    pieces, (q_ref, k_ref, v_ref, wo_ref, inner_ref, *vecs, inner_all, bias) = refs[:-15], refs[-15:]
    depth = q_ref.shape[0]
    height = depth + EXTRA
    cols = LANES
    total = None
    for r, block in enumerate(Cube.blocks(pieces)):
        block = jnp.concatenate([p[...] for p in block], axis=0)
        lanes = block_at(offs_ref[r], cols)
        for i, out in enumerate((q_ref, k_ref, v_ref)):
            out[:, lanes] = block[i * height : i * height + depth, :].astype(F32)
        tails = [block[i * height + depth : (i + 1) * height, :].astype(F32) for i in range(3)]
        bias[0:8, lanes] = jnp.broadcast_to(tails[0][0:1, :], (8, cols))
        bias[8:16, lanes] = jnp.broadcast_to(tails[2][0:1, :], (8, cols))
        inner_all[:, lanes] = jnp.broadcast_to(tails[2][7:8, :], (8, cols))
        tail = jnp.concatenate(tails, axis=1)
        total = tail if total is None else total + tail
        strip = (block.shape[0] - 3 * height) * LANES // wo_ref.shape[1]
        for i in range(wo_ref.shape[1] // LANES):
            row = 3 * height + i * strip
            wo_ref[block_at(offs_ref[r], strip), i * LANES : (i + 1) * LANES] = block[row : row + strip, :].astype(F32)
    mine = block_at(shard_ref[0], depth)
    vecs[0][...] = bias[0:1, mine]
    vecs[1][...] = bias[8:9, mine]
    for i in range(6):
        vecs[2 + i][...] = total[1 + i : 2 + i, :depth]
    inner_ref[...] = inner_all[0:1, :]


def flip(source, bit):
    return lax.ppermute(source, "ctx", [(i, i ^ bit) for i in range(8)])


def shard_flip(source, bit, shards):
    return lax.ppermute(source, "wsh", [(i, i ^ bit) for i in range(shards)])


class Cube:
    def __init__(self):
        self.count = 8

    def at(self, r):
        return lax.axis_index("ctx") ^ r

    def gather(self, own, work=None, early=(), late=()):
        half = own.shape[0] // 32 * 16
        side, down = flip(own, 2), flip(own, 4)
        if work is not None:
            core = flip(own, 1)
            first = work([own, core])
        side, down = after((side, down), *([first] if work is not None else early))
        far_a, far_b = flip(side[:half], 4), flip(down[half:], 2)
        if work is None:
            own_, side_, down_ = after((own, side, down), far_a, far_b)
            core, side1, down1 = flip(own_, 1), flip(side_, 1), flip(down_, 1)
            late = late((far_a, far_b)) if callable(late) else late
        else:
            side1, down1 = flip(side, 1), flip(down, 1)
            second = work([side, side1, down, down1])
        far_a, far_b = after((far_a, far_b), *([second] if work is not None else late))
        far1_a, far1_b = flip(far_a, 1), flip(far_b, 1)
        pieces = [own, core, side, side1, down, down1, far_a, far_b, far1_a, far1_b]
        if work is None:
            return pieces
        third = work(pieces[6:])
        return pieces, [[*a, *b, *c] for a, b, c in zip(first, second, third)]

    def gather_slab(self, own, beside):
        others = after([flip(own, r) for r in (2, 4, 6)], beside)
        four = stack([own, *others])
        return [four, flip(four, 1)]

    slab_order = (0, 2, 4, 6, 1, 3, 5, 7)

    def scatter_whole(self, keep, send, first, second):
        rows, width = keep.shape[0] // 4, keep.shape[1]
        own, side_a, side_b, down_a, down_b, far_a, far_b = call(
            fold_kernel, [], [keep, after(flip(send, 1), first)],
            [struct((rows, width), BF)] + [struct((rows // 2, width), BF)] * 6, 3, "fold",
        )
        over_side, over_down = after((flip(far_a, 2), flip(far_b, 4)), second)
        side_a, down_b = flip(side_a, 2), flip(down_b, 4)
        moved = self.fold(side_b, over_down), self.fold(down_a, over_side)
        side_b, down_a = flip(moved[0], 2), flip(moved[1], 4)
        return [own, side_a, down_a, side_b, down_b], 1, 2

    @staticmethod
    def fold(half, other):
        return (half.astype(F32) + other.astype(F32)).astype(BF)

    def places(self, rows):
        own = [self.at(r) * rows for r in range(8)]
        half = rows // 2
        return own[:6] + [own[6], own[6] + half, own[7], own[7] + half]

    @staticmethod
    def blocks(pieces):
        return [(p,) for p in pieces[:6]] + [(pieces[6], pieces[7]), (pieces[8], pieces[9])]

    def scatter(self, pieces):
        own, core, side, side1, down, down1, far_a, far_b, far1_a, far1_b = pieces
        half = own.shape[0] // 2
        far_a = (far_a.astype(F32) + flip(far1_a, 1).astype(F32)).astype(BF)
        over_side = flip(far_a, 2)
        far_b = (far_b.astype(F32) + flip(far1_b, 1).astype(F32)).astype(BF)
        over_down = flip(far_b, 4)
        side = side.astype(F32) + flip(side1, 1).astype(F32)
        down = down.astype(F32) + flip(down1, 1).astype(F32)
        side_a = flip(side[:half].astype(BF), 2)
        down_b = flip(down[half:].astype(BF), 4)
        side_b = (side[half:] + over_down.astype(F32)).astype(BF)
        down_a = (down[:half] + over_side.astype(F32)).astype(BF)
        return [own, flip(core, 1), side_a, flip(down_a, 4), flip(side_b, 2), down_b], 2, 2, (side_b, down_a)

    parts = ((0, 4), (4, 8))

    def exchange(self, blocks, low):
        return [flip(block, low + i) if low + i else block for i, block in enumerate(blocks)]


class Line:
    def __init__(self, count):
        self.count = count

    def at(self, r):
        return jnp.int32(r)

    def gather(self, own, work=None, early=(), late=()):
        pieces = list(lax.all_gather(own, "ctx", axis=0, tiled=False))
        if callable(late):
            late(own)
        if work is None:
            return pieces
        groups = [work(group) for group in grouped(pieces, 4)]
        return pieces, [[piece for part in parts for piece in part] for parts in zip(*groups)]

    def places(self, rows):
        return [jnp.int32(r * rows) for r in range(self.count)]

    def scatter(self, pieces):
        whole = jnp.concatenate(pieces, axis=0)
        return [lax.psum_scatter(whole, "ctx", scatter_dimension=0, tiled=True)], 1, 0, ()

    @property
    def parts(self):
        return ((0, self.count),)

    def scatter_whole(self, addends, first, second):
        return [lax.psum_scatter(addends, "ctx", scatter_dimension=0, tiled=True)], 1, 0

    def exchange(self, blocks, low):
        return list(lax.all_to_all(jnp.stack(blocks), "ctx", 0, 0, tiled=False))


def grouped(items, size):
    return [items[i : i + size] for i in range(0, len(items), size)]


def local(
    tokens, starts, query_weight, key_weight, value_weight, output_weight, inner_weight, outer_weight,
    query_bias, value_bias, output_bias, first_gain, first_shift, inner_bias, outer_bias,
    second_gain, second_shift, cotangent,
):
    count, shards = lax.axis_size("ctx"), lax.axis_size("wsh")
    net = Cube() if count == 8 else Line(count)
    me, shard = lax.axis_index("ctx"), lax.axis_index("wsh")
    x = tokens[0]
    rows, width = x.shape
    length = rows * count
    size = width // HEADS
    heads = max(1, HEADS // count)
    copies = max(1, count // HEADS)
    cols = heads * size
    wide = -(-cols // LANES) * LANES
    depth = width // shards
    units = outer_weight.shape[0] // count
    strip = depth // count
    scale = size**-0.5
    shard_ids = jnp.stack([shard ^ r for r in range(shards)])
    places = jnp.stack(net.places(rows))

    first_col = me // copies * cols

    def own_columns(w):
        return jnp.pad(lax.dynamic_slice_in_dim(w, first_col, cols, 1), ((0, 0), (0, wide - cols)))

    weights, lane = [query_weight, key_weight, value_weight], first_col
    if cols % LANES:
        weights, lane = [own_columns(w) for w in weights], jnp.int32(0)
    wo_own, wo_at = output_weight, me
    if strip % 16:
        wo_own, wo_at = lax.dynamic_slice_in_dim(output_weight, me * strip, strip, 0), jnp.int32(0)
    vectors = [query_bias, value_bias, output_bias, first_gain, first_shift, outer_bias, second_gain,
               second_shift, inner_bias]
    vectors = [v.reshape(-1, LANES) for v in vectors]
    (pack,) = call(
        pack_kernel, [jnp.stack([lane, wo_at])], [*weights, wo_own, *vectors],
        [struct((3 * depth + VECTORS + strip * width // LANES, LANES), BF)], 20, "pack", (), None,
    )
    packs = [pack] + [shard_flip(pack, r, shards) for r in range(1, shards)]
    share = units * shards
    times = width // share
    inner_own = [
        lax.dynamic_slice_in_dim(inner_weight, s * units * count + me * units, units, 1) for s in range(shards)
    ]
    inner_own = jnp.concatenate(inner_own, axis=1)
    inner_own = jnp.concatenate([inner_own[i * depth // times : (i + 1) * depth // times] for i in range(times)], axis=1)
    outer_own = lax.dynamic_slice_in_dim(outer_weight, me * units, units, 0)
    forward_pack = jnp.concatenate([outer_own, inner_own], axis=0)
    unpacked = []

    def unpack(marker):
        made = call(
            functools.partial(unpack_kernel, shards), [shard_ids], after(packs, marker),
            [struct((8, width), F32), struct((8 * shards, inner_bias.shape[0]), F32)], 20, "unpack",
        )
        unpacked.extend(made)
        return [forward_pack]

    pieces = net.gather(x, early=[pack], late=unpack)
    vec, inner_all = unpacked
    bias = jnp.pad(lax.dynamic_slice(vec, (0, first_col), (8, cols)), ((0, 0), (0, wide - cols)))
    inner_b = lax.dynamic_slice_in_dim(inner_all[::8], me * units, units, 1).reshape(1, -1)

    qkv_rows = []
    done = 0
    for group in grouped(pieces, 10):
        group_rows = sum(p.shape[0] for p in group)
        sheet = struct((group_rows, wide), BF)
        tail = struct((group_rows, LANES), BF)
        qkv, *made = call(
            functools.partial(project_kernel, len(group), shards, wide, scale),
            [shard_ids, places[done : done + len(group)], starts[0]],
            [*group, *packs, bias],
            [struct((width, 3 * wide), BF), sheet, sheet, sheet, tail, tail],
            4, "project",
        )
        qkv_rows.append(made)
        done += len(group)
    q, k, v, qt, kt = [made[0] if len(made) == 1 else jnp.concatenate(made) for made in zip(*qkv_rows)]

    forward_pack = lax.all_gather(after(forward_pack, packs, pieces[6:8]), "wsh", axis=0, tiled=False)

    attended, blocks = [], []
    for low, high in net.parts:
        made = attend(q, qt, k, kt, v, rows, heads, size, low, high)
        attended.append(made)
        mixed = [made[0][i * rows : (i + 1) * rows, :cols] for i in range(high - low)]
        if blocks:
            mixed, *tied = after((mixed, *blocks, slabs[1]), made[0])
            blocks, slabs[1] = tied[:-1], tied[-1]
        blocks += net.exchange(mixed, low)
        if high < count:
            slabs = net.gather_slab(stack(packs, 3 * depth + VECTORS), made[0])
            q, k = after((q, k), slabs[0])
    if isinstance(net, Cube):
        ids = jnp.stack([net.at(r) for r in net.slab_order])
        (wo,) = call(
            functools.partial(assemble_kernel, shards, strip), [shard_ids, ids], slabs,
            [struct((width, width), BF)], 2, "assemble",
        )
    else:
        wo_slab = jnp.zeros((shards, strip, width), BF)
        for r in range(shards):
            part = packs[r][3 * depth + VECTORS :].reshape(width // LANES, strip, LANES).transpose(1, 0, 2).reshape(1, strip, width)
            wo_slab = lax.dynamic_update_slice(wo_slab, part, (shard ^ r, jnp.int32(0), jnp.int32(0)))
        wo = lax.all_gather(wo_slab, "ctx", axis=0, tiled=False)
        wo = wo.transpose(1, 0, 2, 3).reshape(width, width)
    blocks = blocks[::copies]
    offs = jnp.stack([net.at(r) // copies for r in range(0, count, copies)])
    groups = len(blocks)
    low_full, tall = struct((rows, width), BF), struct((rows, 1), F32)
    sums = struct((8, width), F32)
    hidden_low, normed, root = call(
        functools.partial(first_norm_kernel, groups), [offs], [x, wo, vec, *blocks],
        [low_full, low_full, tall], 5, "first_norm",
    )
    inner, outer = call(
        functools.partial(weights_kernel, units), [], [forward_pack],
        [struct((width, share), BF), struct((share, width), BF)], 2, "weights",
    )

    def forward(group):
        sizes = [p.shape[0] for p in group]
        mids = [struct((s, units * shards), BF) for s in sizes]
        made = call(
            functools.partial(forward_kernel, len(group)), [], [inner, inner_b, outer, *group],
            mids + mids + [struct((s, width), BF) for s in sizes], 1.5 * sum(sizes) / 256, "forward",
        )
        n = len(group)
        return made[:n], made[n : 2 * n], made[2 * n :]

    hidden_all, (acts, slopes, branch) = net.gather(hidden_low, forward)
    parts, n_whole, n_half, _ = net.scatter(branch)
    result, branch_grad, sums_two = call(
        functools.partial(second_norm_kernel, n_whole, n_half), [], [hidden_low, vec, cotangent[0], *parts],
        [low_full, low_full, sums], 4, "second_norm",
    )

    inner_sums, waiting, products = [], list(slopes), []

    def backward(group):
        sizes = [p.shape[0] for p in group]
        n, at = len(group), len(acts) - len(waiting)
        slope, waiting[:n] = waiting[:n], []
        made = call(
            functools.partial(backward_kernel, n), [], [inner, outer, *group, *slope],
            [struct((s, units * shards), BF) for s in sizes]
            + [struct((s, width), BF) for s in sizes]
            + [struct((1, units * shards), F32)],
            1.5 * sum(sizes) / 256, "backward",
        )
        inner_sums.append(made[-1])
        terms = [*acts[at : at + n], *group, *hidden_all[at : at + n], *made[:n]]
        if at + n < len(acts):
            given = products[-1] if products else []
            products.append(
                pl.pallas_call(
                    functools.partial(product_kernel, n, len(given)),
                    in_specs=[IN_VMEM] * (4 * n + len(given)),
                    out_specs=[IN_VMEM] * 2,
                    out_shape=[struct((share, width), F32), struct((width, share), F32)],
                    input_output_aliases={4 * n + i: i for i in range(len(given))},
                    compiler_params=params(bytes_of(terms) + 2 * 4 * share * width + 8 * MIB),
                    cost_estimate=micros(3),
                    name="product",
                )(*terms, *given)
            )
            return made[:n], made[n:-1], list(products[-1])
        return made[:n], made[n:-1], terms

    grad_all, (inner_grads, hidden_grads, terms) = net.gather(branch_grad, backward)
    n = len(terms[2 * len(products) :]) // 4
    given, terms = products[-1], terms[2 * len(products) :]
    parts, n_whole, n_half, moved = net.scatter(hidden_grads)
    height = units + depth * share // width
    (forward_wg,) = call(
        functools.partial(last_product_kernel, n, len(given), shards), [], [*after(terms, moved), *given],
        [struct((shards * height, width), BF)], 5, "last_product",
        [pltpu.VMEM((share, width), F32), pltpu.VMEM((width, share), F32)],
    )
    parts = after(parts, forward_wg)
    forward_own = lax.psum_scatter(forward_wg, "wsh", scatter_dimension=0, tiled=True)
    attn_grad, sums_one, *mixed_grads = call(
        functools.partial(first_back_kernel, groups, n_whole, n_half), [offs],
        [branch_grad, normed, root, vec, wo, *parts],
        [low_full, sums] + [struct((rows, cols), BF)] * groups, 5, "first_back", (), None,
    )
    if copies > 1:
        mixed_grads = [b for b in mixed_grads for _ in range(copies)]
    exchanged = []
    for low, high in net.parts:
        exchanged += net.exchange(mixed_grads[low:high], low)
    order = [0, 4, 2, 6, 1, 5, 3, 7] if isinstance(net, Cube) else list(range(count))
    halves = 2 if isinstance(net, Cube) else 1
    ids = jnp.stack([net.at(r) for r in order])

    def mixed_product(offs_ref, ids_ref, low_ref, *refs):
        outs, acc = refs[groups:-1], refs[-1]
        for r, block in enumerate(refs[:groups]):
            acc[block_at(offs_ref[r], cols), :] = dot_tn(block[...], low_ref[...])
        per = count // halves
        for i in range(count):
            for s in range(shards):
                row = (i % per * shards + s) * strip
                at = pl.multiple_of(s * depth + ids_ref[i] * strip, strip)
                outs[i // per][row : row + strip, :] = acc[pl.ds(at, strip), :].astype(BF)

    wo_grad = call(
        mixed_product, [offs, ids], [after(attn_grad, exchanged[1]), *blocks],
        [struct((width // halves, width), BF)] * halves, 4, "mixed_product", [pltpu.VMEM((width, width), F32)],
    )
    if isinstance(net, Cube):
        folded = net.fold(wo_grad[0], flip(wo_grad[1], 1))
    else:
        folded = lax.psum_scatter(wo_grad[0], "ctx", scatter_dimension=0, tiled=True)
    prior = None
    for (low, high), (_, o, lse) in zip(net.parts, attended):
        mgs = [jnp.pad(b, ((0, 0), (0, wide - cols))) for b in exchanged[low:high]]
        mgs = after(mgs, folded)
        prior = attend_back(q, qt, k, kt, v, mgs, o, lse, rows, heads, size, scale, low, high, prior)
        if isinstance(net, Cube):
            half = folded.shape[0] // 2
            sent = flip(folded[half:], 2 if low == 0 else 4)
            folded = net.fold(folded[:half], after(sent, prior if high == count else prior[0]))
    triple = after(prior, folded)
    forward_all = lax.all_gather(after(forward_own, triple), "ctx", axis=0, tiled=False)
    inner_sum = add_up(inner_sums).reshape(shards, units)
    last_pack = struct((3 * (depth + EXTRA) + strip * width // LANES, LANES), BF)
    into = input_terms(triple, qkv, rows, halves, 1.0 / copies)
    packs = pl.pallas_call(
        functools.partial(qkv_product_kernel, len(pieces), shards),
        in_specs=[IN_SMEM] + [IN_VMEM] * 5 + [pl.BlockSpec(memory_space=pl.ANY)] * len(pieces),
        out_specs=[IN_VMEM] * shards,
        out_shape=[last_pack] * shards,
        scratch_shapes=[pltpu.VMEM(p.shape, BF) for p in pieces]
        + [pltpu.VMEM((3 * wide, width), F32), pltpu.VMEM((EXTRA, 3 * wide), F32)]
        + [pltpu.SemaphoreType.DMA((len(pieces),))],
        compiler_params=params(60 * MIB),
        cost_estimate=micros(60),
        name="qkv_product",
    )(shard_ids, after(triple, into), sums_one, sums_two, inner_sum, folded, *pieces)
    packs = [packs[0]] + [shard_flip(packs[r], r, shards) for r in range(1, shards)]
    (last_own,) = call(sum_kernel, [], packs, [last_pack], 2, "last_sum")
    parts, n_whole, n_half = net.scatter_whole(*into, packs[0], last_own)
    (input_grad,) = call(
        functools.partial(input_kernel, n_whole, n_half), [], [attn_grad, *parts], [low_full], 2, "input_sum"
    )
    if isinstance(net, Cube):
        outer_out, inner_out = call(
            functools.partial(finish_forward_kernel, units), [], [forward_all],
            [struct((units * count, width), F32), struct((depth, units * count * shards), F32)], 6, "finish_forward",
            (), None,
        )
        last_all = net.gather(last_own, early=[outer_out])
        square = struct((depth, width), F32)
        query_out, key_out, value_out, wo_out, *vecs = call(
            finish_kernel, [shard_ids, offs], last_all,
            [square] * 4 + [struct((1, units * count), F32)] + [struct((1, depth), F32)] * 8, 4, "finish",
            [pltpu.VMEM((8, units * count), F32), pltpu.VMEM((16, width), F32)], None,
        )
        inner_vec, *vecs = [v.reshape(-1) for v in vecs]
    else:
        last_all = jnp.stack(net.gather(last_own)).astype(F32)
        triples = last_all[:, : 3 * (depth + EXTRA)].reshape(count, 3, depth + EXTRA, LANES)
        wo_out = last_all[:, 3 * (depth + EXTRA) :].reshape(count, width // LANES, strip, LANES)
        wo_out = wo_out.transpose(0, 2, 1, 3).reshape(depth, width)
        out3 = triples[::copies, :, :depth, :cols].transpose(1, 2, 0, 3).reshape(3, depth, width)
        query_out, key_out, value_out = out3[0], out3[1], out3[2]
        both = triples[::copies, :, depth, :cols].transpose(1, 0, 2).reshape(3, width)
        both = lax.dynamic_slice_in_dim(both, shard * depth, depth, 1)
        tail = triples[:, :, depth:].transpose(0, 2, 1, 3).reshape(count, EXTRA, 3 * LANES)
        six = jnp.sum(tail[:, 1:7, :depth], axis=0)
        vecs = [both[0], both[2]] + [six[i] for i in range(6)]
        inner_vec = tail[:, 7, 2 * LANES : 2 * LANES + units].reshape(-1)
        forward_all = forward_all.astype(F32)
        outer_out = forward_all[:, :units].reshape(-1, width)
        inner_out = forward_all[:, units:].reshape(count, depth // times, times, shards, units)
        inner_out = inner_out.transpose(2, 1, 3, 0, 4).reshape(depth, -1)
    return (
        result[None], input_grad[None], query_out, key_out, value_out, wo_out, inner_out, outer_out,
        vecs[0], vecs[1], vecs[2], vecs[3], vecs[4], inner_vec, vecs[5], vecs[6], vecs[7],
    )


def solution(mesh):
    sheet, matrix, vector = P("wsh", "ctx", None), P("wsh", None), P("wsh")
    return jax.shard_map(
        local,
        mesh=mesh,
        in_specs=(sheet, matrix) + (matrix,) * 6 + (vector,) * 9 + (sheet,),
        out_specs=(sheet, sheet) + (matrix,) * 6 + (vector,) * 9,
        check_vma=False,
    )
```

```python
import functools
import math

import jax
import jax.numpy as jnp
from jax import lax
from jax.experimental import pallas as pl
from jax.experimental.pallas import tpu as pltpu
from jax.sharding import PartitionSpec as P

HEADS = 16
LANES = 128
VECTORS = 32
EXTRA = 16
BF = jnp.bfloat16
F32 = jnp.float32
MIB = 1024 * 1024
IN_VMEM = pl.BlockSpec(memory_space=pltpu.VMEM)
IN_SMEM = pl.BlockSpec(memory_space=pltpu.SMEM)


def dot(a, b):
    return lax.dot_general(a, b, (((1,), (0,)), ((), ())), preferred_element_type=F32)


def dot_nt(a, b):
    return lax.dot_general(a, b, (((1,), (1,)), ((), ())), preferred_element_type=F32)


def dot_tn(a, b):
    return lax.dot_general(a, b, (((0,), (0,)), ((), ())), preferred_element_type=F32)


def struct(shape, dtype):
    return jax.ShapeDtypeStruct(shape, dtype)


def micros(us):
    return pl.CostEstimate(flops=int(us * 1e9), bytes_accessed=0, transcendentals=0)


def params(limit):
    return pltpu.CompilerParams(vmem_limit_bytes=min(limit, 60 * MIB))


def after(value, *others):
    return lax.optimization_barrier((value, others))[0]


def bytes_of(arrays):
    return sum(math.prod(a.shape) * a.dtype.itemsize for a in arrays)


def call(kernel, scalars, arrays, out_shape, us, name, scratch=(), room=6):
    limit = 60 * MIB if room is None else bytes_of(arrays) + bytes_of(out_shape) + bytes_of(scratch) + room * MIB
    return pl.pallas_call(
        kernel,
        in_specs=[IN_SMEM] * len(scalars) + [IN_VMEM] * len(arrays),
        out_specs=[IN_VMEM] * len(out_shape),
        out_shape=out_shape,
        scratch_shapes=list(scratch),
        compiler_params=params(limit),
        cost_estimate=micros(us),
        name=name,
    )(*scalars, *arrays)


def block_at(index, size):
    return pl.ds(pl.multiple_of(index * size, size), size)


def as_row(column):
    return jnp.broadcast_to(column, (column.shape[0], LANES)).T[0:1, :]


def add_up(parts):
    total = parts[0].astype(F32)
    for part in parts[1:]:
        total = total + part.astype(F32)
    return total


def pack_kernel(at_ref, q_ref, k_ref, v_ref, wo_ref, *refs):
    vectors, out_ref = refs[:-1], refs[-1]
    depth = q_ref.shape[0]
    strip = (out_ref.shape[0] - 3 * depth - VECTORS) * LANES // wo_ref.shape[1]
    lanes = pl.ds(pl.multiple_of(at_ref[0], LANES), LANES)
    for i, ref in enumerate((q_ref, k_ref, v_ref)):
        out_ref[i * depth : (i + 1) * depth, :] = ref[:, lanes]
    rows = jnp.concatenate([ref[...].astype(F32) for ref in vectors], axis=0)
    rows = jnp.concatenate([rows, jnp.zeros((VECTORS - rows.shape[0], LANES), F32)], axis=0)
    out_ref[3 * depth : 3 * depth + VECTORS, :] = rows.astype(BF)
    for i in range(wo_ref.shape[1] // LANES):
        row = 3 * depth + VECTORS + i * strip
        out_ref[row : row + strip, :] = wo_ref[block_at(at_ref[1], strip), i * LANES : (i + 1) * LANES]


def unpack_kernel(count, shard_ref, *refs):
    packs, (vec_ref, inner_ref) = refs[:count], refs[count:]
    depth = vec_ref.shape[1] // count
    vec_ref[...] = jnp.zeros_like(vec_ref)
    inner_ref[...] = jnp.zeros_like(inner_ref)
    per = depth // LANES
    for r, pack in enumerate(packs):
        at = shard_ref[r]
        rows = pack[3 * depth : 3 * depth + VECTORS, :].astype(F32)
        for i in range(8):
            for j in range(per):
                vec_ref[i : i + 1, block_at(at * per + j, LANES)] = rows[i * per + j : i * per + j + 1, :]
        for j in range(inner_ref.shape[1] // LANES):
            row = rows[8 * per + j : 8 * per + j + 1, :]
            inner_ref[block_at(at, 8), j * LANES : (j + 1) * LANES] = jnp.broadcast_to(row, (8, LANES))


def stack_kernel(start, *refs):
    row = 0
    for ref in refs[:-1]:
        rows = ref.shape[0] - start
        refs[-1][row : row + rows, :] = ref[start:, :]
        row += rows


def stack(arrays, start=0):
    rows = sum(a.shape[0] - start for a in arrays)
    out = struct((rows, arrays[0].shape[1]), arrays[0].dtype)
    return call(functools.partial(stack_kernel, start), [], arrays, [out], 1, "stack", (), 1)[0]


def project_kernel(count, shards, cols, scale, shard_ref, place_ref, starts_ref, *refs):
    pieces, packs = refs[:count], refs[count : count + shards]
    bias_ref, w_ref, q_ref, k_ref, v_ref, qt_ref, kt_ref = refs[count + shards :]
    depth = w_ref.shape[0] // shards
    for r, pack in enumerate(packs):
        for i in range(3):
            rows = pack[i * depth : (i + 1) * depth, :]
            w_ref[block_at(shard_ref[r], depth), i * LANES : (i + 1) * LANES] = rows
    weight = w_ref[...]
    documents = starts_ref.shape[0]
    row = 0
    for p, piece in enumerate(pieces):
        rows = piece.shape[0]
        at = slice(row, row + rows)
        raw = dot(piece[...], weight)
        q_ref[at, :] = ((raw[:, :cols] + bias_ref[0:1, :]) * scale).astype(BF)
        k_ref[at, :] = raw[:, cols : 2 * cols].astype(BF)
        v_ref[at, :] = (raw[:, 2 * cols :] + bias_ref[1:2, :]).astype(BF)
        place = place_ref[p] + lax.broadcasted_iota(jnp.int32, (rows, LANES), 0)
        segment = jnp.full((rows, LANES), -1, jnp.int32)
        for j in range(documents):
            segment = segment + (starts_ref[j] <= place).astype(jnp.int32)
        lane = lax.broadcasted_iota(jnp.int32, (rows, LANES), 1)
        same = segment == lane
        qt_ref[at, :] = jnp.where(same | (lane >= documents), 0.0, -1e30).astype(BF)
        kt_ref[at, :] = jnp.where(same, 1.0, 0.0).astype(BF)
        row += rows


def head_lanes(rows, wide, h, size):
    lane = lax.broadcasted_iota(jnp.int32, (rows, wide), 1)
    return (lane >= h * size) & (lane < (h + 1) * size)


def attend_kernel(heads, size, q_ref, qt_ref, k_ref, kt_ref, v_ref, low_ref, o_ref, lse_ref):
    rows, wide = q_ref.shape
    keys = jnp.concatenate([k_ref[...], kt_ref[...]], axis=1)
    query, tail = q_ref[...], qt_ref[...]
    out = jnp.zeros((rows, wide), F32)
    for h in range(heads):
        mine = head_lanes(rows, wide, h, size)
        scores = dot_nt(jnp.concatenate([jnp.where(mine, query, jnp.zeros_like(query)), tail], axis=1), keys)
        top = jnp.max(scores, axis=1, keepdims=True)
        probs = jnp.exp(scores - top)
        total = jnp.sum(probs, axis=1, keepdims=True)
        out = jnp.where(mine, dot(probs.astype(BF), v_ref[...]) / total, out)
        lse_ref[h : h + 1, :] = as_row(top + jnp.log(total))
    o_ref[...] = out
    low_ref[...] = out.astype(BF)


def attend(q, qt, k, kt, v, rows, heads, size, low, high):
    length, wide = q.shape
    part = pl.BlockSpec((rows, wide), lambda i: (i + low, 0))
    whole = pl.BlockSpec((length, wide), lambda i: (0, 0))
    tail = pl.BlockSpec((length, LANES), lambda i: (0, 0))
    out = pl.BlockSpec((rows, wide), lambda i: (i, 0))
    count = (high - low) * rows
    return pl.pallas_call(
        functools.partial(attend_kernel, heads, size),
        grid=(high - low,),
        in_specs=[part, pl.BlockSpec((rows, LANES), lambda i: (i + low, 0)), whole, tail, whole],
        out_specs=[out, out, pl.BlockSpec((8, rows), lambda i: (0, i))],
        out_shape=[struct((count, wide), BF), struct((count, wide), F32), struct((8, count), F32)],
        compiler_params=params(8 * MIB + 20 * rows * length + 8 * bytes_of([q])),
        cost_estimate=micros(9),
        name="attend",
    )(q, qt, k, kt, v)


def attend_back_kernel(heads, size, scale, first, last, count, done, q_ref, qt_ref, k_ref, kt_ref, v_ref, o_ref, lse_ref, *refs):
    mgs, refs = refs[:count], refs[count:]
    prior = ()
    if not first:
        prior, refs = refs[:3], refs[3:]
    if last:
        out_ref, kx, mg_s, dk_acc, dv_acc = refs
    else:
        out_ref, dk_acc, dv_acc, kx, mg_s = refs
    step = pl.program_id(0)
    rows, wide = q_ref.shape

    @pl.when(step == 0)
    def _():
        if first:
            dk_acc[...] = jnp.zeros_like(dk_acc)
            dv_acc[...] = jnp.zeros_like(dv_acc)
        else:
            out_ref[:done, :wide] = prior[0][...]
            dk_acc[...] = prior[1][...]
            dv_acc[...] = prior[2][...]
        kx[...] = k_ref[...].astype(F32).T.astype(BF)

    each = mg_s.shape[0] // mgs[0].shape[0]
    for i in range(count // each):

        @pl.when(step == i)
        def _(i=i):
            for j in range(each):
                block = mgs[i * each + j]
                mg_s[j * block.shape[0] : (j + 1) * block.shape[0], :] = block[...]

    keys = jnp.concatenate([k_ref[...], kt_ref[...]], axis=1)
    query, tail, mg = q_ref[...], qt_ref[...], mg_s[...]
    spread = mg.astype(F32) * o_ref[...]
    turned = []
    for h in range(heads):
        mine = head_lanes(rows, wide, h, size)
        query_h = jnp.where(mine, query, jnp.zeros_like(query))
        mg_h = jnp.where(mine, mg, jnp.zeros_like(mg))
        row_terms = as_row(jnp.sum(jnp.where(mine, spread, 0.0), axis=1, keepdims=True))
        scores = dot_nt(keys, jnp.concatenate([query_h, tail], axis=1))
        probs = jnp.exp(scores - lse_ref[h : h + 1, :])
        dv_acc[...] += dot(probs.astype(BF), mg_h)
        grads = (probs * (dot_nt(v_ref[...], mg_h) - row_terms)).astype(BF)
        dk_acc[...] += dot(grads, query_h)
        turned.append(dot(kx[h * size : (h + 1) * size, :], grads))
    if heads * size < wide:
        turned.append(jnp.zeros((wide - heads * size, rows), F32))
    at = pl.ds(pl.multiple_of(done + step * rows, rows), rows) if last else block_at(step, rows)
    out_ref[at, :wide] = (jnp.concatenate(turned, axis=0).T * scale).astype(BF)
    if last:

        @pl.when(step == pl.num_programs(0) - 1)
        def _():
            out_ref[:, wide : 2 * wide] = dk_acc[...].astype(BF)
            out_ref[:, 2 * wide :] = dv_acc[...].astype(BF)


def attend_back(q, qt, k, kt, v, mgs, o, lse, rows, heads, size, scale, low, high, prior):
    length, wide = q.shape
    last = high * rows == length
    piece, count = rows, high - low
    if count % 2 == 0 and low % 2 == 0 and 2 * rows * length <= MIB:
        rows, low, high = 2 * rows, low // 2, high // 2
    fixed = lambda i: (0, 0)
    whole = pl.BlockSpec((length, wide), fixed)
    full = struct((length, wide), F32)
    scratch = [pltpu.VMEM((wide, length), BF), pltpu.VMEM((rows, wide), BF)]
    if last:
        out_specs = pl.BlockSpec((length, 3 * wide), fixed)
        out_shape = struct((length, 3 * wide), BF)
        scratch += [pltpu.VMEM((length, wide), F32)] * 2
    else:
        out_specs = [pl.BlockSpec((count * piece, wide), fixed), whole, whole]
        out_shape = [struct((count * piece, wide), BF), full, full]
    return pl.pallas_call(
        functools.partial(
            attend_back_kernel, heads, size, scale, prior is None, last, count, low * rows
        ),
        grid=(high - low,),
        in_specs=[
            pl.BlockSpec((rows, wide), lambda i: (i + low, 0)),
            pl.BlockSpec((rows, LANES), lambda i: (i + low, 0)),
            whole,
            pl.BlockSpec((length, LANES), fixed),
            whole,
            pl.BlockSpec((rows, wide), lambda i: (i, 0)),
            pl.BlockSpec((8, rows), lambda i: (0, i)),
        ]
        + [pl.BlockSpec((piece, wide), fixed)] * count
        + ([] if prior is None else [pl.BlockSpec((low * rows, wide), fixed), whole, whole]),
        out_specs=out_specs,
        out_shape=out_shape,
        scratch_shapes=scratch,
        compiler_params=params(60 * MIB),
        cost_estimate=micros(7),
        name="attend_back",
    )(q, qt, k, kt, v, o, lse, *mgs, *(prior or ()))


def normalize(source):
    mean = jnp.mean(source, axis=-1, keepdims=True)
    centered = source - mean
    root = lax.rsqrt(jnp.mean(centered * centered, axis=-1, keepdims=True) + 1e-05)
    return centered * root, root


def norm_back(normed, root, grad, gain):
    scaled = grad * gain
    mean = jnp.mean(scaled, axis=-1, keepdims=True)
    mix = jnp.mean(scaled * normed, axis=-1, keepdims=True)
    return root * (scaled - mean - normed * mix)


def column_sums(sums_ref, rows):
    sums_ref[...] = jnp.zeros_like(sums_ref)
    for i, row in enumerate(rows):
        sums_ref[i : i + 1, :] = jnp.sum(row, axis=0, keepdims=True)


def collected(refs, whole, halves):
    full = add_up([r[...] for r in refs[:whole]])
    if not halves:
        return full
    upper = add_up([r[...] for r in refs[whole : whole + halves]])
    lower = add_up([r[...] for r in refs[whole + halves : whole + 2 * halves]])
    return full + jnp.concatenate([upper, lower], axis=0)


def first_norm_kernel(count, offs_ref, x_ref, wo_ref, vec_ref, *refs):
    blocks, (low_ref, normed_ref, root_ref) = refs[:count], refs[count:]
    wide = wo_ref.shape[0] // count
    out = x_ref[...].astype(F32) + vec_ref[2:3, :]
    for r, block in enumerate(blocks):
        out = out + dot(block[...], wo_ref[block_at(offs_ref[r], wide), :])
    normed, root = normalize(out)
    low_ref[...] = (normed * vec_ref[3:4, :] + vec_ref[4:5, :]).astype(BF)
    normed_ref[...] = normed.astype(BF)
    root_ref[...] = root


def second_norm_kernel(whole, halves, hidden_ref, vec_ref, cot_ref, *refs):
    parts, (res_ref, low_ref, sums_ref) = refs[:-3], refs[-3:]
    normed, root = normalize(hidden_ref[...].astype(F32) + collected(parts, whole, halves) + vec_ref[5:6, :])
    gain = vec_ref[6:7, :]
    res_ref[...] = (normed * gain + vec_ref[7:8, :]).astype(BF)
    grad = cot_ref[...].astype(F32)
    low = norm_back(normed, root, grad, gain).astype(BF)
    low_ref[...] = low
    column_sums(sums_ref, [low.astype(F32), grad * normed, grad])


def first_back_kernel(count, whole, halves, offs_ref, resid_ref, normed_ref, root_ref, vec_ref, wo_ref, *refs):
    parts = refs[: whole + 2 * halves]
    low_ref, sums_ref, *outs = refs[whole + 2 * halves :]
    wide = wo_ref.shape[0] // count
    grad = resid_ref[...].astype(F32) + collected(parts, whole, halves)
    normed = normed_ref[...].astype(F32)
    low = norm_back(normed, root_ref[...], grad, vec_ref[3:4, :]).astype(BF)
    low_ref[...] = low
    for r in range(count):
        outs[r][...] = dot_nt(low, wo_ref[block_at(offs_ref[r], wide), :]).astype(BF)
    column_sums(sums_ref, [low.astype(F32), grad * normed, grad])


def input_kernel(whole, halves, first_ref, *refs):
    parts, out_ref = refs[:-1], refs[-1]
    out_ref[...] = (first_ref[...].astype(F32) + collected(parts, whole, halves)).astype(BF)


def assemble_kernel(shards, strip, shard_ref, ids_ref, *refs):
    slabs, out_ref = refs[:-1], refs[-1]
    tiles = out_ref.shape[1] // LANES
    per = slabs[0].shape[0] // (shards * tiles * strip)
    depth = out_ref.shape[0] // shards
    for i, slab in enumerate(slabs):
        for b in range(per):
            for r in range(shards):
                row = pl.multiple_of(shard_ref[r] * depth + ids_ref[i * per + b] * strip, strip)
                for t in range(tiles):
                    source = ((b * shards + r) * tiles + t) * strip
                    out_ref[pl.ds(row, strip), t * LANES : (t + 1) * LANES] = slab[source : source + strip, :]


def gelu_pair(source):
    bell = 0.5 * (1.0 + lax.erf(source * (0.5**0.5)))
    slope = bell + source * jnp.exp(-0.5 * source * source) * ((2.0 * jnp.pi) ** -0.5)
    return source * bell, slope


def forward_kernel(count, inner_ref, bias_ref, outer_ref, *refs):
    for p in range(count):
        act, slope = gelu_pair(dot(refs[p][...], inner_ref[...]) + bias_ref[...])
        low = act.astype(BF)
        refs[count + p][...] = low
        refs[2 * count + p][...] = slope.astype(BF)
        refs[3 * count + p][...] = dot(low, outer_ref[...]).astype(BF)


def backward_kernel(count, inner_ref, outer_ref, *refs):
    total = jnp.zeros((1, inner_ref.shape[1]), F32)
    for p in range(count):
        grad = (dot_nt(refs[p][...], outer_ref[...]) * refs[count + p][...].astype(F32)).astype(BF)
        refs[2 * count + p][...] = grad
        refs[3 * count + p][...] = dot_nt(grad, inner_ref[...]).astype(BF)
        total = total + jnp.sum(grad.astype(F32), axis=0, keepdims=True)
    refs[-1][...] = total


def product_kernel(count, given, *refs):
    acts, grads, hidden, inner = [refs[i * count : (i + 1) * count] for i in range(4)]
    prior, outs = refs[4 * count : 4 * count + given], refs[4 * count + given :]
    for i, (left, right, out) in enumerate(((acts, grads, outs[0]), (hidden, inner, outs[1]))):
        total = prior[i][...] if given else None
        for p in range(count):
            term = dot_tn(left[p][...], right[p][...])
            total = term if total is None else total + term
        out[...] = total


def last_product_kernel(count, given, shards, *refs):
    outer_acc, inner_acc = refs[-2:]
    out_ref = refs[-3]
    product_kernel(count, given, *refs[:-3], outer_acc, inner_acc)
    units = outer_acc.shape[0] // shards
    height = out_ref.shape[0] // shards
    depth, share = inner_acc.shape[0] // shards, inner_acc.shape[1]
    rows = height - units
    for s in range(shards):
        out_ref[s * height : s * height + units, :] = outer_acc[s * units : (s + 1) * units, :].astype(BF)
        for i in range(depth // rows):
            out_ref[s * height + units : (s + 1) * height, i * share : (i + 1) * share] = inner_acc[
                s * depth + i * rows : s * depth + (i + 1) * rows, :
            ].astype(BF)


def weights_kernel(units, all_ref, inner_ref, outer_ref):
    shards, height, width = all_ref.shape
    rows = height - units
    share = inner_ref.shape[1]
    for s in range(shards):
        outer_ref[s * units : (s + 1) * units, :] = all_ref[s, :units, :]
        for i in range(width // share):
            row = (s * (width // share) + i) * rows
            inner_ref[row : row + rows, :] = all_ref[s, units:, i * share : (i + 1) * share]


def finish_forward_kernel(units, all_ref, outer_ref, inner_ref):
    count, height, width = all_ref.shape
    rows = height - units
    times = inner_ref.shape[0] // rows
    share = width // times
    stretch = units * count
    for c in range(count):
        outer_ref[c * units : (c + 1) * units, :] = all_ref[c, :units, :].astype(F32)
        for i in range(times):
            for s in range(share // units):
                inner_ref[i * rows : (i + 1) * rows, s * stretch + c * units : s * stretch + (c + 1) * units] = all_ref[
                    c, units:, i * share + s * units : i * share + (s + 1) * units
                ].astype(F32)


def into_kernel(factor, rows, triple_ref, w_ref, *outs):
    for i in range(triple_ref.shape[0] // rows):
        term = dot_nt(triple_ref[i * rows : (i + 1) * rows, :], w_ref[...])
        at = i // len(outs) * rows
        outs[i % len(outs)][at : at + rows, :] = (term if factor == 1.0 else term * factor).astype(BF)


def input_terms(triple, w, rows, outs, factor):
    shape = struct((triple.shape[0] // outs, w.shape[0]), BF)
    return call(functools.partial(into_kernel, factor, rows), [], [triple, w], [shape] * outs, 4, "into", (), None)


def qkv_product_kernel(count, shards, shard_ref, triple_ref, one_ref, two_ref, inner_ref, wo_ref, *refs):
    sources, outs, buffers = refs[:count], refs[count : count + shards], refs[count + shards : 2 * count + shards]
    acc, bias, sems = refs[2 * count + shards :]
    copies = [pltpu.make_async_copy(a, b, sems.at[i]) for i, (a, b) in enumerate(zip(sources, buffers))]
    for copy in copies:
        copy.start()
    row = 0
    bias[...] = jnp.zeros_like(bias)
    bias[0:1, :] = jnp.sum(triple_ref[...].astype(F32), axis=0, keepdims=True)
    for p, piece in enumerate(buffers):
        copies[p].wait()
        rows = piece.shape[0]
        term = dot_tn(triple_ref[row : row + rows, :], piece[...])
        if p == 0:
            acc[...] = term
        else:
            acc[...] += term
        row += rows
    depth = acc.shape[1] // len(outs)
    units = inner_ref.shape[1]
    strip = wo_ref.shape[0] // len(outs)
    height = depth + EXTRA
    for r, out in enumerate(outs):
        at = shard_ref[r]
        for i in range(3):
            bias[1 + i : 2 + i, :depth] = one_ref[i : i + 1, block_at(at, depth)]
            bias[4 + i : 5 + i, :depth] = two_ref[i : i + 1, block_at(at, depth)]
        bias[7:8, 2 * LANES : 2 * LANES + units] = inner_ref[pl.ds(at, 1), :]
        for i in range(3):
            lanes = slice(i * LANES, (i + 1) * LANES)
            out[i * height : i * height + depth, :] = acc[lanes, block_at(at, depth)].T.astype(BF)
            out[i * height + depth : (i + 1) * height, :] = bias[:, lanes].astype(BF)
        for i in range(wo_ref.shape[1] // LANES):
            row = 3 * height + i * strip
            out[row : row + strip, :] = wo_ref[block_at(at, strip), i * LANES : (i + 1) * LANES]


def sum_kernel(*refs):
    refs[-1][...] = add_up([r[...] for r in refs[:-1]]).astype(BF)


def fold_kernel(keep_ref, other_ref, own_ref, *outs):
    total = keep_ref[...].astype(F32) + other_ref[...].astype(F32)
    rows = own_ref.shape[0]
    own_ref[...] = total[:rows].astype(BF)
    for i, out in enumerate(outs):
        out[...] = total[rows + i * rows // 2 : rows + (i + 1) * rows // 2].astype(BF)


def finish_kernel(shard_ref, offs_ref, *refs):
    pieces, (q_ref, k_ref, v_ref, wo_ref, inner_ref, *vecs, inner_all, bias) = refs[:-15], refs[-15:]
    depth = q_ref.shape[0]
    height = depth + EXTRA
    cols = LANES
    total = None
    for r, block in enumerate(Cube.blocks(pieces)):
        block = jnp.concatenate([p[...] for p in block], axis=0)
        lanes = block_at(offs_ref[r], cols)
        for i, out in enumerate((q_ref, k_ref, v_ref)):
            out[:, lanes] = block[i * height : i * height + depth, :].astype(F32)
        tails = [block[i * height + depth : (i + 1) * height, :].astype(F32) for i in range(3)]
        bias[0:8, lanes] = jnp.broadcast_to(tails[0][0:1, :], (8, cols))
        bias[8:16, lanes] = jnp.broadcast_to(tails[2][0:1, :], (8, cols))
        inner_all[:, lanes] = jnp.broadcast_to(tails[2][7:8, :], (8, cols))
        tail = jnp.concatenate(tails, axis=1)
        total = tail if total is None else total + tail
        strip = (block.shape[0] - 3 * height) * LANES // wo_ref.shape[1]
        for i in range(wo_ref.shape[1] // LANES):
            row = 3 * height + i * strip
            wo_ref[block_at(offs_ref[r], strip), i * LANES : (i + 1) * LANES] = block[row : row + strip, :].astype(F32)
    mine = block_at(shard_ref[0], depth)
    vecs[0][...] = bias[0:1, mine]
    vecs[1][...] = bias[8:9, mine]
    for i in range(6):
        vecs[2 + i][...] = total[1 + i : 2 + i, :depth]
    inner_ref[...] = inner_all[0:1, :]


def flip(source, bit):
    return lax.ppermute(source, "ctx", [(i, i ^ bit) for i in range(8)])


def shard_flip(source, bit, shards):
    return lax.ppermute(source, "wsh", [(i, i ^ bit) for i in range(shards)])


class Cube:
    def __init__(self):
        self.count = 8

    def at(self, r):
        return lax.axis_index("ctx") ^ r

    def gather(self, own, work=None, early=(), late=()):
        half = own.shape[0] // 32 * 16
        side, down = flip(own, 2), flip(own, 4)
        if work is not None:
            core = flip(own, 1)
            first = work([own, core])
        side, down = after((side, down), *([first] if work is not None else early))
        far_a, far_b = flip(side[:half], 4), flip(down[half:], 2)
        if work is None:
            own_, side_, down_ = after((own, side, down), far_a, far_b)
            core, side1, down1 = flip(own_, 1), flip(side_, 1), flip(down_, 1)
            late = late((far_a, far_b)) if callable(late) else late
        else:
            side1, down1 = flip(side, 1), flip(down, 1)
            second = work([side, side1, down, down1])
        far_a, far_b = after((far_a, far_b), *([second] if work is not None else late))
        far1_a, far1_b = flip(far_a, 1), flip(far_b, 1)
        pieces = [own, core, side, side1, down, down1, far_a, far_b, far1_a, far1_b]
        if work is None:
            return pieces
        third = work(pieces[6:])
        return pieces, [[*a, *b, *c] for a, b, c in zip(first, second, third)]

    def gather_slab(self, own, beside):
        others = after([flip(own, r) for r in (2, 4, 6)], beside)
        four = stack([own, *others])
        return [four, flip(four, 1)]

    slab_order = (0, 2, 4, 6, 1, 3, 5, 7)

    def scatter_whole(self, keep, send, first, second):
        rows, width = keep.shape[0] // 4, keep.shape[1]
        own, side_a, side_b, down_a, down_b, far_a, far_b = call(
            fold_kernel, [], [keep, after(flip(send, 1), first)],
            [struct((rows, width), BF)] + [struct((rows // 2, width), BF)] * 6, 3, "fold",
        )
        over_side, over_down = after((flip(far_a, 2), flip(far_b, 4)), second)
        side_a, down_b = flip(side_a, 2), flip(down_b, 4)
        moved = self.fold(side_b, over_down), self.fold(down_a, over_side)
        side_b, down_a = flip(moved[0], 2), flip(moved[1], 4)
        return [own, side_a, down_a, side_b, down_b], 1, 2

    @staticmethod
    def fold(half, other):
        return (half.astype(F32) + other.astype(F32)).astype(BF)

    def places(self, rows):
        own = [self.at(r) * rows for r in range(8)]
        half = rows // 2
        return own[:6] + [own[6], own[6] + half, own[7], own[7] + half]

    @staticmethod
    def blocks(pieces):
        return [(p,) for p in pieces[:6]] + [(pieces[6], pieces[7]), (pieces[8], pieces[9])]

    def scatter(self, pieces):
        own, core, side, side1, down, down1, far_a, far_b, far1_a, far1_b = pieces
        half = own.shape[0] // 2
        far_a = (far_a.astype(F32) + flip(far1_a, 1).astype(F32)).astype(BF)
        over_side = flip(far_a, 2)
        far_b = (far_b.astype(F32) + flip(far1_b, 1).astype(F32)).astype(BF)
        over_down = flip(far_b, 4)
        side = side.astype(F32) + flip(side1, 1).astype(F32)
        down = down.astype(F32) + flip(down1, 1).astype(F32)
        side_a = flip(side[:half].astype(BF), 2)
        down_b = flip(down[half:].astype(BF), 4)
        side_b = (side[half:] + over_down.astype(F32)).astype(BF)
        down_a = (down[:half] + over_side.astype(F32)).astype(BF)
        return [own, flip(core, 1), side_a, flip(down_a, 4), flip(side_b, 2), down_b], 2, 2, (side_b, down_a)

    parts = ((0, 4), (4, 8))

    def exchange(self, blocks, low):
        return [flip(block, low + i) if low + i else block for i, block in enumerate(blocks)]


class Line:
    def __init__(self, count):
        self.count = count

    def at(self, r):
        return jnp.int32(r)

    def gather(self, own, work=None, early=(), late=()):
        pieces = list(lax.all_gather(own, "ctx", axis=0, tiled=False))
        if callable(late):
            late(own)
        if work is None:
            return pieces
        groups = [work(group) for group in grouped(pieces, 4)]
        return pieces, [[piece for part in parts for piece in part] for parts in zip(*groups)]

    def places(self, rows):
        return [jnp.int32(r * rows) for r in range(self.count)]

    def scatter(self, pieces):
        whole = jnp.concatenate(pieces, axis=0)
        return [lax.psum_scatter(whole, "ctx", scatter_dimension=0, tiled=True)], 1, 0, ()

    @property
    def parts(self):
        return ((0, self.count),)

    def scatter_whole(self, addends, first, second):
        return [lax.psum_scatter(addends, "ctx", scatter_dimension=0, tiled=True)], 1, 0

    def exchange(self, blocks, low):
        return list(lax.all_to_all(jnp.stack(blocks), "ctx", 0, 0, tiled=False))


def grouped(items, size):
    return [items[i : i + size] for i in range(0, len(items), size)]


def local(
    tokens, starts, query_weight, key_weight, value_weight, output_weight, inner_weight, outer_weight,
    query_bias, value_bias, output_bias, first_gain, first_shift, inner_bias, outer_bias,
    second_gain, second_shift, cotangent,
):
    count, shards = lax.axis_size("ctx"), lax.axis_size("wsh")
    net = Cube() if count == 8 else Line(count)
    me, shard = lax.axis_index("ctx"), lax.axis_index("wsh")
    x = tokens[0]
    rows, width = x.shape
    length = rows * count
    size = width // HEADS
    heads = max(1, HEADS // count)
    copies = max(1, count // HEADS)
    cols = heads * size
    wide = -(-cols // LANES) * LANES
    depth = width // shards
    units = outer_weight.shape[0] // count
    strip = depth // count
    scale = size**-0.5
    shard_ids = jnp.stack([shard ^ r for r in range(shards)])
    places = jnp.stack(net.places(rows))

    first_col = me // copies * cols

    def own_columns(w):
        return jnp.pad(lax.dynamic_slice_in_dim(w, first_col, cols, 1), ((0, 0), (0, wide - cols)))

    weights, lane = [query_weight, key_weight, value_weight], first_col
    if cols % LANES:
        weights, lane = [own_columns(w) for w in weights], jnp.int32(0)
    wo_own, wo_at = output_weight, me
    if strip % 16:
        wo_own, wo_at = lax.dynamic_slice_in_dim(output_weight, me * strip, strip, 0), jnp.int32(0)
    vectors = [query_bias, value_bias, output_bias, first_gain, first_shift, outer_bias, second_gain,
               second_shift, inner_bias]
    vectors = [v.reshape(-1, LANES) for v in vectors]
    (pack,) = call(
        pack_kernel, [jnp.stack([lane, wo_at])], [*weights, wo_own, *vectors],
        [struct((3 * depth + VECTORS + strip * width // LANES, LANES), BF)], 20, "pack", (), None,
    )
    packs = [pack] + [shard_flip(pack, r, shards) for r in range(1, shards)]
    share = units * shards
    times = width // share
    inner_own = [
        lax.dynamic_slice_in_dim(inner_weight, s * units * count + me * units, units, 1) for s in range(shards)
    ]
    inner_own = jnp.concatenate(inner_own, axis=1)
    inner_own = jnp.concatenate([inner_own[i * depth // times : (i + 1) * depth // times] for i in range(times)], axis=1)
    outer_own = lax.dynamic_slice_in_dim(outer_weight, me * units, units, 0)
    forward_pack = jnp.concatenate([outer_own, inner_own], axis=0)
    unpacked = []

    def unpack(marker):
        made = call(
            functools.partial(unpack_kernel, shards), [shard_ids], after(packs, marker),
            [struct((8, width), F32), struct((8 * shards, inner_bias.shape[0]), F32)], 20, "unpack",
        )
        unpacked.extend(made)
        return [forward_pack]

    pieces = net.gather(x, early=[pack], late=unpack)
    vec, inner_all = unpacked
    bias = jnp.pad(lax.dynamic_slice(vec, (0, first_col), (8, cols)), ((0, 0), (0, wide - cols)))
    inner_b = lax.dynamic_slice_in_dim(inner_all[::8], me * units, units, 1).reshape(1, -1)

    qkv_rows = []
    done = 0
    for group in grouped(pieces, 10):
        group_rows = sum(p.shape[0] for p in group)
        sheet = struct((group_rows, wide), BF)
        tail = struct((group_rows, LANES), BF)
        qkv, *made = call(
            functools.partial(project_kernel, len(group), shards, wide, scale),
            [shard_ids, places[done : done + len(group)], starts[0]],
            [*group, *packs, bias],
            [struct((width, 3 * wide), BF), sheet, sheet, sheet, tail, tail],
            4, "project",
        )
        qkv_rows.append(made)
        done += len(group)
    q, k, v, qt, kt = [made[0] if len(made) == 1 else jnp.concatenate(made) for made in zip(*qkv_rows)]

    forward_pack = lax.all_gather(after(forward_pack, packs, pieces[6:8]), "wsh", axis=0, tiled=False)

    attended, blocks = [], []
    for low, high in net.parts:
        made = attend(q, qt, k, kt, v, rows, heads, size, low, high)
        attended.append(made)
        mixed = [made[0][i * rows : (i + 1) * rows, :cols] for i in range(high - low)]
        if blocks:
            mixed, *tied = after((mixed, *blocks, slabs[1]), made[0])
            blocks, slabs[1] = tied[:-1], tied[-1]
        blocks += net.exchange(mixed, low)
        if high < count:
            slabs = net.gather_slab(stack(packs, 3 * depth + VECTORS), made[0])
            q, k = after((q, k), slabs[0])
    if isinstance(net, Cube):
        ids = jnp.stack([net.at(r) for r in net.slab_order])
        (wo,) = call(
            functools.partial(assemble_kernel, shards, strip), [shard_ids, ids], slabs,
            [struct((width, width), BF)], 2, "assemble",
        )
    else:
        wo_slab = jnp.zeros((shards, strip, width), BF)
        for r in range(shards):
            part = packs[r][3 * depth + VECTORS :].reshape(width // LANES, strip, LANES).transpose(1, 0, 2).reshape(1, strip, width)
            wo_slab = lax.dynamic_update_slice(wo_slab, part, (shard ^ r, jnp.int32(0), jnp.int32(0)))
        wo = lax.all_gather(wo_slab, "ctx", axis=0, tiled=False)
        wo = wo.transpose(1, 0, 2, 3).reshape(width, width)
    blocks = blocks[::copies]
    offs = jnp.stack([net.at(r) // copies for r in range(0, count, copies)])
    groups = len(blocks)
    low_full, tall = struct((rows, width), BF), struct((rows, 1), F32)
    sums = struct((8, width), F32)
    hidden_low, normed, root = call(
        functools.partial(first_norm_kernel, groups), [offs], [x, wo, vec, *blocks],
        [low_full, low_full, tall], 5, "first_norm",
    )
    inner, outer = call(
        functools.partial(weights_kernel, units), [], [forward_pack],
        [struct((width, share), BF), struct((share, width), BF)], 2, "weights",
    )

    def forward(group):
        sizes = [p.shape[0] for p in group]
        mids = [struct((s, units * shards), BF) for s in sizes]
        made = call(
            functools.partial(forward_kernel, len(group)), [], [inner, inner_b, outer, *group],
            mids + mids + [struct((s, width), BF) for s in sizes], 1.5 * sum(sizes) / 256, "forward",
        )
        n = len(group)
        return made[:n], made[n : 2 * n], made[2 * n :]

    hidden_all, (acts, slopes, branch) = net.gather(hidden_low, forward)
    parts, n_whole, n_half, _ = net.scatter(branch)
    result, branch_grad, sums_two = call(
        functools.partial(second_norm_kernel, n_whole, n_half), [], [hidden_low, vec, cotangent[0], *parts],
        [low_full, low_full, sums], 4, "second_norm",
    )

    inner_sums, waiting, products = [], list(slopes), []

    def backward(group):
        sizes = [p.shape[0] for p in group]
        n, at = len(group), len(acts) - len(waiting)
        slope, waiting[:n] = waiting[:n], []
        made = call(
            functools.partial(backward_kernel, n), [], [inner, outer, *group, *slope],
            [struct((s, units * shards), BF) for s in sizes]
            + [struct((s, width), BF) for s in sizes]
            + [struct((1, units * shards), F32)],
            1.5 * sum(sizes) / 256, "backward",
        )
        inner_sums.append(made[-1])
        terms = [*acts[at : at + n], *group, *hidden_all[at : at + n], *made[:n]]
        if at + n < len(acts):
            given = products[-1] if products else []
            products.append(
                pl.pallas_call(
                    functools.partial(product_kernel, n, len(given)),
                    in_specs=[IN_VMEM] * (4 * n + len(given)),
                    out_specs=[IN_VMEM] * 2,
                    out_shape=[struct((share, width), F32), struct((width, share), F32)],
                    input_output_aliases={4 * n + i: i for i in range(len(given))},
                    compiler_params=params(bytes_of(terms) + 2 * 4 * share * width + 8 * MIB),
                    cost_estimate=micros(3),
                    name="product",
                )(*terms, *given)
            )
            return made[:n], made[n:-1], list(products[-1])
        return made[:n], made[n:-1], terms

    grad_all, (inner_grads, hidden_grads, terms) = net.gather(branch_grad, backward)
    n = len(terms[2 * len(products) :]) // 4
    given, terms = products[-1], terms[2 * len(products) :]
    parts, n_whole, n_half, moved = net.scatter(hidden_grads)
    height = units + depth * share // width
    (forward_wg,) = call(
        functools.partial(last_product_kernel, n, len(given), shards), [], [*after(terms, moved), *given],
        [struct((shards * height, width), BF)], 5, "last_product",
        [pltpu.VMEM((share, width), F32), pltpu.VMEM((width, share), F32)],
    )
    parts = after(parts, forward_wg)
    forward_own = lax.psum_scatter(forward_wg, "wsh", scatter_dimension=0, tiled=True)
    attn_grad, sums_one, *mixed_grads = call(
        functools.partial(first_back_kernel, groups, n_whole, n_half), [offs],
        [branch_grad, normed, root, vec, wo, *parts],
        [low_full, sums] + [struct((rows, cols), BF)] * groups, 5, "first_back", (), None,
    )
    if copies > 1:
        mixed_grads = [b for b in mixed_grads for _ in range(copies)]
    exchanged = []
    for low, high in net.parts:
        exchanged += net.exchange(mixed_grads[low:high], low)
    order = [0, 4, 2, 6, 1, 5, 3, 7] if isinstance(net, Cube) else list(range(count))
    halves = 2 if isinstance(net, Cube) else 1
    ids = jnp.stack([net.at(r) for r in order])

    def mixed_product(offs_ref, ids_ref, low_ref, *refs):
        outs, acc = refs[groups:-1], refs[-1]
        for r, block in enumerate(refs[:groups]):
            acc[block_at(offs_ref[r], cols), :] = dot_tn(block[...], low_ref[...])
        per = count // halves
        for i in range(count):
            for s in range(shards):
                row = (i % per * shards + s) * strip
                at = pl.multiple_of(s * depth + ids_ref[i] * strip, strip)
                outs[i // per][row : row + strip, :] = acc[pl.ds(at, strip), :].astype(BF)

    wo_grad = call(
        mixed_product, [offs, ids], [after(attn_grad, exchanged[1]), *blocks],
        [struct((width // halves, width), BF)] * halves, 4, "mixed_product", [pltpu.VMEM((width, width), F32)],
    )
    if isinstance(net, Cube):
        folded = net.fold(wo_grad[0], flip(wo_grad[1], 1))
    else:
        folded = lax.psum_scatter(wo_grad[0], "ctx", scatter_dimension=0, tiled=True)
    prior = None
    for (low, high), (_, o, lse) in zip(net.parts, attended):
        mgs = [jnp.pad(b, ((0, 0), (0, wide - cols))) for b in exchanged[low:high]]
        mgs = after(mgs, folded)
        prior = attend_back(q, qt, k, kt, v, mgs, o, lse, rows, heads, size, scale, low, high, prior)
        if isinstance(net, Cube):
            half = folded.shape[0] // 2
            sent = flip(folded[half:], 2 if low == 0 else 4)
            folded = net.fold(folded[:half], after(sent, prior if high == count else prior[0]))
    triple = after(prior, folded)
    forward_all = lax.all_gather(after(forward_own, triple), "ctx", axis=0, tiled=False)
    inner_sum = add_up(inner_sums).reshape(shards, units)
    last_pack = struct((3 * (depth + EXTRA) + strip * width // LANES, LANES), BF)
    into = input_terms(triple, qkv, rows, halves, 1.0 / copies)
    packs = pl.pallas_call(
        functools.partial(qkv_product_kernel, len(pieces), shards),
        in_specs=[IN_SMEM] + [IN_VMEM] * 5 + [pl.BlockSpec(memory_space=pl.ANY)] * len(pieces),
        out_specs=[IN_VMEM] * shards,
        out_shape=[last_pack] * shards,
        scratch_shapes=[pltpu.VMEM(p.shape, BF) for p in pieces]
        + [pltpu.VMEM((3 * wide, width), F32), pltpu.VMEM((EXTRA, 3 * wide), F32)]
        + [pltpu.SemaphoreType.DMA((len(pieces),))],
        compiler_params=params(60 * MIB),
        cost_estimate=micros(60),
        name="qkv_product",
    )(shard_ids, after(triple, into), sums_one, sums_two, inner_sum, folded, *pieces)
    packs = [packs[0]] + [shard_flip(packs[r], r, shards) for r in range(1, shards)]
    (last_own,) = call(sum_kernel, [], packs, [last_pack], 2, "last_sum")
    parts, n_whole, n_half = net.scatter_whole(*into, packs[0], last_own)
    (input_grad,) = call(
        functools.partial(input_kernel, n_whole, n_half), [], [attn_grad, *parts], [low_full], 2, "input_sum"
    )
    if isinstance(net, Cube):
        outer_out, inner_out = call(
            functools.partial(finish_forward_kernel, units), [], [forward_all],
            [struct((units * count, width), F32), struct((depth, units * count * shards), F32)], 6, "finish_forward",
            (), 2,
        )
        last_all = net.gather(last_own, early=[outer_out, parts[1], parts[4]])
        square = struct((depth, width), F32)
        query_out, key_out, value_out, wo_out, *vecs = call(
            finish_kernel, [shard_ids, offs], last_all,
            [square] * 4 + [struct((1, units * count), F32)] + [struct((1, depth), F32)] * 8, 4, "finish",
            [pltpu.VMEM((8, units * count), F32), pltpu.VMEM((16, width), F32)], 3,
        )
        inner_vec, *vecs = [v.reshape(-1) for v in vecs]
    else:
        last_all = jnp.stack(net.gather(last_own)).astype(F32)
        triples = last_all[:, : 3 * (depth + EXTRA)].reshape(count, 3, depth + EXTRA, LANES)
        wo_out = last_all[:, 3 * (depth + EXTRA) :].reshape(count, width // LANES, strip, LANES)
        wo_out = wo_out.transpose(0, 2, 1, 3).reshape(depth, width)
        out3 = triples[::copies, :, :depth, :cols].transpose(1, 2, 0, 3).reshape(3, depth, width)
        query_out, key_out, value_out = out3[0], out3[1], out3[2]
        both = triples[::copies, :, depth, :cols].transpose(1, 0, 2).reshape(3, width)
        both = lax.dynamic_slice_in_dim(both, shard * depth, depth, 1)
        tail = triples[:, :, depth:].transpose(0, 2, 1, 3).reshape(count, EXTRA, 3 * LANES)
        six = jnp.sum(tail[:, 1:7, :depth], axis=0)
        vecs = [both[0], both[2]] + [six[i] for i in range(6)]
        inner_vec = tail[:, 7, 2 * LANES : 2 * LANES + units].reshape(-1)
        forward_all = forward_all.astype(F32)
        outer_out = forward_all[:, :units].reshape(-1, width)
        inner_out = forward_all[:, units:].reshape(count, depth // times, times, shards, units)
        inner_out = inner_out.transpose(2, 1, 3, 0, 4).reshape(depth, -1)
    return (
        result[None], input_grad[None], query_out, key_out, value_out, wo_out, inner_out, outer_out,
        vecs[0], vecs[1], vecs[2], vecs[3], vecs[4], inner_vec, vecs[5], vecs[6], vecs[7],
    )


def solution(mesh):
    sheet, matrix, vector = P("wsh", "ctx", None), P("wsh", None), P("wsh")
    return jax.shard_map(
        local,
        mesh=mesh,
        in_specs=(sheet, matrix) + (matrix,) * 6 + (vector,) * 9 + (sheet,),
        out_specs=(sheet, sheet) + (matrix,) * 6 + (vector,) * 9,
        check_vma=False,
    )
```

```python
import functools
import math

import jax
import jax.numpy as jnp
from jax import lax
from jax.experimental import pallas as pl
from jax.experimental.pallas import tpu as pltpu
from jax.sharding import PartitionSpec as P

HEADS = 16
LANES = 128
VECTORS = 32
EXTRA = 16
BF = jnp.bfloat16
F32 = jnp.float32
MIB = 1024 * 1024
IN_VMEM = pl.BlockSpec(memory_space=pltpu.VMEM)
IN_SMEM = pl.BlockSpec(memory_space=pltpu.SMEM)


def dot(a, b):
    return lax.dot_general(a, b, (((1,), (0,)), ((), ())), preferred_element_type=F32)


def dot_nt(a, b):
    return lax.dot_general(a, b, (((1,), (1,)), ((), ())), preferred_element_type=F32)


def dot_tn(a, b):
    return lax.dot_general(a, b, (((0,), (0,)), ((), ())), preferred_element_type=F32)


def struct(shape, dtype):
    return jax.ShapeDtypeStruct(shape, dtype)


def micros(us):
    return pl.CostEstimate(flops=int(us * 1e9), bytes_accessed=0, transcendentals=0)


def params(limit):
    return pltpu.CompilerParams(vmem_limit_bytes=min(limit, 60 * MIB))


def after(value, *others):
    return lax.optimization_barrier((value, others))[0]


def bytes_of(arrays):
    return sum(math.prod(a.shape) * a.dtype.itemsize for a in arrays)


def call(kernel, scalars, arrays, out_shape, us, name, scratch=(), room=6):
    limit = 60 * MIB if room is None else bytes_of(arrays) + bytes_of(out_shape) + bytes_of(scratch) + room * MIB
    return pl.pallas_call(
        kernel,
        in_specs=[IN_SMEM] * len(scalars) + [IN_VMEM] * len(arrays),
        out_specs=[IN_VMEM] * len(out_shape),
        out_shape=out_shape,
        scratch_shapes=list(scratch),
        compiler_params=params(limit),
        cost_estimate=micros(us),
        name=name,
    )(*scalars, *arrays)


def block_at(index, size):
    return pl.ds(pl.multiple_of(index * size, size), size)


def as_row(column):
    return jnp.broadcast_to(column, (column.shape[0], LANES)).T[0:1, :]


def add_up(parts):
    total = parts[0].astype(F32)
    for part in parts[1:]:
        total = total + part.astype(F32)
    return total


def pack_kernel(at_ref, q_ref, k_ref, v_ref, wo_ref, *refs):
    vectors, out_ref = refs[:-1], refs[-1]
    depth = q_ref.shape[0]
    strip = (out_ref.shape[0] - 3 * depth - VECTORS) * LANES // wo_ref.shape[1]
    lanes = pl.ds(pl.multiple_of(at_ref[0], LANES), LANES)
    for i, ref in enumerate((q_ref, k_ref, v_ref)):
        out_ref[i * depth : (i + 1) * depth, :] = ref[:, lanes]
    rows = jnp.concatenate([ref[...].astype(F32) for ref in vectors], axis=0)
    rows = jnp.concatenate([rows, jnp.zeros((VECTORS - rows.shape[0], LANES), F32)], axis=0)
    out_ref[3 * depth : 3 * depth + VECTORS, :] = rows.astype(BF)
    for i in range(wo_ref.shape[1] // LANES):
        row = 3 * depth + VECTORS + i * strip
        out_ref[row : row + strip, :] = wo_ref[block_at(at_ref[1], strip), i * LANES : (i + 1) * LANES]


def unpack_kernel(count, shard_ref, *refs):
    packs, (vec_ref, inner_ref) = refs[:count], refs[count:]
    depth = vec_ref.shape[1] // count
    vec_ref[...] = jnp.zeros_like(vec_ref)
    inner_ref[...] = jnp.zeros_like(inner_ref)
    per = depth // LANES
    for r, pack in enumerate(packs):
        at = shard_ref[r]
        rows = pack[3 * depth : 3 * depth + VECTORS, :].astype(F32)
        for i in range(8):
            for j in range(per):
                vec_ref[i : i + 1, block_at(at * per + j, LANES)] = rows[i * per + j : i * per + j + 1, :]
        for j in range(inner_ref.shape[1] // LANES):
            row = rows[8 * per + j : 8 * per + j + 1, :]
            inner_ref[block_at(at, 8), j * LANES : (j + 1) * LANES] = jnp.broadcast_to(row, (8, LANES))


def stack_kernel(start, *refs):
    row = 0
    for ref in refs[:-1]:
        rows = ref.shape[0] - start
        refs[-1][row : row + rows, :] = ref[start:, :]
        row += rows


def stack(arrays, start=0):
    rows = sum(a.shape[0] - start for a in arrays)
    out = struct((rows, arrays[0].shape[1]), arrays[0].dtype)
    return call(functools.partial(stack_kernel, start), [], arrays, [out], 1, "stack", (), 1)[0]


def project_kernel(count, shards, cols, scale, shard_ref, place_ref, starts_ref, *refs):
    pieces, packs = refs[:count], refs[count : count + shards]
    bias_ref, w_ref, q_ref, k_ref, v_ref, qt_ref, kt_ref = refs[count + shards :]
    depth = w_ref.shape[0] // shards
    for r, pack in enumerate(packs):
        for i in range(3):
            rows = pack[i * depth : (i + 1) * depth, :]
            w_ref[block_at(shard_ref[r], depth), i * LANES : (i + 1) * LANES] = rows
    weight = w_ref[...]
    documents = starts_ref.shape[0]
    row = 0
    for p, piece in enumerate(pieces):
        rows = piece.shape[0]
        at = slice(row, row + rows)
        raw = dot(piece[...], weight)
        q_ref[at, :] = ((raw[:, :cols] + bias_ref[0:1, :]) * scale).astype(BF)
        k_ref[at, :] = raw[:, cols : 2 * cols].astype(BF)
        v_ref[at, :] = (raw[:, 2 * cols :] + bias_ref[1:2, :]).astype(BF)
        place = place_ref[p] + lax.broadcasted_iota(jnp.int32, (rows, LANES), 0)
        segment = jnp.full((rows, LANES), -1, jnp.int32)
        for j in range(documents):
            segment = segment + (starts_ref[j] <= place).astype(jnp.int32)
        lane = lax.broadcasted_iota(jnp.int32, (rows, LANES), 1)
        same = segment == lane
        qt_ref[at, :] = jnp.where(same | (lane >= documents), 0.0, -1e30).astype(BF)
        kt_ref[at, :] = jnp.where(same, 1.0, 0.0).astype(BF)
        row += rows


def head_lanes(rows, wide, h, size):
    lane = lax.broadcasted_iota(jnp.int32, (rows, wide), 1)
    return (lane >= h * size) & (lane < (h + 1) * size)


def attend_kernel(heads, size, q_ref, qt_ref, k_ref, kt_ref, v_ref, low_ref, o_ref, lse_ref):
    rows, wide = q_ref.shape
    keys = jnp.concatenate([k_ref[...], kt_ref[...]], axis=1)
    query, tail = q_ref[...], qt_ref[...]
    out = jnp.zeros((rows, wide), F32)
    for h in range(heads):
        mine = head_lanes(rows, wide, h, size)
        scores = dot_nt(jnp.concatenate([jnp.where(mine, query, jnp.zeros_like(query)), tail], axis=1), keys)
        top = jnp.max(scores, axis=1, keepdims=True)
        probs = jnp.exp(scores - top)
        total = jnp.sum(probs, axis=1, keepdims=True)
        out = jnp.where(mine, dot(probs.astype(BF), v_ref[...]) / total, out)
        lse_ref[h : h + 1, :] = as_row(top + jnp.log(total))
    o_ref[...] = out
    low_ref[...] = out.astype(BF)


def attend(q, qt, k, kt, v, rows, heads, size, low, high):
    length, wide = q.shape
    part = pl.BlockSpec((rows, wide), lambda i: (i + low, 0))
    whole = pl.BlockSpec((length, wide), lambda i: (0, 0))
    tail = pl.BlockSpec((length, LANES), lambda i: (0, 0))
    out = pl.BlockSpec((rows, wide), lambda i: (i, 0))
    count = (high - low) * rows
    return pl.pallas_call(
        functools.partial(attend_kernel, heads, size),
        grid=(high - low,),
        in_specs=[part, pl.BlockSpec((rows, LANES), lambda i: (i + low, 0)), whole, tail, whole],
        out_specs=[out, out, pl.BlockSpec((8, rows), lambda i: (0, i))],
        out_shape=[struct((count, wide), BF), struct((count, wide), F32), struct((8, count), F32)],
        compiler_params=params(8 * MIB + 20 * rows * length + 8 * bytes_of([q])),
        cost_estimate=micros(9),
        name="attend",
    )(q, qt, k, kt, v)


def attend_back_kernel(heads, size, scale, first, last, count, done, q_ref, qt_ref, k_ref, kt_ref, v_ref, o_ref, lse_ref, *refs):
    mgs, refs = refs[:count], refs[count:]
    prior = ()
    if not first:
        prior, refs = refs[:3], refs[3:]
    if last:
        out_ref, kx, mg_s, dk_acc, dv_acc = refs
    else:
        out_ref, dk_acc, dv_acc, kx, mg_s = refs
    step = pl.program_id(0)
    rows, wide = q_ref.shape

    @pl.when(step == 0)
    def _():
        if first:
            dk_acc[...] = jnp.zeros_like(dk_acc)
            dv_acc[...] = jnp.zeros_like(dv_acc)
        else:
            out_ref[:done, :wide] = prior[0][...]
            dk_acc[...] = prior[1][...]
            dv_acc[...] = prior[2][...]
        kx[...] = k_ref[...].astype(F32).T.astype(BF)

    each = mg_s.shape[0] // mgs[0].shape[0]
    for i in range(count // each):

        @pl.when(step == i)
        def _(i=i):
            for j in range(each):
                block = mgs[i * each + j]
                mg_s[j * block.shape[0] : (j + 1) * block.shape[0], :] = block[...]

    keys = jnp.concatenate([k_ref[...], kt_ref[...]], axis=1)
    query, tail, mg = q_ref[...], qt_ref[...], mg_s[...]
    spread = mg.astype(F32) * o_ref[...]
    turned = []
    for h in range(heads):
        mine = head_lanes(rows, wide, h, size)
        query_h = jnp.where(mine, query, jnp.zeros_like(query))
        mg_h = jnp.where(mine, mg, jnp.zeros_like(mg))
        row_terms = as_row(jnp.sum(jnp.where(mine, spread, 0.0), axis=1, keepdims=True))
        scores = dot_nt(keys, jnp.concatenate([query_h, tail], axis=1))
        probs = jnp.exp(scores - lse_ref[h : h + 1, :])
        dv_acc[...] += dot(probs.astype(BF), mg_h)
        grads = (probs * (dot_nt(v_ref[...], mg_h) - row_terms)).astype(BF)
        dk_acc[...] += dot(grads, query_h)
        turned.append(dot(kx[h * size : (h + 1) * size, :], grads))
    if heads * size < wide:
        turned.append(jnp.zeros((wide - heads * size, rows), F32))
    at = pl.ds(pl.multiple_of(done + step * rows, rows), rows) if last else block_at(step, rows)
    out_ref[at, :wide] = (jnp.concatenate(turned, axis=0).T * scale).astype(BF)
    if last:

        @pl.when(step == pl.num_programs(0) - 1)
        def _():
            out_ref[:, wide : 2 * wide] = dk_acc[...].astype(BF)
            out_ref[:, 2 * wide :] = dv_acc[...].astype(BF)


def attend_back(q, qt, k, kt, v, mgs, o, lse, rows, heads, size, scale, low, high, prior):
    length, wide = q.shape
    last = high * rows == length
    piece, count = rows, high - low
    if count % 2 == 0 and low % 2 == 0 and 2 * rows * length <= MIB:
        rows, low, high = 2 * rows, low // 2, high // 2
    fixed = lambda i: (0, 0)
    whole = pl.BlockSpec((length, wide), fixed)
    full = struct((length, wide), F32)
    scratch = [pltpu.VMEM((wide, length), BF), pltpu.VMEM((rows, wide), BF)]
    if last:
        out_specs = pl.BlockSpec((length, 3 * wide), fixed)
        out_shape = struct((length, 3 * wide), BF)
        scratch += [pltpu.VMEM((length, wide), F32)] * 2
    else:
        out_specs = [pl.BlockSpec((count * piece, wide), fixed), whole, whole]
        out_shape = [struct((count * piece, wide), BF), full, full]
    return pl.pallas_call(
        functools.partial(
            attend_back_kernel, heads, size, scale, prior is None, last, count, low * rows
        ),
        grid=(high - low,),
        in_specs=[
            pl.BlockSpec((rows, wide), lambda i: (i + low, 0)),
            pl.BlockSpec((rows, LANES), lambda i: (i + low, 0)),
            whole,
            pl.BlockSpec((length, LANES), fixed),
            whole,
            pl.BlockSpec((rows, wide), lambda i: (i, 0)),
            pl.BlockSpec((8, rows), lambda i: (0, i)),
        ]
        + [pl.BlockSpec((piece, wide), fixed)] * count
        + ([] if prior is None else [pl.BlockSpec((low * rows, wide), fixed), whole, whole]),
        out_specs=out_specs,
        out_shape=out_shape,
        scratch_shapes=scratch,
        compiler_params=params(60 * MIB),
        cost_estimate=micros(7),
        name="attend_back",
    )(q, qt, k, kt, v, o, lse, *mgs, *(prior or ()))


def normalize(source):
    mean = jnp.mean(source, axis=-1, keepdims=True)
    centered = source - mean
    root = lax.rsqrt(jnp.mean(centered * centered, axis=-1, keepdims=True) + 1e-05)
    return centered * root, root


def norm_back(normed, root, grad, gain):
    scaled = grad * gain
    mean = jnp.mean(scaled, axis=-1, keepdims=True)
    mix = jnp.mean(scaled * normed, axis=-1, keepdims=True)
    return root * (scaled - mean - normed * mix)


def column_sums(sums_ref, rows):
    sums_ref[...] = jnp.zeros_like(sums_ref)
    for i, row in enumerate(rows):
        sums_ref[i : i + 1, :] = jnp.sum(row, axis=0, keepdims=True)


def collected(refs, whole, halves):
    full = add_up([r[...] for r in refs[:whole]])
    if not halves:
        return full
    upper = add_up([r[...] for r in refs[whole : whole + halves]])
    lower = add_up([r[...] for r in refs[whole + halves : whole + 2 * halves]])
    return full + jnp.concatenate([upper, lower], axis=0)


def first_norm_kernel(count, offs_ref, x_ref, wo_ref, vec_ref, *refs):
    blocks, (low_ref, normed_ref, root_ref) = refs[:count], refs[count:]
    wide = wo_ref.shape[0] // count
    out = x_ref[...].astype(F32) + vec_ref[2:3, :]
    for r, block in enumerate(blocks):
        out = out + dot(block[...], wo_ref[block_at(offs_ref[r], wide), :])
    normed, root = normalize(out)
    low_ref[...] = (normed * vec_ref[3:4, :] + vec_ref[4:5, :]).astype(BF)
    normed_ref[...] = normed.astype(BF)
    root_ref[...] = root


def second_norm_kernel(whole, halves, hidden_ref, vec_ref, cot_ref, *refs):
    parts, (res_ref, low_ref, sums_ref) = refs[:-3], refs[-3:]
    normed, root = normalize(hidden_ref[...].astype(F32) + collected(parts, whole, halves) + vec_ref[5:6, :])
    gain = vec_ref[6:7, :]
    res_ref[...] = (normed * gain + vec_ref[7:8, :]).astype(BF)
    grad = cot_ref[...].astype(F32)
    low = norm_back(normed, root, grad, gain).astype(BF)
    low_ref[...] = low
    column_sums(sums_ref, [low.astype(F32), grad * normed, grad])


def first_back_kernel(count, whole, halves, offs_ref, resid_ref, normed_ref, root_ref, vec_ref, wo_ref, *refs):
    parts = refs[: whole + 2 * halves]
    low_ref, sums_ref, *outs = refs[whole + 2 * halves :]
    wide = wo_ref.shape[0] // count
    grad = resid_ref[...].astype(F32) + collected(parts, whole, halves)
    normed = normed_ref[...].astype(F32)
    low = norm_back(normed, root_ref[...], grad, vec_ref[3:4, :]).astype(BF)
    low_ref[...] = low
    for r in range(count):
        outs[r][...] = dot_nt(low, wo_ref[block_at(offs_ref[r], wide), :]).astype(BF)
    column_sums(sums_ref, [low.astype(F32), grad * normed, grad])


def input_kernel(whole, halves, first_ref, *refs):
    parts, out_ref = refs[:-1], refs[-1]
    out_ref[...] = (first_ref[...].astype(F32) + collected(parts, whole, halves)).astype(BF)


def assemble_kernel(shards, strip, shard_ref, ids_ref, *refs):
    slabs, out_ref = refs[:-1], refs[-1]
    tiles = out_ref.shape[1] // LANES
    per = slabs[0].shape[0] // (shards * tiles * strip)
    depth = out_ref.shape[0] // shards
    for i, slab in enumerate(slabs):
        for b in range(per):
            for r in range(shards):
                row = pl.multiple_of(shard_ref[r] * depth + ids_ref[i * per + b] * strip, strip)
                for t in range(tiles):
                    source = ((b * shards + r) * tiles + t) * strip
                    out_ref[pl.ds(row, strip), t * LANES : (t + 1) * LANES] = slab[source : source + strip, :]


def gelu_pair(source):
    bell = 0.5 * (1.0 + lax.erf(source * (0.5**0.5)))
    slope = bell + source * jnp.exp(-0.5 * source * source) * ((2.0 * jnp.pi) ** -0.5)
    return source * bell, slope


def forward_kernel(count, inner_ref, bias_ref, outer_ref, *refs):
    for p in range(count):
        act, slope = gelu_pair(dot(refs[p][...], inner_ref[...]) + bias_ref[...])
        low = act.astype(BF)
        refs[count + p][...] = low
        refs[2 * count + p][...] = slope.astype(BF)
        refs[3 * count + p][...] = dot(low, outer_ref[...]).astype(BF)


def backward_kernel(count, inner_ref, outer_ref, *refs):
    total = jnp.zeros((1, inner_ref.shape[1]), F32)
    for p in range(count):
        grad = (dot_nt(refs[p][...], outer_ref[...]) * refs[count + p][...].astype(F32)).astype(BF)
        refs[2 * count + p][...] = grad
        refs[3 * count + p][...] = dot_nt(grad, inner_ref[...]).astype(BF)
        total = total + jnp.sum(grad.astype(F32), axis=0, keepdims=True)
    refs[-1][...] = total


def product_kernel(count, given, *refs):
    acts, grads, hidden, inner = [refs[i * count : (i + 1) * count] for i in range(4)]
    prior, outs = refs[4 * count : 4 * count + given], refs[4 * count + given :]
    for i, (left, right, out) in enumerate(((acts, grads, outs[0]), (hidden, inner, outs[1]))):
        total = prior[i][...] if given else None
        for p in range(count):
            term = dot_tn(left[p][...], right[p][...])
            total = term if total is None else total + term
        out[...] = total


def last_product_kernel(count, given, shards, *refs):
    outer_acc, inner_acc = refs[-2:]
    out_ref = refs[-3]
    product_kernel(count, given, *refs[:-3], outer_acc, inner_acc)
    units = outer_acc.shape[0] // shards
    height = out_ref.shape[0] // shards
    depth, share = inner_acc.shape[0] // shards, inner_acc.shape[1]
    rows = height - units
    for s in range(shards):
        out_ref[s * height : s * height + units, :] = outer_acc[s * units : (s + 1) * units, :].astype(BF)
        for i in range(depth // rows):
            out_ref[s * height + units : (s + 1) * height, i * share : (i + 1) * share] = inner_acc[
                s * depth + i * rows : s * depth + (i + 1) * rows, :
            ].astype(BF)


def weights_kernel(units, all_ref, inner_ref, outer_ref):
    shards, height, width = all_ref.shape
    rows = height - units
    share = inner_ref.shape[1]
    for s in range(shards):
        outer_ref[s * units : (s + 1) * units, :] = all_ref[s, :units, :]
        for i in range(width // share):
            row = (s * (width // share) + i) * rows
            inner_ref[row : row + rows, :] = all_ref[s, units:, i * share : (i + 1) * share]


def finish_forward_kernel(units, all_ref, outer_ref, inner_ref):
    count, height, width = all_ref.shape
    rows = height - units
    times = inner_ref.shape[0] // rows
    share = width // times
    stretch = units * count
    for c in range(count):
        outer_ref[c * units : (c + 1) * units, :] = all_ref[c, :units, :].astype(F32)
        for i in range(times):
            for s in range(share // units):
                inner_ref[i * rows : (i + 1) * rows, s * stretch + c * units : s * stretch + (c + 1) * units] = all_ref[
                    c, units:, i * share + s * units : i * share + (s + 1) * units
                ].astype(F32)


def into_kernel(factor, rows, triple_ref, w_ref, *outs):
    for i in range(triple_ref.shape[0] // rows):
        term = dot_nt(triple_ref[i * rows : (i + 1) * rows, :], w_ref[...])
        at = i // len(outs) * rows
        outs[i % len(outs)][at : at + rows, :] = (term if factor == 1.0 else term * factor).astype(BF)


def input_terms(triple, w, rows, outs, factor):
    shape = struct((triple.shape[0] // outs, w.shape[0]), BF)
    return call(functools.partial(into_kernel, factor, rows), [], [triple, w], [shape] * outs, 4, "into", (), 3)


def qkv_product_kernel(count, shards, shard_ref, triple_ref, one_ref, two_ref, inner_ref, wo_ref, *refs):
    sources, outs, buffers = refs[:count], refs[count : count + shards], refs[count + shards : 2 * count + shards]
    acc, bias, sems = refs[2 * count + shards :]
    copies = [pltpu.make_async_copy(a, b, sems.at[i]) for i, (a, b) in enumerate(zip(sources, buffers))]
    for copy in copies:
        copy.start()
    row = 0
    bias[...] = jnp.zeros_like(bias)
    bias[0:1, :] = jnp.sum(triple_ref[...].astype(F32), axis=0, keepdims=True)
    for p, piece in enumerate(buffers):
        copies[p].wait()
        rows = piece.shape[0]
        term = dot_tn(triple_ref[row : row + rows, :], piece[...])
        if p == 0:
            acc[...] = term
        else:
            acc[...] += term
        row += rows
    depth = acc.shape[1] // len(outs)
    units = inner_ref.shape[1]
    strip = wo_ref.shape[0] // len(outs)
    height = depth + EXTRA
    for r, out in enumerate(outs):
        at = shard_ref[r]
        for i in range(3):
            bias[1 + i : 2 + i, :depth] = one_ref[i : i + 1, block_at(at, depth)]
            bias[4 + i : 5 + i, :depth] = two_ref[i : i + 1, block_at(at, depth)]
        bias[7:8, 2 * LANES : 2 * LANES + units] = inner_ref[pl.ds(at, 1), :]
        for i in range(3):
            lanes = slice(i * LANES, (i + 1) * LANES)
            out[i * height : i * height + depth, :] = acc[lanes, block_at(at, depth)].T.astype(BF)
            out[i * height + depth : (i + 1) * height, :] = bias[:, lanes].astype(BF)
        for i in range(wo_ref.shape[1] // LANES):
            row = 3 * height + i * strip
            out[row : row + strip, :] = wo_ref[block_at(at, strip), i * LANES : (i + 1) * LANES]


def sum_kernel(*refs):
    refs[-1][...] = add_up([r[...] for r in refs[:-1]]).astype(BF)


def fold_kernel(keep_ref, other_ref, own_ref, *outs):
    total = keep_ref[...].astype(F32) + other_ref[...].astype(F32)
    rows = own_ref.shape[0]
    own_ref[...] = total[:rows].astype(BF)
    for i, out in enumerate(outs):
        out[...] = total[rows + i * rows // 2 : rows + (i + 1) * rows // 2].astype(BF)


def finish_kernel(shard_ref, offs_ref, *refs):
    pieces, (q_ref, k_ref, v_ref, wo_ref, inner_ref, *vecs, inner_all, bias) = refs[:-15], refs[-15:]
    depth = q_ref.shape[0]
    height = depth + EXTRA
    cols = LANES
    total = None
    for r, block in enumerate(Cube.blocks(pieces)):
        block = jnp.concatenate([p[...] for p in block], axis=0)
        lanes = block_at(offs_ref[r], cols)
        for i, out in enumerate((q_ref, k_ref, v_ref)):
            out[:, lanes] = block[i * height : i * height + depth, :].astype(F32)
        tails = [block[i * height + depth : (i + 1) * height, :].astype(F32) for i in range(3)]
        bias[0:8, lanes] = jnp.broadcast_to(tails[0][0:1, :], (8, cols))
        bias[8:16, lanes] = jnp.broadcast_to(tails[2][0:1, :], (8, cols))
        inner_all[:, lanes] = jnp.broadcast_to(tails[2][7:8, :], (8, cols))
        tail = jnp.concatenate(tails, axis=1)
        total = tail if total is None else total + tail
        strip = (block.shape[0] - 3 * height) * LANES // wo_ref.shape[1]
        for i in range(wo_ref.shape[1] // LANES):
            row = 3 * height + i * strip
            wo_ref[block_at(offs_ref[r], strip), i * LANES : (i + 1) * LANES] = block[row : row + strip, :].astype(F32)
    mine = block_at(shard_ref[0], depth)
    vecs[0][...] = bias[0:1, mine]
    vecs[1][...] = bias[8:9, mine]
    for i in range(6):
        vecs[2 + i][...] = total[1 + i : 2 + i, :depth]
    inner_ref[...] = inner_all[0:1, :]


def flip(source, bit):
    return lax.ppermute(source, "ctx", [(i, i ^ bit) for i in range(8)])


def shard_flip(source, bit, shards):
    return lax.ppermute(source, "wsh", [(i, i ^ bit) for i in range(shards)])


class Cube:
    def __init__(self):
        self.count = 8

    def at(self, r):
        return lax.axis_index("ctx") ^ r

    def gather(self, own, work=None, early=(), late=()):
        half = own.shape[0] // 32 * 16
        side, down = flip(own, 2), flip(own, 4)
        if work is not None:
            core = flip(own, 1)
            first = work([own, core])
        side, down = after((side, down), *([first] if work is not None else early))
        far_a, far_b = flip(side[:half], 4), flip(down[half:], 2)
        if work is None:
            own_, side_, down_ = after((own, side, down), far_a, far_b)
            core, side1, down1 = flip(own_, 1), flip(side_, 1), flip(down_, 1)
            late = late((far_a, far_b)) if callable(late) else late
        else:
            side1, down1 = flip(side, 1), flip(down, 1)
            second = work([side, side1, down, down1])
        far_a, far_b = after((far_a, far_b), *([second] if work is not None else late))
        far1_a, far1_b = flip(far_a, 1), flip(far_b, 1)
        pieces = [own, core, side, side1, down, down1, far_a, far_b, far1_a, far1_b]
        if work is None:
            return pieces
        third = work(pieces[6:])
        return pieces, [[*a, *b, *c] for a, b, c in zip(first, second, third)]

    def gather_slab(self, own, beside):
        others = after([flip(own, r) for r in (2, 4, 6)], beside)
        four = stack([own, *others])
        return [four, flip(four, 1)]

    slab_order = (0, 2, 4, 6, 1, 3, 5, 7)

    def scatter_whole(self, keep, send, first, second):
        rows, width = keep.shape[0] // 4, keep.shape[1]
        own, side_a, side_b, down_a, down_b, far_a, far_b = call(
            fold_kernel, [], [keep, after(flip(send, 1), first)],
            [struct((rows, width), BF)] + [struct((rows // 2, width), BF)] * 6, 3, "fold",
        )
        over_side, over_down = after((flip(far_a, 2), flip(far_b, 4)), second)
        side_a, down_b = flip(side_a, 2), flip(down_b, 4)
        moved = self.fold(side_b, over_down), self.fold(down_a, over_side)
        side_b, down_a = flip(moved[0], 2), flip(moved[1], 4)
        return [own, side_a, down_a, side_b, down_b], 1, 2

    @staticmethod
    def fold(half, other):
        return (half.astype(F32) + other.astype(F32)).astype(BF)

    def places(self, rows):
        own = [self.at(r) * rows for r in range(8)]
        half = rows // 2
        return own[:6] + [own[6], own[6] + half, own[7], own[7] + half]

    @staticmethod
    def blocks(pieces):
        return [(p,) for p in pieces[:6]] + [(pieces[6], pieces[7]), (pieces[8], pieces[9])]

    def scatter(self, pieces):
        own, core, side, side1, down, down1, far_a, far_b, far1_a, far1_b = pieces
        half = own.shape[0] // 2
        far_a = (far_a.astype(F32) + flip(far1_a, 1).astype(F32)).astype(BF)
        over_side = flip(far_a, 2)
        far_b = (far_b.astype(F32) + flip(far1_b, 1).astype(F32)).astype(BF)
        over_down = flip(far_b, 4)
        side = side.astype(F32) + flip(side1, 1).astype(F32)
        down = down.astype(F32) + flip(down1, 1).astype(F32)
        side_a = flip(side[:half].astype(BF), 2)
        down_b = flip(down[half:].astype(BF), 4)
        side_b = (side[half:] + over_down.astype(F32)).astype(BF)
        down_a = (down[:half] + over_side.astype(F32)).astype(BF)
        return [own, flip(core, 1), side_a, flip(down_a, 4), flip(side_b, 2), down_b], 2, 2, (side_b, down_a)

    parts = ((0, 4), (4, 8))

    def exchange(self, blocks, low):
        return [flip(block, low + i) if low + i else block for i, block in enumerate(blocks)]


class Line:
    def __init__(self, count):
        self.count = count

    def at(self, r):
        return jnp.int32(r)

    def gather(self, own, work=None, early=(), late=()):
        pieces = list(lax.all_gather(own, "ctx", axis=0, tiled=False))
        if callable(late):
            late(own)
        if work is None:
            return pieces
        groups = [work(group) for group in grouped(pieces, 4)]
        return pieces, [[piece for part in parts for piece in part] for parts in zip(*groups)]

    def places(self, rows):
        return [jnp.int32(r * rows) for r in range(self.count)]

    def scatter(self, pieces):
        whole = jnp.concatenate(pieces, axis=0)
        return [lax.psum_scatter(whole, "ctx", scatter_dimension=0, tiled=True)], 1, 0, ()

    @property
    def parts(self):
        return ((0, self.count),)

    def scatter_whole(self, addends, first, second):
        return [lax.psum_scatter(addends, "ctx", scatter_dimension=0, tiled=True)], 1, 0

    def exchange(self, blocks, low):
        return list(lax.all_to_all(jnp.stack(blocks), "ctx", 0, 0, tiled=False))


def grouped(items, size):
    return [items[i : i + size] for i in range(0, len(items), size)]


def local(
    tokens, starts, query_weight, key_weight, value_weight, output_weight, inner_weight, outer_weight,
    query_bias, value_bias, output_bias, first_gain, first_shift, inner_bias, outer_bias,
    second_gain, second_shift, cotangent,
):
    count, shards = lax.axis_size("ctx"), lax.axis_size("wsh")
    net = Cube() if count == 8 else Line(count)
    me, shard = lax.axis_index("ctx"), lax.axis_index("wsh")
    x = tokens[0]
    rows, width = x.shape
    length = rows * count
    size = width // HEADS
    heads = max(1, HEADS // count)
    copies = max(1, count // HEADS)
    cols = heads * size
    wide = -(-cols // LANES) * LANES
    depth = width // shards
    units = outer_weight.shape[0] // count
    strip = depth // count
    scale = size**-0.5
    shard_ids = jnp.stack([shard ^ r for r in range(shards)])
    places = jnp.stack(net.places(rows))

    first_col = me // copies * cols

    def own_columns(w):
        return jnp.pad(lax.dynamic_slice_in_dim(w, first_col, cols, 1), ((0, 0), (0, wide - cols)))

    weights, lane = [query_weight, key_weight, value_weight], first_col
    if cols % LANES:
        weights, lane = [own_columns(w) for w in weights], jnp.int32(0)
    wo_own, wo_at = output_weight, me
    if strip % 16:
        wo_own, wo_at = lax.dynamic_slice_in_dim(output_weight, me * strip, strip, 0), jnp.int32(0)
    vectors = [query_bias, value_bias, output_bias, first_gain, first_shift, outer_bias, second_gain,
               second_shift, inner_bias]
    vectors = [v.reshape(-1, LANES) for v in vectors]
    (pack,) = call(
        pack_kernel, [jnp.stack([lane, wo_at])], [*weights, wo_own, *vectors],
        [struct((3 * depth + VECTORS + strip * width // LANES, LANES), BF)], 20, "pack", (), None,
    )
    packs = [pack] + [shard_flip(pack, r, shards) for r in range(1, shards)]
    share = units * shards
    times = width // share
    inner_own = [
        lax.dynamic_slice_in_dim(inner_weight, s * units * count + me * units, units, 1) for s in range(shards)
    ]
    inner_own = jnp.concatenate(inner_own, axis=1)
    inner_own = jnp.concatenate([inner_own[i * depth // times : (i + 1) * depth // times] for i in range(times)], axis=1)
    outer_own = lax.dynamic_slice_in_dim(outer_weight, me * units, units, 0)
    forward_pack = jnp.concatenate([outer_own, inner_own], axis=0)
    unpacked = []

    def unpack(marker):
        made = call(
            functools.partial(unpack_kernel, shards), [shard_ids], after(packs, marker),
            [struct((8, width), F32), struct((8 * shards, inner_bias.shape[0]), F32)], 20, "unpack",
        )
        unpacked.extend(made)
        return [forward_pack]

    pieces = net.gather(x, early=[pack], late=unpack)
    vec, inner_all = unpacked
    bias = jnp.pad(lax.dynamic_slice(vec, (0, first_col), (8, cols)), ((0, 0), (0, wide - cols)))
    inner_b = lax.dynamic_slice_in_dim(inner_all[::8], me * units, units, 1).reshape(1, -1)

    qkv_rows = []
    done = 0
    for group in grouped(pieces, 10):
        group_rows = sum(p.shape[0] for p in group)
        sheet = struct((group_rows, wide), BF)
        tail = struct((group_rows, LANES), BF)
        qkv, *made = call(
            functools.partial(project_kernel, len(group), shards, wide, scale),
            [shard_ids, places[done : done + len(group)], starts[0]],
            [*group, *packs, bias],
            [struct((width, 3 * wide), BF), sheet, sheet, sheet, tail, tail],
            4, "project",
        )
        qkv_rows.append(made)
        done += len(group)
    q, k, v, qt, kt = [made[0] if len(made) == 1 else jnp.concatenate(made) for made in zip(*qkv_rows)]

    forward_pack = lax.all_gather(after(forward_pack, packs, pieces[6:8]), "wsh", axis=0, tiled=False)

    attended, blocks = [], []
    for low, high in net.parts:
        made = attend(q, qt, k, kt, v, rows, heads, size, low, high)
        attended.append(made)
        mixed = [made[0][i * rows : (i + 1) * rows, :cols] for i in range(high - low)]
        if blocks:
            mixed, *tied = after((mixed, *blocks, slabs[1]), made[0])
            blocks, slabs[1] = tied[:-1], tied[-1]
        blocks += net.exchange(mixed, low)
        if high < count:
            slabs = net.gather_slab(stack(packs, 3 * depth + VECTORS), made[0])
            q, k = after((q, k), slabs[0])
    if isinstance(net, Cube):
        ids = jnp.stack([net.at(r) for r in net.slab_order])
        (wo,) = call(
            functools.partial(assemble_kernel, shards, strip), [shard_ids, ids], slabs,
            [struct((width, width), BF)], 2, "assemble",
        )
    else:
        wo_slab = jnp.zeros((shards, strip, width), BF)
        for r in range(shards):
            part = packs[r][3 * depth + VECTORS :].reshape(width // LANES, strip, LANES).transpose(1, 0, 2).reshape(1, strip, width)
            wo_slab = lax.dynamic_update_slice(wo_slab, part, (shard ^ r, jnp.int32(0), jnp.int32(0)))
        wo = lax.all_gather(wo_slab, "ctx", axis=0, tiled=False)
        wo = wo.transpose(1, 0, 2, 3).reshape(width, width)
    blocks = blocks[::copies]
    offs = jnp.stack([net.at(r) // copies for r in range(0, count, copies)])
    groups = len(blocks)
    low_full, tall = struct((rows, width), BF), struct((rows, 1), F32)
    sums = struct((8, width), F32)
    hidden_low, normed, root = call(
        functools.partial(first_norm_kernel, groups), [offs], [x, wo, vec, *blocks],
        [low_full, low_full, tall], 5, "first_norm",
    )
    inner, outer = call(
        functools.partial(weights_kernel, units), [], [forward_pack],
        [struct((width, share), BF), struct((share, width), BF)], 2, "weights",
    )

    def forward(group):
        sizes = [p.shape[0] for p in group]
        mids = [struct((s, units * shards), BF) for s in sizes]
        made = call(
            functools.partial(forward_kernel, len(group)), [], [inner, inner_b, outer, *group],
            mids + mids + [struct((s, width), BF) for s in sizes], 1.5 * sum(sizes) / 256, "forward",
        )
        n = len(group)
        return made[:n], made[n : 2 * n], made[2 * n :]

    hidden_all, (acts, slopes, branch) = net.gather(hidden_low, forward)
    parts, n_whole, n_half, _ = net.scatter(branch)
    result, branch_grad, sums_two = call(
        functools.partial(second_norm_kernel, n_whole, n_half), [], [hidden_low, vec, cotangent[0], *parts],
        [low_full, low_full, sums], 4, "second_norm",
    )

    inner_sums, waiting, products = [], list(slopes), []

    def backward(group):
        sizes = [p.shape[0] for p in group]
        n, at = len(group), len(acts) - len(waiting)
        slope, waiting[:n] = waiting[:n], []
        made = call(
            functools.partial(backward_kernel, n), [], [inner, outer, *group, *slope],
            [struct((s, units * shards), BF) for s in sizes]
            + [struct((s, width), BF) for s in sizes]
            + [struct((1, units * shards), F32)],
            1.5 * sum(sizes) / 256, "backward",
        )
        inner_sums.append(made[-1])
        terms = [*acts[at : at + n], *group, *hidden_all[at : at + n], *made[:n]]
        if at + n < len(acts):
            given = products[-1] if products else []
            products.append(
                pl.pallas_call(
                    functools.partial(product_kernel, n, len(given)),
                    in_specs=[IN_VMEM] * (4 * n + len(given)),
                    out_specs=[IN_VMEM] * 2,
                    out_shape=[struct((share, width), F32), struct((width, share), F32)],
                    input_output_aliases={4 * n + i: i for i in range(len(given))},
                    compiler_params=params(bytes_of(terms) + 2 * 4 * share * width + 8 * MIB),
                    cost_estimate=micros(3),
                    name="product",
                )(*terms, *given)
            )
            return made[:n], made[n:-1], list(products[-1])
        return made[:n], made[n:-1], terms

    grad_all, (inner_grads, hidden_grads, terms) = net.gather(branch_grad, backward)
    n = len(terms[2 * len(products) :]) // 4
    given, terms = products[-1], terms[2 * len(products) :]
    parts, n_whole, n_half, moved = net.scatter(hidden_grads)
    height = units + depth * share // width
    (forward_wg,) = call(
        functools.partial(last_product_kernel, n, len(given), shards), [], [*after(terms, moved), *given],
        [struct((shards * height, width), BF)], 5, "last_product",
        [pltpu.VMEM((share, width), F32), pltpu.VMEM((width, share), F32)],
    )
    parts = after(parts, forward_wg)
    forward_own = lax.psum_scatter(forward_wg, "wsh", scatter_dimension=0, tiled=True)
    attn_grad, sums_one, *mixed_grads = call(
        functools.partial(first_back_kernel, groups, n_whole, n_half), [offs],
        [branch_grad, normed, root, vec, wo, *parts],
        [low_full, sums] + [struct((rows, cols), BF)] * groups, 5, "first_back", (), None,
    )
    if copies > 1:
        mixed_grads = [b for b in mixed_grads for _ in range(copies)]
    exchanged = []
    for low, high in net.parts:
        exchanged += net.exchange(mixed_grads[low:high], low)
    order = [0, 4, 2, 6, 1, 5, 3, 7] if isinstance(net, Cube) else list(range(count))
    halves = 2 if isinstance(net, Cube) else 1
    ids = jnp.stack([net.at(r) for r in order])

    def mixed_product(offs_ref, ids_ref, low_ref, *refs):
        outs, acc = refs[groups:-1], refs[-1]
        for r, block in enumerate(refs[:groups]):
            acc[block_at(offs_ref[r], cols), :] = dot_tn(block[...], low_ref[...])
        per = count // halves
        for i in range(count):
            for s in range(shards):
                row = (i % per * shards + s) * strip
                at = pl.multiple_of(s * depth + ids_ref[i] * strip, strip)
                outs[i // per][row : row + strip, :] = acc[pl.ds(at, strip), :].astype(BF)

    wo_grad = call(
        mixed_product, [offs, ids], [after(attn_grad, exchanged[1]), *blocks],
        [struct((width // halves, width), BF)] * halves, 4, "mixed_product", [pltpu.VMEM((width, width), F32)],
    )
    if isinstance(net, Cube):
        folded = net.fold(wo_grad[0], flip(wo_grad[1], 1))
    else:
        folded = lax.psum_scatter(wo_grad[0], "ctx", scatter_dimension=0, tiled=True)
    prior = None
    for (low, high), (_, o, lse) in zip(net.parts, attended):
        mgs = [jnp.pad(b, ((0, 0), (0, wide - cols))) for b in exchanged[low:high]]
        mgs = after(mgs, folded)
        prior = attend_back(q, qt, k, kt, v, mgs, o, lse, rows, heads, size, scale, low, high, prior)
        if isinstance(net, Cube):
            half = folded.shape[0] // 2
            sent = flip(folded[half:], 2 if low == 0 else 4)
            folded = net.fold(folded[:half], after(sent, prior if high == count else prior[0]))
    triple = after(prior, folded)
    forward_all = lax.all_gather(after(forward_own, triple), "ctx", axis=0, tiled=False)
    inner_sum = add_up(inner_sums).reshape(shards, units)
    last_pack = struct((3 * (depth + EXTRA) + strip * width // LANES, LANES), BF)
    into = input_terms(triple, qkv, rows, halves, 1.0 / copies)
    packs = pl.pallas_call(
        functools.partial(qkv_product_kernel, len(pieces), shards),
        in_specs=[IN_SMEM] + [IN_VMEM] * 5 + [pl.BlockSpec(memory_space=pl.ANY)] * len(pieces),
        out_specs=[IN_VMEM] * shards,
        out_shape=[last_pack] * shards,
        scratch_shapes=[pltpu.VMEM(p.shape, BF) for p in pieces]
        + [pltpu.VMEM((3 * wide, width), F32), pltpu.VMEM((EXTRA, 3 * wide), F32)]
        + [pltpu.SemaphoreType.DMA((len(pieces),))],
        compiler_params=params(bytes_of(pieces) + bytes_of([triple]) + 9 * MIB),
        cost_estimate=micros(60),
        name="qkv_product",
    )(shard_ids, after(triple, into), sums_one, sums_two, inner_sum, folded, *pieces)
    packs = [packs[0]] + [shard_flip(packs[r], r, shards) for r in range(1, shards)]
    (last_own,) = call(sum_kernel, [], packs, [last_pack], 2, "last_sum")
    parts, n_whole, n_half = net.scatter_whole(*into, packs[0], last_own)
    (input_grad,) = call(
        functools.partial(input_kernel, n_whole, n_half), [], [attn_grad, *parts], [low_full], 2, "input_sum"
    )
    if isinstance(net, Cube):
        outer_out, inner_out = call(
            functools.partial(finish_forward_kernel, units), [], [forward_all],
            [struct((units * count, width), F32), struct((depth, units * count * shards), F32)], 6, "finish_forward",
            (), 2,
        )
        last_all = net.gather(last_own, early=[outer_out, parts[1], parts[4]])
        square = struct((depth, width), F32)
        query_out, key_out, value_out, wo_out, *vecs = call(
            finish_kernel, [shard_ids, offs], last_all,
            [square] * 4 + [struct((1, units * count), F32)] + [struct((1, depth), F32)] * 8, 4, "finish",
            [pltpu.VMEM((8, units * count), F32), pltpu.VMEM((16, width), F32)], 3,
        )
        inner_vec, *vecs = [v.reshape(-1) for v in vecs]
    else:
        last_all = jnp.stack(net.gather(last_own)).astype(F32)
        triples = last_all[:, : 3 * (depth + EXTRA)].reshape(count, 3, depth + EXTRA, LANES)
        wo_out = last_all[:, 3 * (depth + EXTRA) :].reshape(count, width // LANES, strip, LANES)
        wo_out = wo_out.transpose(0, 2, 1, 3).reshape(depth, width)
        out3 = triples[::copies, :, :depth, :cols].transpose(1, 2, 0, 3).reshape(3, depth, width)
        query_out, key_out, value_out = out3[0], out3[1], out3[2]
        both = triples[::copies, :, depth, :cols].transpose(1, 0, 2).reshape(3, width)
        both = lax.dynamic_slice_in_dim(both, shard * depth, depth, 1)
        tail = triples[:, :, depth:].transpose(0, 2, 1, 3).reshape(count, EXTRA, 3 * LANES)
        six = jnp.sum(tail[:, 1:7, :depth], axis=0)
        vecs = [both[0], both[2]] + [six[i] for i in range(6)]
        inner_vec = tail[:, 7, 2 * LANES : 2 * LANES + units].reshape(-1)
        forward_all = forward_all.astype(F32)
        outer_out = forward_all[:, :units].reshape(-1, width)
        inner_out = forward_all[:, units:].reshape(count, depth // times, times, shards, units)
        inner_out = inner_out.transpose(2, 1, 3, 0, 4).reshape(depth, -1)
    return (
        result[None], input_grad[None], query_out, key_out, value_out, wo_out, inner_out, outer_out,
        vecs[0], vecs[1], vecs[2], vecs[3], vecs[4], inner_vec, vecs[5], vecs[6], vecs[7],
    )


def solution(mesh):
    sheet, matrix, vector = P("wsh", "ctx", None), P("wsh", None), P("wsh")
    return jax.shard_map(
        local,
        mesh=mesh,
        in_specs=(sheet, matrix) + (matrix,) * 6 + (vector,) * 9 + (sheet,),
        out_specs=(sheet, sheet) + (matrix,) * 6 + (vector,) * 9,
        check_vma=False,
    )
```
